128 devices in a mesh: wide: 16 (over z, x), narrow: 8 (over y, core).
Axes of the slice: x: 4, y: 4, z: 4, core: 2. Of those that a mesh axis runs over, the one named last changes fastest.
Arguments:
- factors: bfloat16 [768, 256, 768], P(('wide', 'narrow')), may hold values from -0.1875 to 0.1875
- integrals: bfloat16 [768, 256, 768], P(('wide', 'narrow')), may hold values from -6 to 6
- pao_energy: float32 [768, 256], replicated, may hold values from 0.3 to 4
- lmo_energy: float32 [768], replicated, may hold values from -1.5 to -0.3
- partners: int32 [768, 4], replicated, may hold values from 0 to 767, as said below
Outputs:
- auxiliary_density: float32 [768, 768], P('wide', 'narrow')
The draws below stay inside these ranges and needn't reach their ends.
Inputs may be any that keep to these rules, and one draw needn't show every extreme that they name: LMO i is held by device i // 6, devices counted with wide outermost. Each LMO's 4 partners are LMOs other than itself, held by devices with the same narrow index as its own holder, in 4 different wide groups (its own device may be one). The listed pairs of one device's 6 LMOs point to exactly 8 devices, with exactly 3 pairs and exactly 2 distinct partners on each of them.
All inputs are finite; a program needn't handle non-finite values.
Results may differ from the reference program's by a relative error of at most 0.0035.
Values may be sent and summed in bfloat16 or wider, within the bound.
A program may use at most 128 MiB of HBM per device.

```python
import math
import jax
import jax.numpy as jnp
from jax import lax

LMO_DEV = 6
PARTNERS = 4
PAO = 256
AUX = 768
LMOS = 768
N_WIDE = 16
N_NARROW = 8
DEVICES = 128


def draw_partners(key, part):
    device_count = N_WIDE * N_NARROW
    half = LMO_DEV // 2
    groups = 2 * PARTNERS
    subkeys = jax.random.split(jax.random.fold_in(key, 11), 6)
    offsets = jax.vmap(lambda subkey: jax.random.permutation(subkey, N_WIDE))(jax.random.split(subkeys[0], device_count))[:, :groups].astype(jnp.int32)
    slot_order = jax.vmap(lambda subkey: jax.random.permutation(subkey, LMO_DEV))(jax.random.split(subkeys[1], device_count)).astype(jnp.int32)
    partner_order = jax.vmap(lambda subkey: jax.random.permutation(subkey, PARTNERS))(jax.random.split(subkeys[2], device_count * LMO_DEV)).astype(jnp.int32)
    partner_order = partner_order.reshape(device_count, LMO_DEV, PARTNERS)
    odd_member = jax.random.randint(subkeys[3], (device_count, groups), 0, 3, dtype=jnp.int32)
    pick = jax.random.randint(subkeys[4], (device_count, groups), 0, LMO_DEV, dtype=jnp.int32)
    stride = jax.random.randint(subkeys[5], (device_count, groups), 1, LMO_DEV, dtype=jnp.int32)
    device_ids = jnp.arange(device_count, dtype=jnp.int32)
    target = (device_ids[:, None] // N_NARROW + offsets) % N_WIDE
    owner = target * N_NARROW + (device_ids % N_NARROW)[:, None]
    side = jnp.arange(groups, dtype=jnp.int32) // PARTNERS
    member = jnp.arange(3, dtype=jnp.int32)
    triple = slot_order[:, side[:, None] * half + member[None, :]]
    others = slot_order[:, (1 - side)[:, None] * half + member[None, :]]
    first_local = jnp.take_along_axis(others, (pick % 3)[:, :, None], axis=2)[:, :, 0]
    second_local = jnp.take_along_axis(others, ((pick % 3 + 1 + stride % 2) % 3)[:, :, None], axis=2)[:, :, 0]
    same_device = offsets == 0
    first_local = jnp.where(same_device, first_local, pick)
    second_local = jnp.where(same_device, second_local, (pick + stride) % LMO_DEV)
    chosen = jnp.where(member[None, None, :] == odd_member[:, :, None], second_local[:, :, None], first_local[:, :, None])
    values = owner[:, :, None] * LMO_DEV + chosen
    flat_slots = triple.reshape(device_count, groups * 3)
    column_pos = jnp.broadcast_to((jnp.arange(groups, dtype=jnp.int32) % PARTNERS)[None, :, None], (device_count, groups, 3)).reshape(device_count, groups * 3)
    rows = jnp.take_along_axis(partner_order, flat_slots[:, :, None], axis=1)
    columns = jnp.take_along_axis(rows, column_pos[:, :, None], axis=2)[:, :, 0]
    table = jnp.zeros((device_count, LMO_DEV, PARTNERS), jnp.int32)
    table = table.at[device_ids[:, None], flat_slots, columns].set(values.reshape(device_count, groups * 3))
    return table.reshape(device_count * LMO_DEV, PARTNERS)


def block_scale(rng, shape, pieces, smallest, high):
    def one(position, blocks):
        heights = jax.random.uniform(jax.random.fold_in(jax.random.fold_in(rng, 6), position), (blocks,), jnp.float32, smallest / len(pieces), high / len(pieces))
        return jnp.repeat(jnp.exp(heights), shape[position] // blocks).reshape((-1,) + (1,) * (len(shape) - position - 1))

    factor_of = one(*pieces[0])
    for cut in pieces[1:]:
        factor_of = factor_of * one(*cut)
    return factor_of


def gaussian(key, extent, deviation, bound, cuts=(), kind=jnp.bfloat16):
    level = block_scale(key, extent, cuts, -0.22, 0.18) if cuts else 1.0
    values = jax.random.normal(key, extent, jnp.float32) * deviation * level
    return jnp.minimum(jnp.maximum(values, -bound), bound).astype(kind)


def setup_inputs(seed: int = 0) -> dict:
    arg_keys = jax.random.split(jax.random.key(seed), 6)
    factors = gaussian(arg_keys[0], (LMOS, PAO, AUX), (1.3 * (AUX * PAO * PAO * DEVICES) ** -0.16666667), 0.1875, ((0, 128),))
    integrals = gaussian(arg_keys[1], (LMOS, PAO, AUX), 1.0, 6.0, ((0, 128),))
    pao_energy = jnp.clip(jnp.exp(jax.random.uniform(arg_keys[2], (LMOS, PAO), jnp.float32, math.log(0.3), math.log(4.0))), 0.3, 4.0)
    lmo_energy = jnp.clip(jax.random.uniform(arg_keys[3], (LMOS,), jnp.float32, -1.5, -0.3), -1.5, -0.3)
    partners = draw_partners(jax.random.fold_in(arg_keys[5], 71), 0)
    return {"factors": factors, "integrals": integrals, "pao_energy": pao_energy, "lmo_energy": lmo_energy, "partners": partners}


def reference(factors, integrals, pao_energy, lmo_energy, partners):
    block_count = LMOS // LMO_DEV

    def one_block(total, block):
        first_lmo = (block * LMO_DEV).astype(jnp.int32)
        own = lax.dynamic_slice_in_dim(factors, first_lmo, LMO_DEV, 0).astype(jnp.float32)
        resident = lax.dynamic_slice_in_dim(integrals, first_lmo, LMO_DEV, 0)
        listed = lax.dynamic_slice_in_dim(partners, first_lmo, LMO_DEV, 0).astype(jnp.int32)
        other = jnp.take(factors, listed, axis=0).astype(jnp.float32)
        own_pao = lax.dynamic_slice_in_dim(pao_energy, first_lmo, LMO_DEV, 0)
        other_pao = jnp.take(pao_energy, listed, axis=0)
        own_lmo = lax.dynamic_slice_in_dim(lmo_energy, first_lmo, LMO_DEV, 0)
        other_lmo = jnp.take(lmo_energy, listed, axis=0)
        denominator = (own_pao[:, None, :, None] + other_pao[:, :, None, :]
                       - own_lmo[:, None, None, None] - other_lmo[:, :, None, None])
        pair_integral = jnp.einsum('sar,skbr->skab', own, other)
        amplitude = (pair_integral / denominator).astype(jnp.bfloat16)
        fitted_density = jnp.einsum('skab,skbr->sar', amplitude.astype(jnp.float32), other).astype(jnp.bfloat16)
        partial_total = jnp.dot(resident.reshape(-1, AUX).T, fitted_density.reshape(-1, AUX),
                                preferred_element_type=jnp.float32)
        return total + partial_total, None

    total, _ = lax.scan(one_block, jnp.zeros((AUX, AUX), jnp.float32),
                        jnp.arange(block_count, dtype=jnp.int32))
    return 0.5 * (total + total.T)
```

```python
import functools

import jax
import jax.numpy as jnp
import numpy as np
from jax import lax
from jax.experimental import pallas as pl
from jax.experimental.pallas import tpu as pltpu
from jax.sharding import PartitionSpec as P

MESH = pl.DeviceIdType.MESH
LMO = 6
PARTNERS = 4
PAIRS = LMO * PARTNERS
PAO = 256
AUX = 768
ROTS = 4
PIECE = PAO // ROTS

MASKS = (1, 4, 3, 12)


def order(rot):
    return [MASKS[(rot + step) % 4] for step in range(4)]


def flip(position, mask):
    if mask == 0:
        return position
    if mask == 3:
        return 3 - position
    return position + 1 - 2 * lax.rem(position, 2)


def neighbour(mask):
    wide = lax.axis_index("wide")
    z, x = wide // 4, lax.rem(wide, 4)
    return (flip(z, mask // 4) * 4 + flip(x, mask % 4), lax.axis_index("narrow"))


def kernel(table, factors, integrals, own_energy, other_energy, total, *scratch):
    row = list(scratch[0:4])
    send3 = list(scratch[4:8])
    send4 = list(scratch[8:12])
    passing = list(scratch[12:16])
    final = list(scratch[16:20])
    flipped, fitted, energy, local_sem, send_sem, recv_sem = scratch[20:]

    barrier = pltpu.get_barrier_semaphore()
    for mask in MASKS:
        pl.semaphore_signal(barrier, inc=1, device_id=neighbour(mask), device_id_type=MESH)
    pl.semaphore_wait(barrier, 4)

    def copy(rot, kind, src, dst, mask):
        return pltpu.make_async_remote_copy(
            src_ref=src,
            dst_ref=dst,
            send_sem=send_sem.at[rot, kind],
            recv_sem=recv_sem.at[rot, kind],
            device_id=neighbour(mask),
            device_id_type=MESH,
        )

    copies = []
    for rot in range(ROTS):
        m1, m2, m3, m4 = order(rot)
        own = factors.at[:, pl.ds(rot * PIECE, PIECE), :]
        copies.append(
            [
                copy(rot, 0, own, row[rot].at[pl.ds(6, 6)], m1),
                copy(rot, 1, own, row[rot].at[pl.ds(12, 6)], m2),
                copy(rot, 2, row[rot].at[pl.ds(6, 6)], row[rot].at[pl.ds(18, 6)], m2),
                copy(rot, 3, send3[rot].at[1], passing[rot], m3),
                copy(rot, 4, send3[rot].at[0], final[rot].at[pl.ds(8, 8)], m3),
                copy(rot, 5, send4[rot], final[rot].at[pl.ds(16, 8)], m4),
                copy(rot, 6, passing[rot], final[rot].at[pl.ds(24, 8)], m4),
            ]
        )
    for rot in range(ROTS):
        copies[rot][0].start()
    for rot in range(ROTS):
        copies[rot][1].start()
    local = []
    for rot in range(ROTS):
        own = factors.at[:, pl.ds(rot * PIECE, PIECE), :]
        local.append(pltpu.make_async_copy(own, row[rot].at[pl.ds(0, 6)], local_sem.at[rot]))
        local[rot].start()

    columns = jnp.transpose(own_energy[...])
    for i in range(LMO):
        energy[i] = jnp.broadcast_to(columns[:, i : i + 1], (PAO, PAO))
        flipped[:, i * PAO : (i + 1) * PAO] = jnp.transpose(integrals[i])

    for rot in range(ROTS):
        copies[rot][0].wait_recv()
        copies[rot][2].start()

    def gather(rot, receiver, put):
        def body(slot, carry):
            put(slot, row[rot][table[rot * 32 + receiver * 8 + slot]])
            return carry

        lax.fori_loop(0, 8, body, 0)

    def put_into(ref, base):
        def put(slot, value):
            ref[base + slot] = value

        return put

    def put_send3(rot, which):
        def put(slot, value):
            send3[rot][which, slot] = value

        return put

    for rot in range(ROTS):
        local[rot].wait()
        copies[rot][1].wait_recv()
        copies[rot][2].wait_recv()
        gather(rot, 1, put_send3(rot, 1))
        copies[rot][3].start()
    for rot in range(ROTS):
        gather(rot, 0, put_send3(rot, 0))
        copies[rot][4].start()
        gather(rot, 2, put_into(send4[rot], 0))
        copies[rot][5].start()
    for rot in range(ROTS):
        gather(rot, 3, put_into(final[rot], 0))
    for rot in range(ROTS):
        copies[rot][3].wait_recv()
        copies[rot][6].start()
    for rot in range(ROTS):
        for kind in (4, 5, 6):
            copies[rot][kind].wait_recv()

    def one(i, carry):
        mine = factors[i]
        gathered = jnp.zeros((PAO, AUX), jnp.float32)
        for k in range(PARTNERS):
            pair = i * PARTNERS + k
            other = jnp.concatenate(
                [final[rot][table[128 + rot * PAIRS + pair]] for rot in range(ROTS)], axis=0
            )
            integral = lax.dot_general(
                mine, other, (((1,), (1,)), ((), ())), preferred_element_type=jnp.float32
            )
            amplitude = (integral / (energy[i] + other_energy[pair])).astype(jnp.bfloat16)
            gathered = gathered + jnp.dot(amplitude, other, preferred_element_type=jnp.float32)
        fitted[pl.ds(pl.multiple_of(i * PAO, PAO), PAO), :] = gathered.astype(jnp.bfloat16)
        return carry

    lax.fori_loop(0, LMO, one, 0)

    def rows(block, carry):
        at = pl.ds(pl.multiple_of(block * 256, 256), 256)
        total[at, :] = jnp.dot(flipped[at, :], fitted[...], preferred_element_type=jnp.float32)
        return carry

    lax.fori_loop(0, AUX // 256, rows, 0)

    for rot in range(ROTS):
        for kind in range(7):
            copies[rot][kind].wait_send()


def exchange_and_multiply(table, factors, integrals, own_energy, other_energy):
    vmem = pl.BlockSpec(memory_space=pltpu.VMEM)
    piece = (PIECE, AUX)
    scratch = []
    for shape in ((24,), (2, 8), (8,), (8,), (32,)):
        scratch += [pltpu.VMEM(shape + piece, jnp.bfloat16) for _ in range(ROTS)]
    scratch += [
        pltpu.VMEM((AUX, LMO * PAO), jnp.bfloat16),
        pltpu.VMEM((LMO * PAO, AUX), jnp.bfloat16),
        pltpu.VMEM((LMO, PAO, PAO), jnp.float32),
        pltpu.SemaphoreType.DMA((ROTS,)),
        pltpu.SemaphoreType.DMA((ROTS, 7)),
        pltpu.SemaphoreType.DMA((ROTS, 7)),
    ]
    return pl.pallas_call(
        kernel,
        out_shape=jax.ShapeDtypeStruct((AUX, AUX), jnp.float32),
        in_specs=[pl.BlockSpec(memory_space=pltpu.SMEM), vmem, vmem, vmem, vmem],
        out_specs=vmem,
        scratch_shapes=scratch,
        compiler_params=pltpu.CompilerParams(
            collective_id=0, has_side_effects=True, vmem_limit_bytes=60 * 2**20
        ),
    )(table, factors, integrals, own_energy, other_energy)


def make_table(column, wide_index):
    relative = jnp.take(column, wide_index ^ jnp.arange(16, dtype=jnp.int32), axis=0)
    source = (relative // (LMO * 8)) ^ wide_index
    slot = relative % LMO
    at = source[:, None, :] == jnp.arange(16, dtype=jnp.int32)[None, :, None]
    low = jnp.min(jnp.where(at, slot[:, None, :], LMO - 1), axis=2)
    high = jnp.max(jnp.where(at, slot[:, None, :], 0), axis=2)
    wanted = jnp.stack([low, high], axis=-1).reshape(-1)
    pick, base = [], []
    for rot in range(ROTS):
        m1, m2, m3, m4 = order(rot)
        for receiver in (m3, m3 ^ m4, m4, 0):
            for q in range(4):
                sender = (m1 if q & 1 else 0) ^ (m2 if q & 2 else 0)
                for k in range(2):
                    pick.append((receiver * 16 + sender) * 2 + k)
                    base.append(q * LMO)
    sends = wanted[np.array(pick)] + np.array(base, np.int32)

    mine, mine_slot = source[0], slot[0]
    is_high = mine_slot == jnp.sum(jnp.where(at[0], high[0][:, None], 0), axis=0)
    digit = {}
    for low_mask, high_mask, part in ((1, 3, mine % 4), (4, 12, mine // 4)):
        digit[low_mask] = ((part == 1) | (part == 2)).astype(jnp.int32)
        digit[high_mask] = ((part == 3) | (part == 2)).astype(jnp.int32)
    places = []
    for rot in range(ROTS):
        m1, m2, m3, m4 = order(rot)
        group = digit[m3] + 2 * digit[m4]
        places.append((group * 4 + digit[m1] + 2 * digit[m2]) * 2 + is_high.astype(jnp.int32))
    return jnp.concatenate([sends] + places).astype(jnp.int32)


def in_blocks(value, dim, count):
    dims = value.shape
    tiles = value.reshape(*dims[:dim], count, dims[dim] // count, *dims[dim + 1 :])
    return jnp.moveaxis(tiles, dim, 0)


def sum_at_owner(value, axis, dim):
    count = lax.axis_size(axis)
    tiles = lax.all_to_all(in_blocks(value, dim, count), axis, 0, 0, tiled=True)
    return jnp.sum(tiles, axis=0)


def local(factors, integrals, pao_energy, lmo_energy, partners):
    wide_index = lax.axis_index("wide")
    narrow_index = lax.axis_index("narrow")
    first_lmo = (wide_index * 8 + narrow_index) * LMO
    column = lax.dynamic_index_in_dim(
        partners.reshape(16, 8, PAIRS), narrow_index, 1, keepdims=False
    )
    table = make_table(column, wide_index)
    listed = lax.dynamic_slice_in_dim(partners, first_lmo, LMO, 0).reshape(PAIRS)
    shifted = pao_energy - lmo_energy[:, None]
    own_energy = lax.dynamic_slice_in_dim(shifted, first_lmo, LMO, 0)
    own_energy = jnp.pad(own_energy, ((0, 8 - LMO), (0, 0)))
    other_energy = jnp.take(shifted, listed, axis=0).reshape(PAIRS, 1, PAO)
    partial_total = exchange_and_multiply(table, factors, integrals, own_energy, other_energy)
    symmetric = 0.5 * (partial_total + partial_total.T)
    row_block = sum_at_owner(symmetric, "wide", 0)
    return sum_at_owner(row_block, "narrow", 1)


def solution(mesh):
    in_specs = (P(("wide", "narrow"), None, None), P(("wide", "narrow"), None, None), P(), P(), P())
    out_specs = P("wide", "narrow")
    return jax.shard_map(local, mesh=mesh, in_specs=in_specs, out_specs=out_specs, check_vma=False)
```

```python
import functools

import jax
import jax.numpy as jnp
import numpy as np
from jax import lax
from jax.experimental import pallas as pl
from jax.experimental.pallas import tpu as pltpu
from jax.sharding import PartitionSpec as P

MESH = pl.DeviceIdType.MESH
LMO = 6
PARTNERS = 4
PAIRS = LMO * PARTNERS
PAO = 256
AUX = 768
ROWS = AUX // 8
HEIGHT = AUX // 16
ROTS = 4
PIECE = PAO // ROTS

MASKS = (1, 4, 3, 12)


def order(rot):
    return [MASKS[(rot + step) % 4] for step in range(4)]


def flip(position, mask):
    if mask == 0:
        return position
    if mask == 3:
        return 3 - position
    if mask == 2:
        return lax.rem(position + 2, 4)
    return position + 1 - 2 * lax.rem(position, 2)


def neighbour(mask):
    wide = lax.axis_index("wide")
    z, x = wide // 4, lax.rem(wide, 4)
    return (flip(z, mask // 4) * 4 + flip(x, mask % 4), lax.axis_index("narrow"))


def along_y(mask, core=0):
    narrow = lax.axis_index("narrow")
    y, c = narrow // 2, lax.rem(narrow, 2)
    return (lax.axis_index("wide"), flip(y, mask) * 2 + flip(c, core))


def reduce_total(
    tile, total, core_in, summed, first_out, first_in, second_out, second_in, block, turned, tiles_in,
    core_sem, y_sem, wide_sem,
):
    narrow, wide = lax.axis_index("narrow"), lax.axis_index("wide")
    y, core = narrow // 2, lax.rem(narrow, 2)

    def send(src, dst, sems, device):
        return pltpu.make_async_remote_copy(
            src_ref=src, dst_ref=dst, send_sem=sems[0], recv_sem=sems[1],
            device_id=device, device_id_type=MESH,
        )

    for i in range(3):
        for j in range(i, 3):
            at_i, at_j = slice(i * 256, i * 256 + 256), slice(j * 256, j * 256 + 256)
            half = 0.5 * (total[at_i, at_j] + jnp.transpose(total[at_j, at_i]))
            total[at_i, at_j] = half
            if i != j:
                total[at_j, at_i] = jnp.transpose(half)

    def band(u, c):
        return pl.ds(pl.multiple_of((flip(y, u) * 2 + c) * ROWS, ROWS), ROWS)

    steps = []
    for u in range(4):
        steps.append(
            send(total.at[band(u, 1 - core)], core_in.at[u],
                 (core_sem.at[0, u], core_sem.at[1, u]), along_y(0, 1))
        )
        steps[u].start()
    for u in (1, 2, 3, 0):
        steps[u].wait_recv()
        summed[u] = total[band(u, core), :] + core_in[u]

    left, right = slice(0, AUX // 2), slice(AUX // 2, AUX)
    plan = ((left, 1, 3, (1, 2)), (right, 3, 1, (3, 2)))
    firsts, seconds = [], []
    for h, (columns, near, far, sent) in enumerate(plan):
        for slot, u in enumerate(sent):
            first_out[h, slot] = summed[u, :, columns].astype(first_out.dtype)
        firsts.append(
            send(first_out.at[h], first_in.at[h], (y_sem.at[0, h], y_sem.at[1, h]), along_y(near))
        )
        firsts[h].start()
    for h, (columns, near, far, sent) in enumerate(plan):
        firsts[h].wait_recv()
        passed = summed[far, :, columns] + first_in[h, 1].astype(jnp.float32)
        second_out[h] = passed.astype(second_out.dtype)
        seconds.append(
            send(second_out.at[h], second_in.at[h], (y_sem.at[2, h], y_sem.at[3, h]), along_y(far))
        )
        seconds[h].start()
    block[pl.ds(ROWS, 128 - ROWS), :] = jnp.zeros((128 - ROWS, AUX), jnp.float32)
    for h, (columns, near, far, sent) in enumerate(plan):
        kept = summed[0, :, columns] + first_in[h, 0].astype(jnp.float32)
        seconds[h].wait_recv()
        block[pl.ds(0, ROWS), columns] = kept + second_in[h].astype(jnp.float32)

    for j in range(AUX // 128):
        at = slice(j * 128, j * 128 + 128)
        turned[at, :] = jnp.transpose(block[:, at])

    def rows(t):
        peer = flip(wide // 4, t // 4) * 4 + flip(lax.rem(wide, 4), t % 4)
        return pl.ds(pl.multiple_of(peer * HEIGHT, HEIGHT), HEIGHT)

    spread = []
    for t in range(1, 16):
        spread.append(
            send(turned.at[rows(t)], tiles_in.at[t - 1],
                 (wide_sem.at[0, t - 1], wide_sem.at[1, t - 1]), neighbour(t))
        )
        spread[-1].start()
    result = turned[rows(0), :]
    for t in range(1, 16):
        spread[t - 1].wait_recv()
        result = result + tiles_in[t - 1]
    tile[...] = result[:, :ROWS]

    for step in steps + firsts + seconds + spread:
        step.wait_send()


def kernel(table, factors, integrals, own_energy, other_energy, tile, *scratch):
    row = list(scratch[0:4])
    send3 = list(scratch[4:8])
    send4 = list(scratch[8:12])
    passing = list(scratch[12:16])
    final = list(scratch[16:20])
    flipped, fitted, energy, local_sem, send_sem, recv_sem = scratch[20:26]
    reduction = scratch[26:]
    total = reduction[0]

    barrier = pltpu.get_barrier_semaphore()
    greeted = [neighbour(mask) for mask in range(1, 16)]
    greeted += [along_y(0, 1), along_y(1), along_y(3)]
    for device in greeted:
        pl.semaphore_signal(barrier, inc=1, device_id=device, device_id_type=MESH)
    pl.semaphore_wait(barrier, len(greeted))

    def copy(rot, kind, src, dst, mask):
        return pltpu.make_async_remote_copy(
            src_ref=src,
            dst_ref=dst,
            send_sem=send_sem.at[rot, kind],
            recv_sem=recv_sem.at[rot, kind],
            device_id=neighbour(mask),
            device_id_type=MESH,
        )

    copies = []
    for rot in range(ROTS):
        m1, m2, m3, m4 = order(rot)
        own = factors.at[:, pl.ds(rot * PIECE, PIECE), :]
        copies.append(
            [
                copy(rot, 0, own, row[rot].at[pl.ds(6, 6)], m1),
                copy(rot, 1, own, row[rot].at[pl.ds(12, 6)], m2),
                copy(rot, 2, row[rot].at[pl.ds(6, 6)], row[rot].at[pl.ds(18, 6)], m2),
                copy(rot, 3, send3[rot].at[1], passing[rot], m3),
                copy(rot, 4, send3[rot].at[0], final[rot].at[pl.ds(8, 8)], m3),
                copy(rot, 5, send4[rot], final[rot].at[pl.ds(16, 8)], m4),
                copy(rot, 6, passing[rot], final[rot].at[pl.ds(24, 8)], m4),
            ]
        )
    for rot in range(ROTS):
        copies[rot][0].start()
    for rot in range(ROTS):
        copies[rot][1].start()
    local = []
    for rot in range(ROTS):
        own = factors.at[:, pl.ds(rot * PIECE, PIECE), :]
        local.append(pltpu.make_async_copy(own, row[rot].at[pl.ds(0, 6)], local_sem.at[rot]))
        local[rot].start()

    columns = jnp.transpose(own_energy[...])
    for i in range(LMO):
        energy[i] = jnp.broadcast_to(columns[:, i : i + 1], (PAO, PAO))
        flipped[:, i * PAO : (i + 1) * PAO] = jnp.transpose(integrals[i])

    for rot in range(ROTS):
        copies[rot][0].wait_recv()
        copies[rot][2].start()

    def gather(rot, receiver, put):
        def body(slot, carry):
            put(slot, row[rot][table[rot * 32 + receiver * 8 + slot]])
            return carry

        lax.fori_loop(0, 8, body, 0)

    def put_into(ref, base):
        def put(slot, value):
            ref[base + slot] = value

        return put

    def put_send3(rot, which):
        def put(slot, value):
            send3[rot][which, slot] = value

        return put

    for rot in range(ROTS):
        local[rot].wait()
        copies[rot][1].wait_recv()
        copies[rot][2].wait_recv()
        gather(rot, 1, put_send3(rot, 1))
        copies[rot][3].start()
    for rot in range(ROTS):
        gather(rot, 0, put_send3(rot, 0))
        copies[rot][4].start()
        gather(rot, 2, put_into(send4[rot], 0))
        copies[rot][5].start()
    for rot in range(ROTS):
        gather(rot, 3, put_into(final[rot], 0))
    for rot in range(ROTS):
        copies[rot][3].wait_recv()
        copies[rot][6].start()
    for rot in range(ROTS):
        for kind in (4, 5, 6):
            copies[rot][kind].wait_recv()

    def one(i, carry):
        mine = factors[i]
        gathered = jnp.zeros((PAO, AUX), jnp.float32)
        for k in range(PARTNERS):
            pair = i * PARTNERS + k
            other = jnp.concatenate(
                [final[rot][table[128 + rot * PAIRS + pair]] for rot in range(ROTS)], axis=0
            )
            integral = lax.dot_general(
                mine, other, (((1,), (1,)), ((), ())), preferred_element_type=jnp.float32
            )
            amplitude = (integral / (energy[i] + other_energy[pair])).astype(jnp.bfloat16)
            gathered = gathered + jnp.dot(amplitude, other, preferred_element_type=jnp.float32)
        fitted[pl.ds(pl.multiple_of(i * PAO, PAO), PAO), :] = gathered.astype(jnp.bfloat16)
        return carry

    lax.fori_loop(0, LMO, one, 0)

    def rows(block, carry):
        at = pl.ds(pl.multiple_of(block * 256, 256), 256)
        total[at, :] = jnp.dot(flipped[at, :], fitted[...], preferred_element_type=jnp.float32)
        return carry

    lax.fori_loop(0, AUX // 256, rows, 0)

    reduce_total(tile, *reduction)

    for rot in range(ROTS):
        for kind in range(7):
            copies[rot][kind].wait_send()


def exchange_and_multiply(table, factors, integrals, own_energy, other_energy):
    vmem = pl.BlockSpec(memory_space=pltpu.VMEM)
    piece = (PIECE, AUX)
    scratch = []
    for shape in ((24,), (2, 8), (8,), (8,), (32,)):
        scratch += [pltpu.VMEM(shape + piece, jnp.bfloat16) for _ in range(ROTS)]
    scratch += [
        pltpu.VMEM((AUX, LMO * PAO), jnp.bfloat16),
        pltpu.VMEM((LMO * PAO, AUX), jnp.bfloat16),
        pltpu.VMEM((LMO, PAO, PAO), jnp.float32),
        pltpu.SemaphoreType.DMA((ROTS,)),
        pltpu.SemaphoreType.DMA((ROTS, 7)),
        pltpu.SemaphoreType.DMA((ROTS, 7)),
        pltpu.VMEM((AUX, AUX), jnp.float32),
        pltpu.VMEM((4, ROWS, AUX), jnp.float32),
        pltpu.VMEM((4, ROWS, AUX), jnp.float32),
        pltpu.VMEM((2, 2, ROWS, AUX // 2), jnp.bfloat16),
        pltpu.VMEM((2, 2, ROWS, AUX // 2), jnp.bfloat16),
        pltpu.VMEM((2, ROWS, AUX // 2), jnp.bfloat16),
        pltpu.VMEM((2, ROWS, AUX // 2), jnp.bfloat16),
        pltpu.VMEM((128, AUX), jnp.float32),
        pltpu.VMEM((AUX, 128), jnp.float32),
        pltpu.VMEM((15, HEIGHT, 128), jnp.float32),
        pltpu.SemaphoreType.DMA((2, 4)),
        pltpu.SemaphoreType.DMA((4, 2)),
        pltpu.SemaphoreType.DMA((2, 15)),
    ]
    return pl.pallas_call(
        kernel,
        out_shape=jax.ShapeDtypeStruct((HEIGHT, ROWS), jnp.float32),
        in_specs=[pl.BlockSpec(memory_space=pltpu.SMEM), vmem, vmem, vmem, vmem],
        out_specs=vmem,
        scratch_shapes=scratch,
        compiler_params=pltpu.CompilerParams(
            collective_id=0, has_side_effects=True, vmem_limit_bytes=60 * 2**20
        ),
    )(table, factors, integrals, own_energy, other_energy)


def make_table(column, wide_index):
    relative = jnp.take(column, wide_index ^ jnp.arange(16, dtype=jnp.int32), axis=0)
    source = (relative // (LMO * 8)) ^ wide_index
    slot = relative % LMO
    at = source[:, None, :] == jnp.arange(16, dtype=jnp.int32)[None, :, None]
    low = jnp.min(jnp.where(at, slot[:, None, :], LMO - 1), axis=2)
    high = jnp.max(jnp.where(at, slot[:, None, :], 0), axis=2)
    wanted = jnp.stack([low, high], axis=-1).reshape(-1)
    pick, base = [], []
    for rot in range(ROTS):
        m1, m2, m3, m4 = order(rot)
        for receiver in (m3, m3 ^ m4, m4, 0):
            for q in range(4):
                sender = (m1 if q & 1 else 0) ^ (m2 if q & 2 else 0)
                for k in range(2):
                    pick.append((receiver * 16 + sender) * 2 + k)
                    base.append(q * LMO)
    sends = wanted[np.array(pick)] + np.array(base, np.int32)

    mine, mine_slot = source[0], slot[0]
    is_high = mine_slot == jnp.sum(jnp.where(at[0], high[0][:, None], 0), axis=0)
    digit = {}
    for low_mask, high_mask, part in ((1, 3, mine % 4), (4, 12, mine // 4)):
        digit[low_mask] = ((part == 1) | (part == 2)).astype(jnp.int32)
        digit[high_mask] = ((part == 3) | (part == 2)).astype(jnp.int32)
    places = []
    for rot in range(ROTS):
        m1, m2, m3, m4 = order(rot)
        group = digit[m3] + 2 * digit[m4]
        places.append((group * 4 + digit[m1] + 2 * digit[m2]) * 2 + is_high.astype(jnp.int32))
    return jnp.concatenate([sends] + places).astype(jnp.int32)


def local(factors, integrals, pao_energy, lmo_energy, partners):
    wide_index = lax.axis_index("wide")
    narrow_index = lax.axis_index("narrow")
    first_lmo = (wide_index * 8 + narrow_index) * LMO
    column = lax.dynamic_index_in_dim(
        partners.reshape(16, 8, PAIRS), narrow_index, 1, keepdims=False
    )
    table = make_table(column, wide_index)
    listed = lax.dynamic_slice_in_dim(partners, first_lmo, LMO, 0).reshape(PAIRS)
    shifted = pao_energy - lmo_energy[:, None]
    own_energy = lax.dynamic_slice_in_dim(shifted, first_lmo, LMO, 0)
    own_energy = jnp.pad(own_energy, ((0, 8 - LMO), (0, 0)))
    other_energy = jnp.take(shifted, listed, axis=0).reshape(PAIRS, 1, PAO)
    return exchange_and_multiply(table, factors, integrals, own_energy, other_energy)


def solution(mesh):
    in_specs = (P(("wide", "narrow"), None, None), P(("wide", "narrow"), None, None), P(), P(), P())
    out_specs = P("wide", "narrow")
    return jax.shard_map(local, mesh=mesh, in_specs=in_specs, out_specs=out_specs, check_vma=False)
```

```python
import jax
import jax.numpy as jnp
from jax import lax
from jax.experimental import pallas as pl
from jax.experimental.pallas import tpu as pltpu
from jax.sharding import PartitionSpec as P

MESH = pl.DeviceIdType.MESH
LMO = 6
PARTNERS = 4
PAIRS = LMO * PARTNERS
PAO = 256
AUX = 768
ROWS = AUX // 8
HEIGHT = AUX // 16
ROTS = 4
PIECE = PAO // ROTS

MASKS = (1, 4, 3, 12)


def order(rot):
    return [MASKS[(rot + step) % 4] for step in range(4)]


def flip(position, mask):
    if mask == 0:
        return position
    if mask == 3:
        return 3 - position
    if mask == 2:
        return lax.rem(position + 2, 4)
    return position + 1 - 2 * lax.rem(position, 2)


def neighbour(mask):
    wide = lax.axis_index("wide")
    z, x = wide // 4, lax.rem(wide, 4)
    return (flip(z, mask // 4) * 4 + flip(x, mask % 4), lax.axis_index("narrow"))


def along_y(mask, core=0):
    narrow = lax.axis_index("narrow")
    y, c = narrow // 2, lax.rem(narrow, 2)
    return (lax.axis_index("wide"), flip(y, mask) * 2 + flip(c, core))


def reduce_total(
    tile, total, core_in, summed, first_out, first_in, second_out, second_in, block, turned, tiles_in,
    core_sem, y_sem, wide_sem,
):
    narrow, wide = lax.axis_index("narrow"), lax.axis_index("wide")
    y, core = narrow // 2, lax.rem(narrow, 2)

    def send(src, dst, sems, device):
        return pltpu.make_async_remote_copy(
            src_ref=src, dst_ref=dst, send_sem=sems[0], recv_sem=sems[1],
            device_id=device, device_id_type=MESH,
        )

    for i in range(3):
        for j in range(i, 3):
            at_i, at_j = slice(i * 256, i * 256 + 256), slice(j * 256, j * 256 + 256)
            half = 0.5 * (total[at_i, at_j] + jnp.transpose(total[at_j, at_i]))
            total[at_i, at_j] = half
            if i != j:
                total[at_j, at_i] = jnp.transpose(half)

    def band(u, c):
        return pl.ds(pl.multiple_of((flip(y, u) * 2 + c) * ROWS, ROWS), ROWS)

    steps = []
    for u in range(4):
        steps.append(
            send(total.at[band(u, 1 - core)], core_in.at[u],
                 (core_sem.at[0, u], core_sem.at[1, u]), along_y(0, 1))
        )
        steps[u].start()
    for u in (1, 2, 3, 0):
        steps[u].wait_recv()
        summed[u] = total[band(u, core), :] + core_in[u]

    left, right = slice(0, AUX // 2), slice(AUX // 2, AUX)
    plan = ((left, 1, 3, (1, 2)), (right, 3, 1, (3, 2)))
    firsts, seconds = [], []
    for h, (columns, near, far, sent) in enumerate(plan):
        for slot, u in enumerate(sent):
            first_out[h, slot] = summed[u, :, columns].astype(first_out.dtype)
        firsts.append(
            send(first_out.at[h], first_in.at[h], (y_sem.at[0, h], y_sem.at[1, h]), along_y(near))
        )
        firsts[h].start()
    for h, (columns, near, far, sent) in enumerate(plan):
        firsts[h].wait_recv()
        passed = summed[far, :, columns] + first_in[h, 1].astype(jnp.float32)
        second_out[h] = passed.astype(second_out.dtype)
        seconds.append(
            send(second_out.at[h], second_in.at[h], (y_sem.at[2, h], y_sem.at[3, h]), along_y(far))
        )
        seconds[h].start()
    block[pl.ds(ROWS, 128 - ROWS), :] = jnp.zeros((128 - ROWS, AUX), jnp.float32)
    for h, (columns, near, far, sent) in enumerate(plan):
        kept = summed[0, :, columns] + first_in[h, 0].astype(jnp.float32)
        seconds[h].wait_recv()
        block[pl.ds(0, ROWS), columns] = kept + second_in[h].astype(jnp.float32)

    for j in range(AUX // 128):
        at = slice(j * 128, j * 128 + 128)
        turned[at, :] = jnp.transpose(block[:, at])

    def rows(t):
        peer = flip(wide // 4, t // 4) * 4 + flip(lax.rem(wide, 4), t % 4)
        return pl.ds(pl.multiple_of(peer * HEIGHT, HEIGHT), HEIGHT)

    spread = []
    for t in range(1, 16):
        spread.append(
            send(turned.at[rows(t)], tiles_in.at[t - 1],
                 (wide_sem.at[0, t - 1], wide_sem.at[1, t - 1]), neighbour(t))
        )
        spread[-1].start()
    result = turned[rows(0), :]
    for t in range(1, 16):
        spread[t - 1].wait_recv()
        result = result + tiles_in[t - 1]
    tile[...] = result[:, :ROWS]

    for step in steps + firsts + seconds + spread:
        step.wait_send()


def fill_table(table, source, slot, partners):
    wide, narrow = lax.axis_index("wide"), lax.axis_index("narrow")
    z, x = wide // 4, lax.rem(wide, 4)

    def group(mask):
        return flip(z, mask // 4) * 4 + flip(x, mask % 4)

    for rot in range(ROTS):
        m1, m2, m3, m4 = order(rot)
        senders = [group(mask) for mask in (0, m1, m2, m1 ^ m2)]
        for receiver, mask in enumerate((m3, m3 ^ m4, m4, 0)):
            first = (group(mask) * 8 + narrow) * LMO

            def scan(i, found):
                found = list(found)
                for k in range(PARTNERS):
                    listed = partners[k, first + i]
                    owner = lax.div(listed, LMO)
                    place = listed - owner * LMO
                    holder = lax.div(owner, 8)
                    for q in range(4):
                        hit = holder == senders[q]
                        low, high = found[2 * q], found[2 * q + 1]
                        found[2 * q] = jnp.where(hit, jnp.minimum(low, place), low)
                        found[2 * q + 1] = jnp.where(hit, jnp.maximum(high, place), high)
                return tuple(found)

            found = lax.fori_loop(0, LMO, scan, (jnp.int32(LMO - 1), jnp.int32(0)) * 4)
            for q in range(4):
                for k in range(2):
                    base = q * LMO if q < 3 else 0
                    table[rot * 32 + receiver * 8 + q * 2 + k] = found[2 * q + k] + base

    first = (wide * 8 + narrow) * LMO

    def split(i, carry):
        for k in range(PARTNERS):
            listed = partners[k, first + i]
            owner = lax.div(listed, LMO)
            source[i * PARTNERS + k] = lax.div(owner, 8)
            slot[i * PARTNERS + k] = listed - owner * LMO
        return carry

    lax.fori_loop(0, LMO, split, 0)

    def place(pair, carry):
        mine, mine_slot = source[pair], slot[pair]

        def larger(i, most):
            for k in range(PARTNERS):
                there = slot[i * PARTNERS + k]
                most = jnp.where(source[i * PARTNERS + k] == mine, jnp.maximum(most, there), most)
            return most

        most = lax.fori_loop(0, LMO, larger, jnp.int32(0))
        is_high = jnp.where(mine_slot == most, 1, 0)
        sz = lax.div(mine, 4)
        sx = mine - sz * 4
        digit = {}
        for low_mask, high_mask, here, there in ((1, 3, x, sx), (4, 12, z, sz)):
            digit[low_mask] = jnp.where((flip(here, 1) == there) | (flip(here, 2) == there), 1, 0)
            digit[high_mask] = jnp.where((flip(here, 3) == there) | (flip(here, 2) == there), 1, 0)
        for rot in range(ROTS):
            m1, m2, m3, m4 = order(rot)
            block = (digit[m3] + 2 * digit[m4]) * 4 + digit[m1] + 2 * digit[m2]
            table[128 + rot * PAIRS + pair] = block * 2 + is_high
        return carry

    lax.fori_loop(0, PAIRS, place, 0)


def kernel(partners, lmo_energy, factors, integrals, pao_energy, tile, *scratch):
    row = list(scratch[0:4])
    last = list(scratch[4:8])
    send3 = list(scratch[8:12])
    send4 = list(scratch[12:16])
    passing = list(scratch[16:20])
    final = list(scratch[20:24])
    (table, source, slot, resident, own_rows, other_energy, flipped, fitted, energy,
     local_sem, send_sem, recv_sem) = scratch[24:36]
    reduction = scratch[36:]
    total = reduction[0]

    barrier = pltpu.get_barrier_semaphore()
    greeted = [neighbour(mask) for mask in range(1, 16)]
    greeted += [along_y(0, 1), along_y(1), along_y(3)]
    for device in greeted:
        pl.semaphore_signal(barrier, inc=1, device_id=device, device_id_type=MESH)
    pl.semaphore_wait(barrier, len(greeted))

    def copy(rot, kind, src, dst, mask):
        return pltpu.make_async_remote_copy(
            src_ref=src,
            dst_ref=dst,
            send_sem=send_sem.at[rot, kind],
            recv_sem=recv_sem.at[rot, kind],
            device_id=neighbour(mask),
            device_id_type=MESH,
        )

    early, late = pl.ds(0, 6), pl.ds(6, 2)
    copies = []
    for rot in range(ROTS):
        m1, m2, m3, m4 = order(rot)
        own = factors.at[:, pl.ds(rot * PIECE, PIECE), :]
        copies.append(
            [
                copy(rot, 0, own, row[rot].at[pl.ds(6, 6)], m1),
                copy(rot, 1, own, row[rot].at[pl.ds(12, 6)], m2),
                copy(rot, 2, row[rot].at[pl.ds(6, 6)], last[rot], m2),
                copy(rot, 3, send3[rot].at[1, early], passing[rot].at[early], m3),
                copy(rot, 4, send3[rot].at[0, early], final[rot].at[pl.ds(8, 6)], m3),
                copy(rot, 5, send4[rot].at[early], final[rot].at[pl.ds(16, 6)], m4),
                copy(rot, 6, send3[rot].at[1, late], passing[rot].at[late], m3),
                copy(rot, 7, send3[rot].at[0, late], final[rot].at[pl.ds(14, 2)], m3),
                copy(rot, 8, send4[rot].at[late], final[rot].at[pl.ds(22, 2)], m4),
                copy(rot, 9, passing[rot].at[early], final[rot].at[pl.ds(24, 6)], m4),
                copy(rot, 10, passing[rot].at[late], final[rot].at[pl.ds(30, 2)], m4),
            ]
        )
    for rot in range(ROTS):
        copies[rot][0].start()
    for rot in range(ROTS):
        copies[rot][1].start()
    local = []
    for rot in range(ROTS):
        own = factors.at[:, pl.ds(rot * PIECE, PIECE), :]
        local.append(pltpu.make_async_copy(own, row[rot].at[pl.ds(0, 6)], local_sem.at[rot]))
        local[rot].start()
    local.append(pltpu.make_async_copy(integrals, resident, local_sem.at[ROTS]))
    local[ROTS].start()

    fill_table(table, source, slot, partners)

    first = (lax.axis_index("wide") * 8 + lax.axis_index("narrow")) * LMO
    own_rows[...] = jnp.zeros_like(own_rows)
    for i in range(LMO):
        own_rows[i : i + 1, :] = pao_energy[pl.ds(first + i, 1), :] - lmo_energy[first + i]

    def fetch(i, carry):
        for k in range(PARTNERS):
            listed = partners[k, first + i]
            other_energy[i * PARTNERS + k] = pao_energy[pl.ds(listed, 1), :] - lmo_energy[listed]
        return carry

    lax.fori_loop(0, LMO, fetch, 0)
    columns = jnp.transpose(own_rows[...])
    for copying in local:
        copying.wait()
    for i in range(LMO):
        energy[i] = jnp.broadcast_to(columns[:, i : i + 1], (PAO, PAO))
        flipped[:, i * PAO : (i + 1) * PAO] = jnp.transpose(resident[i])

    for rot in range(ROTS):
        copies[rot][0].wait_recv()
        copies[rot][2].start()
    for rot in range(ROTS):
        copies[rot][1].wait_recv()

    def gather(rot, receiver, part):
        start, stop, held = (0, 6, row[rot]) if part == 0 else (6, 8, last[rot])

        def body(at, carry):
            value = held[table[rot * 32 + receiver * 8 + at]]
            if receiver < 2:
                send3[rot][receiver, at] = value
            elif receiver == 2:
                send4[rot][at] = value
            else:
                final[rot][at] = value
            return carry

        lax.fori_loop(start, stop, body, 0)

    for receiver, kind in ((1, 3), (0, 4), (2, 5)):
        for rot in range(ROTS):
            gather(rot, receiver, 0)
            copies[rot][kind].start()
    for rot in range(ROTS):
        copies[rot][2].wait_recv()
        gather(rot, 1, 1)
        copies[rot][6].start()
    for rot in range(ROTS):
        for receiver, kind in ((0, 7), (2, 8)):
            gather(rot, receiver, 1)
            copies[rot][kind].start()
    for rot in range(ROTS):
        gather(rot, 3, 0)
        gather(rot, 3, 1)
    for rot in range(ROTS):
        copies[rot][3].wait_recv()
        copies[rot][9].start()
    for rot in range(ROTS):
        copies[rot][6].wait_recv()
        copies[rot][10].start()
    for rot in range(ROTS):
        for kind in (4, 5, 7, 8, 9, 10):
            copies[rot][kind].wait_recv()

    def one(i, carry):
        mine = jnp.concatenate([row[rot][i] for rot in range(ROTS)], axis=0)
        gathered = jnp.zeros((PAO, AUX), jnp.float32)
        for k in range(PARTNERS):
            pair = i * PARTNERS + k
            other = jnp.concatenate(
                [final[rot][table[128 + rot * PAIRS + pair]] for rot in range(ROTS)], axis=0
            )
            integral = lax.dot_general(
                mine, other, (((1,), (1,)), ((), ())), preferred_element_type=jnp.float32
            )
            amplitude = (integral / (energy[i] + other_energy[pair])).astype(jnp.bfloat16)
            gathered = gathered + jnp.dot(amplitude, other, preferred_element_type=jnp.float32)
        fitted[pl.ds(pl.multiple_of(i * PAO, PAO), PAO), :] = gathered.astype(jnp.bfloat16)
        return carry

    lax.fori_loop(0, LMO, one, 0)

    def rows(block, carry):
        at = pl.ds(pl.multiple_of(block * 256, 256), 256)
        total[at, :] = jnp.dot(flipped[at, :], fitted[...], preferred_element_type=jnp.float32)
        return carry

    lax.fori_loop(0, AUX // 256, rows, 0)

    reduce_total(tile, *reduction)

    for rot in range(ROTS):
        for kind in range(11):
            copies[rot][kind].wait_send()


def local(factors, integrals, pao_energy, lmo_energy, partners):
    vmem = pl.BlockSpec(memory_space=pltpu.VMEM)
    smem = pl.BlockSpec(memory_space=pltpu.SMEM)
    anywhere = pl.BlockSpec(memory_space=pl.ANY)
    piece = (PIECE, AUX)
    scratch = []
    for shape in ((18,), (6,), (2, 8), (8,), (8,), (32,)):
        scratch += [pltpu.VMEM(shape + piece, jnp.bfloat16) for _ in range(ROTS)]
    scratch += [
        pltpu.SMEM((128 + ROTS * PAIRS,), jnp.int32),
        pltpu.SMEM((PAIRS,), jnp.int32),
        pltpu.SMEM((PAIRS,), jnp.int32),
        pltpu.VMEM((LMO, PAO, AUX), jnp.bfloat16),
        pltpu.VMEM((8, PAO), jnp.float32),
        pltpu.VMEM((PAIRS, 1, PAO), jnp.float32),
        pltpu.VMEM((AUX, LMO * PAO), jnp.bfloat16),
        pltpu.VMEM((LMO * PAO, AUX), jnp.bfloat16),
        pltpu.VMEM((LMO, PAO, PAO), jnp.float32),
        pltpu.SemaphoreType.DMA((ROTS + 1,)),
        pltpu.SemaphoreType.DMA((ROTS, 11)),
        pltpu.SemaphoreType.DMA((ROTS, 11)),
        pltpu.VMEM((AUX, AUX), jnp.float32),
        pltpu.VMEM((4, ROWS, AUX), jnp.float32),
        pltpu.VMEM((4, ROWS, AUX), jnp.float32),
        pltpu.VMEM((2, 2, ROWS, AUX // 2), jnp.bfloat16),
        pltpu.VMEM((2, 2, ROWS, AUX // 2), jnp.bfloat16),
        pltpu.VMEM((2, ROWS, AUX // 2), jnp.bfloat16),
        pltpu.VMEM((2, ROWS, AUX // 2), jnp.bfloat16),
        pltpu.VMEM((128, AUX), jnp.float32),
        pltpu.VMEM((AUX, 128), jnp.float32),
        pltpu.VMEM((15, HEIGHT, 128), jnp.float32),
        pltpu.SemaphoreType.DMA((2, 4)),
        pltpu.SemaphoreType.DMA((4, 2)),
        pltpu.SemaphoreType.DMA((2, 15)),
    ]
    return pl.pallas_call(
        kernel,
        out_shape=jax.ShapeDtypeStruct((HEIGHT, ROWS), jnp.float32),
        in_specs=[smem, smem, anywhere, anywhere, vmem],
        out_specs=vmem,
        scratch_shapes=scratch,
        compiler_params=pltpu.CompilerParams(
            collective_id=0, has_side_effects=True, vmem_limit_bytes=60 * 2**20
        ),
    )(partners.T, lmo_energy, factors, integrals, pao_energy)


def solution(mesh):
    in_specs = (P(("wide", "narrow"), None, None), P(("wide", "narrow"), None, None), P(), P(), P())
    out_specs = P("wide", "narrow")
    return jax.shard_map(local, mesh=mesh, in_specs=in_specs, out_specs=out_specs, check_vma=False)
```

```python
import jax
import jax.numpy as jnp
from jax import lax
from jax.experimental import pallas as pl
from jax.experimental.pallas import tpu as pltpu
from jax.sharding import PartitionSpec as P

MESH = pl.DeviceIdType.MESH
LMO = 6
PARTNERS = 4
PAIRS = LMO * PARTNERS
PAO = 256
AUX = 768
ROWS = AUX // 8
HEIGHT = AUX // 16
ROTS = 4
PIECE = PAO // ROTS

MASKS = (1, 4, 3, 12)


def order(rot):
    return [MASKS[(rot + step) % 4] for step in range(4)]


def flip(position, mask):
    if mask == 0:
        return position
    if mask == 3:
        return 3 - position
    if mask == 2:
        return lax.rem(position + 2, 4)
    return position + 1 - 2 * lax.rem(position, 2)


def neighbour(mask):
    wide = lax.axis_index("wide")
    z, x = wide // 4, lax.rem(wide, 4)
    return (flip(z, mask // 4) * 4 + flip(x, mask % 4), lax.axis_index("narrow"))


def along_y(mask, core=0):
    narrow = lax.axis_index("narrow")
    y, c = narrow // 2, lax.rem(narrow, 2)
    return (lax.axis_index("wide"), flip(y, mask) * 2 + flip(c, core))


def reduce_total(
    tile, total, core_in, summed, first_out, first_in, second_out, second_in, block, turned, tiles_in,
    core_sem, y_sem, wide_sem,
):
    narrow, wide = lax.axis_index("narrow"), lax.axis_index("wide")
    y, core = narrow // 2, lax.rem(narrow, 2)

    def send(src, dst, sems, device):
        return pltpu.make_async_remote_copy(
            src_ref=src, dst_ref=dst, send_sem=sems[0], recv_sem=sems[1],
            device_id=device, device_id_type=MESH,
        )

    for i in range(3):
        for j in range(i, 3):
            at_i, at_j = slice(i * 256, i * 256 + 256), slice(j * 256, j * 256 + 256)
            half = 0.5 * (total[at_i, at_j] + jnp.transpose(total[at_j, at_i]))
            total[at_i, at_j] = half
            if i != j:
                total[at_j, at_i] = jnp.transpose(half)

    def band(u, c):
        return pl.ds(pl.multiple_of((flip(y, u) * 2 + c) * ROWS, ROWS), ROWS)

    steps = []
    for u in range(4):
        steps.append(
            send(total.at[band(u, 1 - core)], core_in.at[u],
                 (core_sem.at[0, u], core_sem.at[1, u]), along_y(0, 1))
        )
        steps[u].start()
    for u in (1, 2, 3, 0):
        steps[u].wait_recv()
        summed[u] = total[band(u, core), :] + core_in[u]

    left, right = slice(0, AUX // 2), slice(AUX // 2, AUX)
    plan = ((left, 1, 3, (1, 2)), (right, 3, 1, (3, 2)))
    firsts, seconds = [], []
    for h, (columns, near, far, sent) in enumerate(plan):
        for slot, u in enumerate(sent):
            first_out[h, slot] = summed[u, :, columns].astype(first_out.dtype)
        firsts.append(
            send(first_out.at[h], first_in.at[h], (y_sem.at[0, h], y_sem.at[1, h]), along_y(near))
        )
        firsts[h].start()
    for h, (columns, near, far, sent) in enumerate(plan):
        firsts[h].wait_recv()
        passed = summed[far, :, columns] + first_in[h, 1].astype(jnp.float32)
        second_out[h] = passed.astype(second_out.dtype)
        seconds.append(
            send(second_out.at[h], second_in.at[h], (y_sem.at[2, h], y_sem.at[3, h]), along_y(far))
        )
        seconds[h].start()
    block[pl.ds(ROWS, 128 - ROWS), :] = jnp.zeros((128 - ROWS, AUX), jnp.float32)
    for h, (columns, near, far, sent) in enumerate(plan):
        kept = summed[0, :, columns] + first_in[h, 0].astype(jnp.float32)
        seconds[h].wait_recv()
        block[pl.ds(0, ROWS), columns] = kept + second_in[h].astype(jnp.float32)

    for j in range(AUX // 128):
        at = slice(j * 128, j * 128 + 128)
        turned[at, :] = jnp.transpose(block[:, at])

    def rows(t):
        peer = flip(wide // 4, t // 4) * 4 + flip(lax.rem(wide, 4), t % 4)
        return pl.ds(pl.multiple_of(peer * HEIGHT, HEIGHT), HEIGHT)

    spread = []
    for t in range(1, 16):
        spread.append(
            send(turned.at[rows(t)], tiles_in.at[t - 1],
                 (wide_sem.at[0, t - 1], wide_sem.at[1, t - 1]), neighbour(t))
        )
        spread[-1].start()
    result = turned[rows(0), :]
    for t in range(1, 16):
        spread[t - 1].wait_recv()
        result = result + tiles_in[t - 1]
    tile[...] = result[:, :ROWS]

    for step in steps + firsts + seconds + spread:
        step.wait_send()


def fill_table(table, source, slot, partners):
    wide, narrow = lax.axis_index("wide"), lax.axis_index("narrow")
    z, x = wide // 4, lax.rem(wide, 4)

    def group(mask):
        return flip(z, mask // 4) * 4 + flip(x, mask % 4)

    for rot in range(ROTS):
        m1, m2, m3, m4 = order(rot)
        senders = [group(mask) for mask in (0, m1, m2, m1 ^ m2)]
        for receiver, mask in enumerate((m3, m3 ^ m4, m4, 0)):
            first = (group(mask) * 8 + narrow) * LMO

            def scan(i, found):
                found = list(found)
                for k in range(PARTNERS):
                    listed = partners[k, first + i]
                    owner = lax.div(listed, LMO)
                    place = listed - owner * LMO
                    holder = lax.div(owner, 8)
                    for q in range(4):
                        hit = holder == senders[q]
                        low, high = found[2 * q], found[2 * q + 1]
                        found[2 * q] = jnp.where(hit, jnp.minimum(low, place), low)
                        found[2 * q + 1] = jnp.where(hit, jnp.maximum(high, place), high)
                return tuple(found)

            found = lax.fori_loop(0, LMO, scan, (jnp.int32(LMO - 1), jnp.int32(0)) * 4)
            for q in range(4):
                for k in range(2):
                    base = q * LMO if q < 3 else 0
                    table[rot * 32 + receiver * 8 + q * 2 + k] = found[2 * q + k] + base

    first = (wide * 8 + narrow) * LMO

    def split(i, carry):
        for k in range(PARTNERS):
            listed = partners[k, first + i]
            owner = lax.div(listed, LMO)
            source[i * PARTNERS + k] = lax.div(owner, 8)
            slot[i * PARTNERS + k] = listed - owner * LMO
        return carry

    lax.fori_loop(0, LMO, split, 0)

    def place(pair, carry):
        mine, mine_slot = source[pair], slot[pair]

        def larger(i, most):
            for k in range(PARTNERS):
                there = slot[i * PARTNERS + k]
                most = jnp.where(source[i * PARTNERS + k] == mine, jnp.maximum(most, there), most)
            return most

        most = lax.fori_loop(0, LMO, larger, jnp.int32(0))
        is_high = jnp.where(mine_slot == most, 1, 0)
        sz = lax.div(mine, 4)
        sx = mine - sz * 4
        digit = {}
        for low_mask, high_mask, here, there in ((1, 3, x, sx), (4, 12, z, sz)):
            digit[low_mask] = jnp.where((flip(here, 1) == there) | (flip(here, 2) == there), 1, 0)
            digit[high_mask] = jnp.where((flip(here, 3) == there) | (flip(here, 2) == there), 1, 0)
        for rot in range(ROTS):
            m1, m2, m3, m4 = order(rot)
            block = (digit[m3] + 2 * digit[m4]) * 4 + digit[m1] + 2 * digit[m2]
            table[128 + rot * PAIRS + pair] = block * 2 + is_high
        return carry

    lax.fori_loop(0, PAIRS, place, 0)


def kernel(partners, lmo_energy, factors, integrals, pao_energy, tile, *scratch):
    row = list(scratch[0:4])
    last = list(scratch[4:8])
    send3 = list(scratch[8:12])
    send4 = list(scratch[12:16])
    passing = list(scratch[16:20])
    final = list(scratch[20:24])
    (table, source, slot, resident, own_rows, other_energy, flipped, fitted, energy,
     local_sem, send_sem, recv_sem) = scratch[24:36]
    reduction = scratch[36:]
    total = reduction[0]

    barrier = pltpu.get_barrier_semaphore()
    greeted = [neighbour(mask) for mask in MASKS] + [along_y(0, 1), along_y(1), along_y(3)]
    for device in greeted:
        pl.semaphore_signal(barrier, inc=1, device_id=device, device_id_type=MESH)
    pl.semaphore_wait(barrier, len(greeted))

    def copy(rot, kind, src, dst, mask):
        return pltpu.make_async_remote_copy(
            src_ref=src,
            dst_ref=dst,
            send_sem=send_sem.at[rot, kind],
            recv_sem=recv_sem.at[rot, kind],
            device_id=neighbour(mask),
            device_id_type=MESH,
        )

    early, late = pl.ds(0, 6), pl.ds(6, 2)
    copies = []
    for rot in range(ROTS):
        m1, m2, m3, m4 = order(rot)
        own = factors.at[:, pl.ds(rot * PIECE, PIECE), :]
        copies.append(
            [
                copy(rot, 0, own, row[rot].at[pl.ds(6, 6)], m1),
                copy(rot, 1, own, row[rot].at[pl.ds(12, 6)], m2),
                copy(rot, 2, row[rot].at[pl.ds(6, 6)], last[rot], m2),
                copy(rot, 3, send3[rot].at[1, early], passing[rot].at[early], m3),
                copy(rot, 4, send3[rot].at[0, early], final[rot].at[pl.ds(8, 6)], m3),
                copy(rot, 5, send4[rot].at[early], final[rot].at[pl.ds(16, 6)], m4),
                copy(rot, 6, send3[rot].at[1, late], passing[rot].at[late], m3),
                copy(rot, 7, send3[rot].at[0, late], final[rot].at[pl.ds(14, 2)], m3),
                copy(rot, 8, send4[rot].at[late], final[rot].at[pl.ds(22, 2)], m4),
                copy(rot, 9, passing[rot].at[early], final[rot].at[pl.ds(24, 6)], m4),
                copy(rot, 10, passing[rot].at[late], final[rot].at[pl.ds(30, 2)], m4),
            ]
        )
    for rot in range(ROTS):
        copies[rot][0].start()
    for rot in range(ROTS):
        copies[rot][1].start()
    local = []
    for rot in range(ROTS):
        own = factors.at[:, pl.ds(rot * PIECE, PIECE), :]
        local.append(pltpu.make_async_copy(own, row[rot].at[pl.ds(0, 6)], local_sem.at[rot]))
        local[rot].start()
    local.append(pltpu.make_async_copy(integrals, resident, local_sem.at[ROTS]))
    local[ROTS].start()

    fill_table(table, source, slot, partners)

    first = (lax.axis_index("wide") * 8 + lax.axis_index("narrow")) * LMO
    own_rows[...] = jnp.zeros_like(own_rows)
    for i in range(LMO):
        own_rows[i : i + 1, :] = pao_energy[pl.ds(first + i, 1), :] - lmo_energy[first + i]

    def fetch(i, carry):
        for k in range(PARTNERS):
            listed = partners[k, first + i]
            other_energy[i * PARTNERS + k] = pao_energy[pl.ds(listed, 1), :] - lmo_energy[listed]
        return carry

    lax.fori_loop(0, LMO, fetch, 0)
    columns = jnp.transpose(own_rows[...])
    for copying in local:
        copying.wait()
    for i in range(LMO):
        energy[i] = jnp.broadcast_to(columns[:, i : i + 1], (PAO, PAO))
        flipped[:, i * PAO : (i + 1) * PAO] = jnp.transpose(resident[i])

    for rot in range(ROTS):
        copies[rot][0].wait_recv()
        copies[rot][2].start()
    for rot in range(ROTS):
        copies[rot][1].wait_recv()

    def gather(rot, receiver, part):
        start, stop, held = (0, 6, row[rot]) if part == 0 else (6, 8, last[rot])

        def body(at, carry):
            value = held[table[rot * 32 + receiver * 8 + at]]
            if receiver < 2:
                send3[rot][receiver, at] = value
            elif receiver == 2:
                send4[rot][at] = value
            else:
                final[rot][at] = value
            return carry

        lax.fori_loop(start, stop, body, 0)

    for receiver, kind in ((1, 3), (0, 4), (2, 5)):
        for rot in range(ROTS):
            gather(rot, receiver, 0)
            copies[rot][kind].start()
    for rot in range(ROTS):
        copies[rot][2].wait_recv()
        gather(rot, 1, 1)
        copies[rot][6].start()
    for rot in range(ROTS):
        for receiver, kind in ((0, 7), (2, 8)):
            gather(rot, receiver, 1)
            copies[rot][kind].start()
    for rot in range(ROTS):
        gather(rot, 3, 0)
        gather(rot, 3, 1)
    for rot in range(ROTS):
        copies[rot][3].wait_recv()
        copies[rot][9].start()
    for rot in range(ROTS):
        copies[rot][6].wait_recv()
        copies[rot][10].start()
    for rot in range(ROTS):
        for kind in (4, 5, 7, 8, 9, 10):
            copies[rot][kind].wait_recv()

    def one(i, carry):
        mine = jnp.concatenate([row[rot][i] for rot in range(ROTS)], axis=0)
        others = jnp.concatenate(
            [
                final[rot][table[128 + rot * PAIRS + i * PARTNERS + k]]
                for k in range(PARTNERS)
                for rot in range(ROTS)
            ],
            axis=0,
        )
        integral = lax.dot_general(
            mine, others, (((1,), (1,)), ((), ())), preferred_element_type=jnp.float32
        )
        amplitude = jnp.concatenate(
            [
                (integral[:, k * PAO : (k + 1) * PAO] / (energy[i] + other_energy[i * PARTNERS + k]))
                for k in range(PARTNERS)
            ],
            axis=1,
        ).astype(jnp.bfloat16)
        gathered = jnp.dot(amplitude, others, preferred_element_type=jnp.float32)
        fitted[pl.ds(pl.multiple_of(i * PAO, PAO), PAO), :] = gathered.astype(jnp.bfloat16)
        return carry

    lax.fori_loop(0, LMO, one, 0)

    def rows(block, carry):
        at = pl.ds(pl.multiple_of(block * 256, 256), 256)
        total[at, :] = jnp.dot(flipped[at, :], fitted[...], preferred_element_type=jnp.float32)
        return carry

    lax.fori_loop(0, AUX // 256, rows, 0)

    reduce_total(tile, *reduction)

    for rot in range(ROTS):
        for kind in range(11):
            copies[rot][kind].wait_send()


def local(factors, integrals, pao_energy, lmo_energy, partners):
    vmem = pl.BlockSpec(memory_space=pltpu.VMEM)
    smem = pl.BlockSpec(memory_space=pltpu.SMEM)
    anywhere = pl.BlockSpec(memory_space=pl.ANY)
    piece = (PIECE, AUX)
    scratch = []
    for shape in ((18,), (6,), (2, 8), (8,), (8,), (32,)):
        scratch += [pltpu.VMEM(shape + piece, jnp.bfloat16) for _ in range(ROTS)]
    scratch += [
        pltpu.SMEM((128 + ROTS * PAIRS,), jnp.int32),
        pltpu.SMEM((PAIRS,), jnp.int32),
        pltpu.SMEM((PAIRS,), jnp.int32),
        pltpu.VMEM((LMO, PAO, AUX), jnp.bfloat16),
        pltpu.VMEM((8, PAO), jnp.float32),
        pltpu.VMEM((PAIRS, 1, PAO), jnp.float32),
        pltpu.VMEM((AUX, LMO * PAO), jnp.bfloat16),
        pltpu.VMEM((LMO * PAO, AUX), jnp.bfloat16),
        pltpu.VMEM((LMO, PAO, PAO), jnp.float32),
        pltpu.SemaphoreType.DMA((ROTS + 1,)),
        pltpu.SemaphoreType.DMA((ROTS, 11)),
        pltpu.SemaphoreType.DMA((ROTS, 11)),
        pltpu.VMEM((AUX, AUX), jnp.float32),
        pltpu.VMEM((4, ROWS, AUX), jnp.float32),
        pltpu.VMEM((4, ROWS, AUX), jnp.float32),
        pltpu.VMEM((2, 2, ROWS, AUX // 2), jnp.bfloat16),
        pltpu.VMEM((2, 2, ROWS, AUX // 2), jnp.bfloat16),
        pltpu.VMEM((2, ROWS, AUX // 2), jnp.bfloat16),
        pltpu.VMEM((2, ROWS, AUX // 2), jnp.bfloat16),
        pltpu.VMEM((128, AUX), jnp.float32),
        pltpu.VMEM((AUX, 128), jnp.float32),
        pltpu.VMEM((15, HEIGHT, 128), jnp.float32),
        pltpu.SemaphoreType.DMA((2, 4)),
        pltpu.SemaphoreType.DMA((4, 2)),
        pltpu.SemaphoreType.DMA((2, 15)),
    ]
    return pl.pallas_call(
        kernel,
        out_shape=jax.ShapeDtypeStruct((HEIGHT, ROWS), jnp.float32),
        in_specs=[smem, smem, anywhere, anywhere, vmem],
        out_specs=vmem,
        scratch_shapes=scratch,
        compiler_params=pltpu.CompilerParams(
            collective_id=0, has_side_effects=True, vmem_limit_bytes=60 * 2**20
        ),
    )(partners.T, lmo_energy, factors, integrals, pao_energy)


def solution(mesh):
    in_specs = (P(("wide", "narrow"), None, None), P(("wide", "narrow"), None, None), P(), P(), P())
    out_specs = P("wide", "narrow")
    return jax.shard_map(local, mesh=mesh, in_specs=in_specs, out_specs=out_specs, check_vma=False)
```

```python
import jax
import jax.numpy as jnp
from jax import lax
from jax.experimental import pallas as pl
from jax.experimental.pallas import tpu as pltpu
from jax.sharding import PartitionSpec as P

MESH = pl.DeviceIdType.MESH
LMO = 6
PARTNERS = 4
PAIRS = LMO * PARTNERS
PAO = 256
AUX = 768
ROWS = AUX // 8
HEIGHT = AUX // 16
CHUNKS = AUX // 2 // 128
ROTS = 4
PIECE = PAO // ROTS

MASKS = (1, 4, 3, 12)


def order(rot):
    return [MASKS[(rot + step) % 4] for step in range(4)]


def flip(position, mask):
    if mask == 0:
        return position
    if mask == 3:
        return 3 - position
    if mask == 2:
        return lax.rem(position + 2, 4)
    return position + 1 - 2 * lax.rem(position, 2)


def neighbour(mask):
    wide = lax.axis_index("wide")
    z, x = wide // 4, lax.rem(wide, 4)
    return (flip(z, mask // 4) * 4 + flip(x, mask % 4), lax.axis_index("narrow"))


def along_y(mask, core=0):
    narrow = lax.axis_index("narrow")
    y, c = narrow // 2, lax.rem(narrow, 2)
    return (lax.axis_index("wide"), flip(y, mask) * 2 + flip(c, core))


def reduce_total(
    tile, total, core_in, summed, first_out, first_in, second_out, second_in, block, turned, outgoing, tiles_in,
    core_sem, y_sem, wide_sem,
):
    narrow, wide = lax.axis_index("narrow"), lax.axis_index("wide")
    y, core = narrow // 2, lax.rem(narrow, 2)

    def send(src, dst, sems, device):
        return pltpu.make_async_remote_copy(
            src_ref=src, dst_ref=dst, send_sem=sems[0], recv_sem=sems[1],
            device_id=device, device_id_type=MESH,
        )

    for i in range(3):
        for j in range(i, 3):
            at_i, at_j = slice(i * 256, i * 256 + 256), slice(j * 256, j * 256 + 256)
            half = 0.5 * (total[at_i, at_j] + jnp.transpose(total[at_j, at_i]))
            total[at_i, at_j] = half
            if i != j:
                total[at_j, at_i] = jnp.transpose(half)

    def band(u, c):
        return pl.ds(pl.multiple_of((flip(y, u) * 2 + c) * ROWS, ROWS), ROWS)

    steps = []
    for u in range(4):
        steps.append(
            send(total.at[band(u, 1 - core)], core_in.at[u],
                 (core_sem.at[0, u], core_sem.at[1, u]), along_y(0, 1))
        )
        steps[u].start()
    for u in (1, 2, 3, 0):
        steps[u].wait_recv()
        summed[u] = total[band(u, core), :] + core_in[u]

    plan = ((1, 3, (1, 2)), (3, 1, (3, 2)))
    firsts, seconds = {}, {}
    chunks = [(h, chunk) for chunk in range(CHUNKS) for h in range(2)]

    def columns(h, chunk):
        start = h * (AUX // 2) + chunk * 128
        return slice(start, start + 128)

    for h, chunk in chunks:
        near, far, sent = plan[h]
        for place, u in enumerate(sent):
            first_out[h, chunk, place] = summed[u, :, columns(h, chunk)].astype(first_out.dtype)
        firsts[h, chunk] = send(
            first_out.at[h, chunk], first_in.at[h, chunk],
            (y_sem.at[0, h, chunk], y_sem.at[1, h, chunk]), along_y(near),
        )
        firsts[h, chunk].start()
    block[pl.ds(ROWS, 128 - ROWS), :] = jnp.zeros((128 - ROWS, AUX), jnp.float32)
    for h, chunk in chunks:
        near, far, sent = plan[h]
        firsts[h, chunk].wait_recv()
        passed = summed[far, :, columns(h, chunk)] + first_in[h, chunk, 1].astype(jnp.float32)
        second_out[h, chunk] = passed.astype(second_out.dtype)
        seconds[h, chunk] = send(
            second_out.at[h, chunk], second_in.at[h, chunk],
            (y_sem.at[2, h, chunk], y_sem.at[3, h, chunk]), along_y(far),
        )
        seconds[h, chunk].start()
    for h, chunk in chunks:
        at = columns(h, chunk)
        kept = summed[0, :, at] + first_in[h, chunk, 0].astype(jnp.float32)
        seconds[h, chunk].wait_recv()
        block[pl.ds(0, ROWS), at] = kept + second_in[h, chunk].astype(jnp.float32)
        turned[at, :] = jnp.transpose(block[:, at])
        outgoing[at, :] = turned[at, :].astype(outgoing.dtype)

    def rows(t):
        peer = flip(wide // 4, t // 4) * 4 + flip(lax.rem(wide, 4), t % 4)
        return pl.ds(pl.multiple_of(peer * HEIGHT, HEIGHT), HEIGHT)

    spread = []
    for t in range(1, 16):
        spread.append(
            send(outgoing.at[rows(t)], tiles_in.at[t - 1],
                 (wide_sem.at[0, t - 1], wide_sem.at[1, t - 1]), neighbour(t))
        )
        spread[-1].start()
    result = turned[rows(0), :]
    for t in range(1, 16):
        spread[t - 1].wait_recv()
        result = result + tiles_in[t - 1].astype(jnp.float32)
    tile[...] = result[:, :ROWS]

    for step in steps + list(firsts.values()) + list(seconds.values()) + spread:
        step.wait_send()


def fill_table(table, source, slot, partners):
    wide, narrow = lax.axis_index("wide"), lax.axis_index("narrow")
    z, x = wide // 4, lax.rem(wide, 4)

    def group(mask):
        return flip(z, mask // 4) * 4 + flip(x, mask % 4)

    for rot in range(ROTS):
        m1, m2, m3, m4 = order(rot)
        senders = [group(mask) for mask in (0, m1, m2, m1 ^ m2)]
        for receiver, mask in enumerate((m3, m3 ^ m4, m4, 0)):
            first = (group(mask) * 8 + narrow) * LMO

            def scan(i, found):
                found = list(found)
                for k in range(PARTNERS):
                    listed = partners[k, first + i]
                    owner = lax.div(listed, LMO)
                    place = listed - owner * LMO
                    holder = lax.div(owner, 8)
                    for q in range(4):
                        hit = holder == senders[q]
                        low, high = found[2 * q], found[2 * q + 1]
                        found[2 * q] = jnp.where(hit, jnp.minimum(low, place), low)
                        found[2 * q + 1] = jnp.where(hit, jnp.maximum(high, place), high)
                return tuple(found)

            found = lax.fori_loop(0, LMO, scan, (jnp.int32(LMO - 1), jnp.int32(0)) * 4)
            for q in range(4):
                for k in range(2):
                    base = q * LMO if q < 3 else 0
                    table[rot * 32 + receiver * 8 + q * 2 + k] = found[2 * q + k] + base

    first = (wide * 8 + narrow) * LMO

    def split(i, carry):
        for k in range(PARTNERS):
            listed = partners[k, first + i]
            owner = lax.div(listed, LMO)
            source[i * PARTNERS + k] = lax.div(owner, 8)
            slot[i * PARTNERS + k] = listed - owner * LMO
        return carry

    lax.fori_loop(0, LMO, split, 0)

    def place(pair, carry):
        mine, mine_slot = source[pair], slot[pair]

        def larger(i, most):
            for k in range(PARTNERS):
                there = slot[i * PARTNERS + k]
                most = jnp.where(source[i * PARTNERS + k] == mine, jnp.maximum(most, there), most)
            return most

        most = lax.fori_loop(0, LMO, larger, jnp.int32(0))
        is_high = jnp.where(mine_slot == most, 1, 0)
        sz = lax.div(mine, 4)
        sx = mine - sz * 4
        digit = {}
        for low_mask, high_mask, here, there in ((1, 3, x, sx), (4, 12, z, sz)):
            digit[low_mask] = jnp.where((flip(here, 1) == there) | (flip(here, 2) == there), 1, 0)
            digit[high_mask] = jnp.where((flip(here, 3) == there) | (flip(here, 2) == there), 1, 0)
        for rot in range(ROTS):
            m1, m2, m3, m4 = order(rot)
            block = (digit[m3] + 2 * digit[m4]) * 4 + digit[m1] + 2 * digit[m2]
            table[128 + rot * PAIRS + pair] = block * 2 + is_high
        return carry

    lax.fori_loop(0, PAIRS, place, 0)


def kernel(partners, lmo_energy, factors, integrals, pao_energy, tile, *scratch):
    row = list(scratch[0:4])
    last = list(scratch[4:8])
    send3 = list(scratch[8:12])
    send4 = list(scratch[12:16])
    passing = list(scratch[16:20])
    final = list(scratch[20:24])
    (table, source, slot, resident, own_rows, other_energy, flipped, fitted, energy,
     local_sem, send_sem, recv_sem) = scratch[24:36]
    reduction = scratch[36:]
    total = reduction[0]

    barrier = pltpu.get_barrier_semaphore()
    greeted = [neighbour(mask) for mask in MASKS] + [along_y(0, 1), along_y(1), along_y(3)]
    for device in greeted:
        pl.semaphore_signal(barrier, inc=1, device_id=device, device_id_type=MESH)
    pl.semaphore_wait(barrier, len(greeted))

    def copy(rot, kind, src, dst, mask):
        return pltpu.make_async_remote_copy(
            src_ref=src,
            dst_ref=dst,
            send_sem=send_sem.at[rot, kind],
            recv_sem=recv_sem.at[rot, kind],
            device_id=neighbour(mask),
            device_id_type=MESH,
        )

    early, late = pl.ds(0, 6), pl.ds(6, 2)
    copies = []
    for rot in range(ROTS):
        m1, m2, m3, m4 = order(rot)
        own = factors.at[:, pl.ds(rot * PIECE, PIECE), :]
        copies.append(
            [
                copy(rot, 0, own, row[rot].at[pl.ds(6, 6)], m1),
                copy(rot, 1, own, row[rot].at[pl.ds(12, 6)], m2),
                copy(rot, 2, row[rot].at[pl.ds(6, 6)], last[rot], m2),
                copy(rot, 3, send3[rot].at[1, early], passing[rot].at[early], m3),
                copy(rot, 4, send3[rot].at[0, early], final[rot].at[pl.ds(8, 6)], m3),
                copy(rot, 5, send4[rot].at[early], final[rot].at[pl.ds(16, 6)], m4),
                copy(rot, 6, send3[rot].at[1, late], passing[rot].at[late], m3),
                copy(rot, 7, send3[rot].at[0, late], final[rot].at[pl.ds(14, 2)], m3),
                copy(rot, 8, send4[rot].at[late], final[rot].at[pl.ds(22, 2)], m4),
                copy(rot, 9, passing[rot].at[early], final[rot].at[pl.ds(24, 6)], m4),
                copy(rot, 10, passing[rot].at[late], final[rot].at[pl.ds(30, 2)], m4),
            ]
        )
    for rot in range(ROTS):
        copies[rot][0].start()
    for rot in range(ROTS):
        copies[rot][1].start()
    local = []
    for rot in range(ROTS):
        own = factors.at[:, pl.ds(rot * PIECE, PIECE), :]
        local.append(pltpu.make_async_copy(own, row[rot].at[pl.ds(0, 6)], local_sem.at[rot]))
        local[rot].start()
    local.append(pltpu.make_async_copy(integrals, resident, local_sem.at[ROTS]))
    local[ROTS].start()

    fill_table(table, source, slot, partners)

    first = (lax.axis_index("wide") * 8 + lax.axis_index("narrow")) * LMO
    own_rows[...] = jnp.zeros_like(own_rows)
    for i in range(LMO):
        own_rows[i : i + 1, :] = pao_energy[pl.ds(first + i, 1), :] - lmo_energy[first + i]

    def fetch(i, carry):
        for k in range(PARTNERS):
            listed = partners[k, first + i]
            other_energy[i * PARTNERS + k] = pao_energy[pl.ds(listed, 1), :] - lmo_energy[listed]
        return carry

    lax.fori_loop(0, LMO, fetch, 0)
    columns = jnp.transpose(own_rows[...])
    for copying in local:
        copying.wait()
    for i in range(LMO):
        energy[i] = jnp.broadcast_to(columns[:, i : i + 1], (PAO, PAO))
        flipped[:, i * PAO : (i + 1) * PAO] = jnp.transpose(resident[i])

    for rot in range(ROTS):
        copies[rot][0].wait_recv()
        copies[rot][2].start()
    for rot in range(ROTS):
        copies[rot][1].wait_recv()

    def gather(rot, receiver, part):
        start, stop, held = (0, 6, row[rot]) if part == 0 else (6, 8, last[rot])

        def body(at, carry):
            value = held[table[rot * 32 + receiver * 8 + at]]
            if receiver < 2:
                send3[rot][receiver, at] = value
            elif receiver == 2:
                send4[rot][at] = value
            else:
                final[rot][at] = value
            return carry

        lax.fori_loop(start, stop, body, 0)

    for receiver, kind in ((1, 3), (0, 4), (2, 5)):
        for rot in range(ROTS):
            gather(rot, receiver, 0)
            copies[rot][kind].start()
    for rot in range(ROTS):
        copies[rot][2].wait_recv()
        gather(rot, 1, 1)
        copies[rot][6].start()
    for rot in range(ROTS):
        for receiver, kind in ((0, 7), (2, 8)):
            gather(rot, receiver, 1)
            copies[rot][kind].start()
    for rot in range(ROTS):
        gather(rot, 3, 0)
        gather(rot, 3, 1)
    for rot in range(ROTS):
        copies[rot][3].wait_recv()
        copies[rot][9].start()
    for rot in range(ROTS):
        copies[rot][6].wait_recv()
        copies[rot][10].start()
    for rot in range(ROTS):
        for kind in (4, 5, 7, 8, 9, 10):
            copies[rot][kind].wait_recv()

    def one(i, carry):
        mine = jnp.concatenate([row[rot][i] for rot in range(ROTS)], axis=0)
        others = jnp.concatenate(
            [
                final[rot][table[128 + rot * PAIRS + i * PARTNERS + k]]
                for k in range(PARTNERS)
                for rot in range(ROTS)
            ],
            axis=0,
        )
        integral = lax.dot_general(
            mine, others, (((1,), (1,)), ((), ())), preferred_element_type=jnp.float32
        )
        amplitude = jnp.concatenate(
            [
                (integral[:, k * PAO : (k + 1) * PAO] / (energy[i] + other_energy[i * PARTNERS + k]))
                for k in range(PARTNERS)
            ],
            axis=1,
        ).astype(jnp.bfloat16)
        gathered = jnp.dot(amplitude, others, preferred_element_type=jnp.float32)
        fitted[pl.ds(pl.multiple_of(i * PAO, PAO), PAO), :] = gathered.astype(jnp.bfloat16)
        return carry

    lax.fori_loop(0, LMO, one, 0)

    def rows(block, carry):
        at = pl.ds(pl.multiple_of(block * 256, 256), 256)
        total[at, :] = jnp.dot(flipped[at, :], fitted[...], preferred_element_type=jnp.float32)
        return carry

    lax.fori_loop(0, AUX // 256, rows, 0)

    reduce_total(tile, *reduction)

    for rot in range(ROTS):
        for kind in range(11):
            copies[rot][kind].wait_send()


def local(factors, integrals, pao_energy, lmo_energy, partners):
    vmem = pl.BlockSpec(memory_space=pltpu.VMEM)
    smem = pl.BlockSpec(memory_space=pltpu.SMEM)
    anywhere = pl.BlockSpec(memory_space=pl.ANY)
    piece = (PIECE, AUX)
    scratch = []
    for shape in ((18,), (6,), (2, 8), (8,), (8,), (32,)):
        scratch += [pltpu.VMEM(shape + piece, jnp.bfloat16) for _ in range(ROTS)]
    scratch += [
        pltpu.SMEM((128 + ROTS * PAIRS,), jnp.int32),
        pltpu.SMEM((PAIRS,), jnp.int32),
        pltpu.SMEM((PAIRS,), jnp.int32),
        pltpu.VMEM((LMO, PAO, AUX), jnp.bfloat16),
        pltpu.VMEM((8, PAO), jnp.float32),
        pltpu.VMEM((PAIRS, 1, PAO), jnp.float32),
        pltpu.VMEM((AUX, LMO * PAO), jnp.bfloat16),
        pltpu.VMEM((LMO * PAO, AUX), jnp.bfloat16),
        pltpu.VMEM((LMO, PAO, PAO), jnp.float32),
        pltpu.SemaphoreType.DMA((ROTS + 1,)),
        pltpu.SemaphoreType.DMA((ROTS, 11)),
        pltpu.SemaphoreType.DMA((ROTS, 11)),
        pltpu.VMEM((AUX, AUX), jnp.float32),
        pltpu.VMEM((4, ROWS, AUX), jnp.float32),
        pltpu.VMEM((4, ROWS, AUX), jnp.float32),
        pltpu.VMEM((2, CHUNKS, 2, ROWS, 128), jnp.bfloat16),
        pltpu.VMEM((2, CHUNKS, 2, ROWS, 128), jnp.bfloat16),
        pltpu.VMEM((2, CHUNKS, ROWS, 128), jnp.bfloat16),
        pltpu.VMEM((2, CHUNKS, ROWS, 128), jnp.bfloat16),
        pltpu.VMEM((128, AUX), jnp.float32),
        pltpu.VMEM((AUX, 128), jnp.float32),
        pltpu.VMEM((AUX, 128), jnp.bfloat16),
        pltpu.VMEM((15, HEIGHT, 128), jnp.bfloat16),
        pltpu.SemaphoreType.DMA((2, 4)),
        pltpu.SemaphoreType.DMA((4, 2, CHUNKS)),
        pltpu.SemaphoreType.DMA((2, 15)),
    ]
    return pl.pallas_call(
        kernel,
        out_shape=jax.ShapeDtypeStruct((HEIGHT, ROWS), jnp.float32),
        in_specs=[smem, smem, anywhere, anywhere, vmem],
        out_specs=vmem,
        scratch_shapes=scratch,
        compiler_params=pltpu.CompilerParams(
            collective_id=0, has_side_effects=True, vmem_limit_bytes=60 * 2**20
        ),
    )(partners.T, lmo_energy, factors, integrals, pao_energy)


def solution(mesh):
    in_specs = (P(("wide", "narrow"), None, None), P(("wide", "narrow"), None, None), P(), P(), P())
    out_specs = P("wide", "narrow")
    return jax.shard_map(local, mesh=mesh, in_specs=in_specs, out_specs=out_specs, check_vma=False)
```

```python
import jax
import jax.numpy as jnp
from jax import lax
from jax.experimental import pallas as pl
from jax.experimental.pallas import tpu as pltpu
from jax.sharding import PartitionSpec as P

MESH = pl.DeviceIdType.MESH
LMO = 6
PARTNERS = 4
PAIRS = LMO * PARTNERS
PAO = 256
AUX = 768
ROWS = AUX // 8
HEIGHT = AUX // 16
CHUNKS = AUX // 2 // 128
ROTS = 4
PIECE = PAO // ROTS
ONCE = 8

AT_ONCE = 128 + ROTS * PAIRS
AT_RANK = AT_ONCE + PAIRS
AT_LIST = AT_RANK + PAIRS

MASKS = (1, 4, 3, 12)


def order(rot):
    return [MASKS[(rot + step) % 4] for step in range(4)]


def flip(position, mask):
    if mask == 0:
        return position
    if mask == 3:
        return 3 - position
    if mask == 2:
        return lax.rem(position + 2, 4)
    return position + 1 - 2 * lax.rem(position, 2)


def neighbour(mask):
    wide = lax.axis_index("wide")
    z, x = wide // 4, lax.rem(wide, 4)
    return (flip(z, mask // 4) * 4 + flip(x, mask % 4), lax.axis_index("narrow"))


def along_y(mask, core=0):
    narrow = lax.axis_index("narrow")
    y, c = narrow // 2, lax.rem(narrow, 2)
    return (lax.axis_index("wide"), flip(y, mask) * 2 + flip(c, core))


def reduce_total(
    tile, flipped, fitted, total, core_in, summed, first_out, first_in, second_out, second_in, block, turned, outgoing, tiles_in,
    core_sem, y_sem, wide_sem,
):
    narrow, wide = lax.axis_index("narrow"), lax.axis_index("wide")
    y, core = narrow // 2, lax.rem(narrow, 2)

    def send(src, dst, sems, device):
        return pltpu.make_async_remote_copy(
            src_ref=src, dst_ref=dst, send_sem=sems[0], recv_sem=sems[1],
            device_id=device, device_id_type=MESH,
        )

    def multiply(i, j):
        rows, columns = slice(i * 256, i * 256 + 256), slice(j * 256, j * 256 + 256)
        total[rows, columns] = jnp.dot(
            flipped[rows, :],
            fitted[:, :, columns].reshape(LMO * PAO, 256),
            preferred_element_type=jnp.float32,
        )

    def symmetrise(i, j):
        at_i, at_j = slice(i * 256, i * 256 + 256), slice(j * 256, j * 256 + 256)
        half = 0.5 * (total[at_i, at_j] + jnp.transpose(total[at_j, at_i]))
        total[at_i, at_j] = half
        if i != j:
            total[at_j, at_i] = jnp.transpose(half)

    def band(place, c):
        return pl.ds(pl.multiple_of((place * 2 + c) * ROWS, ROWS), ROWS)

    steps = []
    for i, ready in enumerate(((0,), (1,), (2, 3))):
        for j in range(i, 3):
            multiply(i, j)
            if i != j:
                multiply(j, i)
        for j in range(i, 3):
            symmetrise(i, j)
        for place in ready:
            steps.append(
                send(total.at[band(place, 1 - core)], core_in.at[place],
                     (core_sem.at[0, place], core_sem.at[1, place]), along_y(0, 1))
            )
            steps[-1].start()
    for step in steps:
        step.wait_recv()
    for u in (1, 2, 3, 0):
        place = flip(y, u)
        summed[u] = total[band(place, core), :] + core_in[place]

    plan = ((1, 3, (1, 2)), (3, 1, (3, 2)))
    firsts, seconds = {}, {}
    chunks = [(h, chunk) for chunk in range(CHUNKS) for h in range(2)]

    def columns(h, chunk):
        start = h * (AUX // 2) + chunk * 128
        return slice(start, start + 128)

    for h, chunk in chunks:
        near, far, sent = plan[h]
        for place, u in enumerate(sent):
            first_out[h, chunk, place] = summed[u, :, columns(h, chunk)].astype(first_out.dtype)
        firsts[h, chunk] = send(
            first_out.at[h, chunk], first_in.at[h, chunk],
            (y_sem.at[0, h, chunk], y_sem.at[1, h, chunk]), along_y(near),
        )
        firsts[h, chunk].start()
    block[pl.ds(ROWS, 128 - ROWS), :] = jnp.zeros((128 - ROWS, AUX), jnp.float32)
    for h, chunk in chunks:
        near, far, sent = plan[h]
        firsts[h, chunk].wait_recv()
        passed = summed[far, :, columns(h, chunk)] + first_in[h, chunk, 1].astype(jnp.float32)
        second_out[h, chunk] = passed.astype(second_out.dtype)
        seconds[h, chunk] = send(
            second_out.at[h, chunk], second_in.at[h, chunk],
            (y_sem.at[2, h, chunk], y_sem.at[3, h, chunk]), along_y(far),
        )
        seconds[h, chunk].start()
    for h, chunk in chunks:
        at = columns(h, chunk)
        kept = summed[0, :, at] + first_in[h, chunk, 0].astype(jnp.float32)
        seconds[h, chunk].wait_recv()
        block[pl.ds(0, ROWS), at] = kept + second_in[h, chunk].astype(jnp.float32)
        turned[at, :] = jnp.transpose(block[:, at])
        outgoing[at, :] = turned[at, :].astype(outgoing.dtype)

    def rows(t):
        peer = flip(wide // 4, t // 4) * 4 + flip(lax.rem(wide, 4), t % 4)
        return pl.ds(pl.multiple_of(peer * HEIGHT, HEIGHT), HEIGHT)

    spread = []
    for t in range(1, 16):
        spread.append(
            send(outgoing.at[rows(t)], tiles_in.at[t - 1],
                 (wide_sem.at[0, t - 1], wide_sem.at[1, t - 1]), neighbour(t))
        )
        spread[-1].start()
    result = turned[rows(0), :]
    for t in range(1, 16):
        spread[t - 1].wait_recv()
        result = result + tiles_in[t - 1].astype(jnp.float32)
    tile[...] = result[:, :ROWS]

    for step in steps + list(firsts.values()) + list(seconds.values()) + spread:
        step.wait_send()


def fill_table(table, source, slot, partners):
    wide, narrow = lax.axis_index("wide"), lax.axis_index("narrow")
    z, x = wide // 4, lax.rem(wide, 4)

    def group(mask):
        return flip(z, mask // 4) * 4 + flip(x, mask % 4)

    for rot in range(ROTS):
        m1, m2, m3, m4 = order(rot)
        senders = [group(mask) for mask in (0, m1, m2, m1 ^ m2)]
        for receiver, mask in enumerate((m3, m3 ^ m4, m4, 0)):
            first = (group(mask) * 8 + narrow) * LMO

            def scan(i, found):
                found = list(found)
                for k in range(PARTNERS):
                    listed = partners[k, first + i]
                    owner = lax.div(listed, LMO)
                    place = listed - owner * LMO
                    holder = lax.div(owner, 8)
                    for q in range(4):
                        hit = holder == senders[q]
                        low, high, summed = found[3 * q : 3 * q + 3]
                        found[3 * q] = jnp.where(hit, jnp.minimum(low, place), low)
                        found[3 * q + 1] = jnp.where(hit, jnp.maximum(high, place), high)
                        found[3 * q + 2] = jnp.where(hit, summed + place, summed)
                return tuple(found)

            found = lax.fori_loop(0, LMO, scan, (jnp.int32(LMO - 1), jnp.int32(0), jnp.int32(0)) * 4)
            for q in range(4):
                low, high, summed = found[3 * q : 3 * q + 3]
                twice = summed - low - high
                for k, chosen in enumerate((twice, low + high - twice)):
                    chosen = jnp.minimum(jnp.maximum(chosen, 0), LMO - 1)
                    table[rot * 32 + receiver * 8 + k * 4 + q] = chosen + (q * LMO if q < 3 else 0)

    first = (wide * 8 + narrow) * LMO

    def split(i, carry):
        for k in range(PARTNERS):
            listed = partners[k, first + i]
            owner = lax.div(listed, LMO)
            source[i * PARTNERS + k] = lax.div(owner, 8)
            slot[i * PARTNERS + k] = listed - owner * LMO
        return carry

    lax.fori_loop(0, LMO, split, 0)

    def place(pair, carry):
        mine, mine_slot = source[pair], slot[pair]

        def same(i, count):
            for k in range(PARTNERS):
                other = i * PARTNERS + k
                count = jnp.where((source[other] == mine) & (slot[other] == mine_slot), count + 1, count)
            return count

        alone = lax.fori_loop(0, LMO, same, jnp.int32(0)) == 1
        table[AT_ONCE + pair] = jnp.where(alone, 1, 0)
        table[AT_RANK + pair] = jnp.where(alone, carry, ONCE)
        sz = lax.div(mine, 4)
        sx = mine - sz * 4
        digit = {}
        for low_mask, high_mask, here, there in ((1, 3, x, sx), (4, 12, z, sz)):
            digit[low_mask] = jnp.where((flip(here, 1) == there) | (flip(here, 2) == there), 1, 0)
            digit[high_mask] = jnp.where((flip(here, 3) == there) | (flip(here, 2) == there), 1, 0)
        for rot in range(ROTS):
            m1, m2, m3, m4 = order(rot)
            block = (digit[m3] + 2 * digit[m4]) * 4 + digit[m1] + 2 * digit[m2]
            table[128 + rot * PAIRS + pair] = block
        return jnp.where(alone, carry + 1, carry)

    lax.fori_loop(0, PAIRS, place, jnp.int32(0))

    def listed_once(rank, carry):
        def find(pair, chosen):
            return jnp.where(table[AT_RANK + pair] == rank, pair, chosen)

        table[AT_LIST + rank] = lax.fori_loop(0, PAIRS, find, jnp.int32(0))
        return carry

    lax.fori_loop(0, ONCE, listed_once, 0)


def kernel(partners, lmo_energy, factors, integrals, pao_energy, tile, *scratch):
    row = list(scratch[0:4])
    last = list(scratch[4:8])
    send3 = list(scratch[8:12])
    send4 = list(scratch[12:16])
    passing = list(scratch[16:20])
    final = [list(scratch[20:24]), list(scratch[24:28])]
    (table, source, slot, own_rows, other_energy, flipped, fitted, energy, early_sum, product,
     local_sem, send_sem, recv_sem) = scratch[28:41]
    reduction = scratch[41:]

    barrier = pltpu.get_barrier_semaphore()
    greeted = [neighbour(mask) for mask in MASKS] + [along_y(0, 1), along_y(1), along_y(3)]
    for device in greeted:
        pl.semaphore_signal(barrier, inc=1, device_id=device, device_id_type=MESH)
    pl.semaphore_wait(barrier, len(greeted))

    def copy(rot, kind, src, dst, mask):
        return pltpu.make_async_remote_copy(
            src_ref=src,
            dst_ref=dst,
            send_sem=send_sem.at[rot, kind],
            recv_sem=recv_sem.at[rot, kind],
            device_id=neighbour(mask),
            device_id_type=MESH,
        )

    copies = []
    for rot in range(ROTS):
        m1, m2, m3, m4 = order(rot)
        own = factors.at[:, pl.ds(rot * PIECE, PIECE), :]
        row_copies = [
            copy(rot, 0, own, row[rot].at[pl.ds(6, 6)], m1),
            copy(rot, 1, own, row[rot].at[pl.ds(12, 6)], m2),
            copy(rot, 2, row[rot].at[pl.ds(6, 6)], last[rot], m2),
        ]
        for k, first, count in ((0, 0, 3), (0, 3, 1), (1, 0, 4)):
            at, kind = pl.ds(first, count), len(row_copies)
            place = [pl.ds(4 * block + first, count) for block in range(4)]
            row_copies += [
                copy(rot, kind, send3[rot].at[k, 1, at], passing[rot].at[k, at], m3),
                copy(rot, kind + 1, send3[rot].at[k, 0, at], final[k][rot].at[place[1]], m3),
                copy(rot, kind + 2, send4[rot].at[k, at], final[k][rot].at[place[2]], m4),
                copy(rot, kind + 3, passing[rot].at[k, at], final[k][rot].at[place[3]], m4),
            ]
        copies.append(row_copies)
    for rot in range(ROTS):
        copies[rot][0].start()
    for rot in range(ROTS):
        copies[rot][1].start()
    local = []
    for rot in range(ROTS):
        own = factors.at[:, pl.ds(rot * PIECE, PIECE), :]
        local.append(pltpu.make_async_copy(own, row[rot].at[pl.ds(0, 6)], local_sem.at[rot]))
        local[rot].start()
    local.append(pltpu.make_async_copy(integrals, fitted, local_sem.at[ROTS]))
    local[ROTS].start()

    fill_table(table, source, slot, partners)

    first = (lax.axis_index("wide") * 8 + lax.axis_index("narrow")) * LMO
    own_rows[...] = jnp.zeros_like(own_rows)
    for i in range(LMO):
        own_rows[i : i + 1, :] = pao_energy[pl.ds(first + i, 1), :] - lmo_energy[first + i]

    def fetch(i, carry):
        for k in range(PARTNERS):
            listed = partners[k, first + i]
            other_energy[i * PARTNERS + k] = pao_energy[pl.ds(listed, 1), :] - lmo_energy[listed]
        return carry

    lax.fori_loop(0, LMO, fetch, 0)
    columns = jnp.transpose(own_rows[...])
    for copying in local:
        copying.wait()
    for i in range(LMO):
        energy[i] = jnp.broadcast_to(columns[:, i : i + 1], (PAO, PAO))
        flipped[:, i * PAO : (i + 1) * PAO] = jnp.transpose(fitted[i])

    for rot in range(ROTS):
        copies[rot][0].wait_recv()
        copies[rot][2].start()
    for rot in range(ROTS):
        copies[rot][1].wait_recv()

    def gather(rot, receiver, k, start, stop):
        held = row[rot] if start < 3 else last[rot]

        def body(q, carry):
            value = held[table[rot * 32 + receiver * 8 + k * 4 + q]]
            if receiver < 2:
                send3[rot][k, receiver, q] = value
            elif receiver == 2:
                send4[rot][k, q] = value
            else:
                final[k][rot][q] = value
            return carry

        lax.fori_loop(start, stop, body, 0)

    for receiver, kind in ((1, 3), (0, 4), (2, 5)):
        for rot in range(ROTS):
            gather(rot, receiver, 0, 0, 3)
            copies[rot][kind].start()
    for rot in range(ROTS):
        copies[rot][2].wait_recv()
        gather(rot, 1, 0, 3, 4)
        copies[rot][7].start()
    for rot in range(ROTS):
        for receiver, kind in ((0, 8), (2, 9)):
            gather(rot, receiver, 0, 3, 4)
            copies[rot][kind].start()
    for rot in range(ROTS):
        for receiver in (1, 0, 2):
            gather(rot, receiver, 1, 0, 3)
            gather(rot, receiver, 1, 3, 4)
    for kind in (3, 7):
        for rot in range(ROTS):
            copies[rot][kind].wait_recv()
            copies[rot][kind + 3].start()
    for kind in (11, 12, 13):
        for rot in range(ROTS):
            copies[rot][kind].start()
    for rot in range(ROTS):
        for k in range(2):
            gather(rot, 3, k, 0, 3)
            gather(rot, 3, k, 3, 4)
    product[ONCE] = jnp.zeros((PAO, AUX), jnp.float32)
    for rot in range(ROTS):
        for kind in (4, 5, 6, 8, 9, 10):
            copies[rot][kind].wait_recv()

    def one(i, carry):
        mine = jnp.concatenate([row[rot][i] for rot in range(ROTS)], axis=0)
        others = jnp.concatenate(
            [
                final[0][rot][table[128 + rot * PAIRS + i * PARTNERS + k]]
                for k in range(PARTNERS)
                for rot in range(ROTS)
            ],
            axis=0,
        )
        integral = lax.dot_general(
            mine, others, (((1,), (1,)), ((), ())), preferred_element_type=jnp.float32
        )
        parts = []
        for k in range(PARTNERS):
            pair = i * PARTNERS + k
            keep = jnp.where(table[AT_ONCE + pair] == 1, 0.0, 1.0)
            parts.append(
                integral[:, k * PAO : (k + 1) * PAO] / (energy[i] + other_energy[pair]) * keep
            )
        amplitude = jnp.concatenate(parts, axis=1).astype(jnp.bfloat16)
        early_sum[i] = jnp.dot(amplitude, others, preferred_element_type=jnp.float32)
        return carry

    lax.fori_loop(0, LMO // 2, one, 0)
    for rot in range(ROTS):
        copies[rot][11].wait_recv()
        copies[rot][14].start()
    lax.fori_loop(LMO // 2, LMO, one, 0)
    for rot in range(ROTS):
        for kind in (12, 13, 14):
            copies[rot][kind].wait_recv()

    def remaining(step, carry):
        for part in range(4):
            rank = step * 4 + part
            pair = table[AT_LIST + rank]
            i = lax.div(pair, PARTNERS)
            mine = jnp.concatenate([row[rot][i] for rot in range(ROTS)], axis=0)
            other = jnp.concatenate(
                [final[1][rot][table[128 + rot * PAIRS + pair]] for rot in range(ROTS)], axis=0
            )
            integral = lax.dot_general(
                mine, other, (((1,), (1,)), ((), ())), preferred_element_type=jnp.float32
            )
            amplitude = (integral / (energy[i] + other_energy[pair])).astype(jnp.bfloat16)
            product[rank] = jnp.dot(amplitude, other, preferred_element_type=jnp.float32)
        return carry

    lax.fori_loop(0, ONCE // 4, remaining, 0)

    def combine(i, carry):
        gathered = early_sum[i]
        for k in range(PARTNERS):
            gathered = gathered + product[table[AT_RANK + i * PARTNERS + k]]
        fitted[i] = gathered.astype(jnp.bfloat16)
        return carry

    lax.fori_loop(0, LMO, combine, 0)

    reduce_total(tile, flipped, fitted, *reduction)

    for rot in range(ROTS):
        for kind in range(15):
            copies[rot][kind].wait_send()


def local(factors, integrals, pao_energy, lmo_energy, partners):
    vmem = pl.BlockSpec(memory_space=pltpu.VMEM)
    smem = pl.BlockSpec(memory_space=pltpu.SMEM)
    anywhere = pl.BlockSpec(memory_space=pl.ANY)
    piece = (PIECE, AUX)
    scratch = []
    for shape in ((18,), (6,), (2, 2, 4), (2, 4), (2, 4), (16,), (16,)):
        scratch += [pltpu.VMEM(shape + piece, jnp.bfloat16) for _ in range(ROTS)]
    scratch += [
        pltpu.SMEM((AT_LIST + ONCE,), jnp.int32),
        pltpu.SMEM((PAIRS,), jnp.int32),
        pltpu.SMEM((PAIRS,), jnp.int32),
        pltpu.VMEM((8, PAO), jnp.float32),
        pltpu.VMEM((PAIRS, 1, PAO), jnp.float32),
        pltpu.VMEM((AUX, LMO * PAO), jnp.bfloat16),
        pltpu.VMEM((LMO, PAO, AUX), jnp.bfloat16),
        pltpu.VMEM((LMO, PAO, PAO), jnp.float32),
        pltpu.VMEM((LMO, PAO, AUX), jnp.float32),
        pltpu.VMEM((ONCE + 1, PAO, AUX), jnp.float32),
        pltpu.SemaphoreType.DMA((ROTS + 1,)),
        pltpu.SemaphoreType.DMA((ROTS, 15)),
        pltpu.SemaphoreType.DMA((ROTS, 15)),
        pltpu.VMEM((AUX, AUX), jnp.float32),
        pltpu.VMEM((4, ROWS, AUX), jnp.float32),
        pltpu.VMEM((4, ROWS, AUX), jnp.float32),
        pltpu.VMEM((2, CHUNKS, 2, ROWS, 128), jnp.bfloat16),
        pltpu.VMEM((2, CHUNKS, 2, ROWS, 128), jnp.bfloat16),
        pltpu.VMEM((2, CHUNKS, ROWS, 128), jnp.bfloat16),
        pltpu.VMEM((2, CHUNKS, ROWS, 128), jnp.bfloat16),
        pltpu.VMEM((128, AUX), jnp.float32),
        pltpu.VMEM((AUX, 128), jnp.float32),
        pltpu.VMEM((AUX, 128), jnp.bfloat16),
        pltpu.VMEM((15, HEIGHT, 128), jnp.bfloat16),
        pltpu.SemaphoreType.DMA((2, 4)),
        pltpu.SemaphoreType.DMA((4, 2, CHUNKS)),
        pltpu.SemaphoreType.DMA((2, 15)),
    ]
    return pl.pallas_call(
        kernel,
        out_shape=jax.ShapeDtypeStruct((HEIGHT, ROWS), jnp.float32),
        in_specs=[smem, smem, anywhere, anywhere, vmem],
        out_specs=vmem,
        scratch_shapes=scratch,
        compiler_params=pltpu.CompilerParams(
            collective_id=0, has_side_effects=True, vmem_limit_bytes=60 * 2**20
        ),
    )(partners.T, lmo_energy, factors, integrals, pao_energy)


def solution(mesh):
    in_specs = (P(("wide", "narrow"), None, None), P(("wide", "narrow"), None, None), P(), P(), P())
    out_specs = P("wide", "narrow")
    return jax.shard_map(local, mesh=mesh, in_specs=in_specs, out_specs=out_specs, check_vma=False)
```

```python
import jax
import jax.numpy as jnp
from jax import lax
from jax.experimental import pallas as pl
from jax.experimental.pallas import tpu as pltpu
from jax.sharding import PartitionSpec as P

MESH = pl.DeviceIdType.MESH
LMO = 6
PARTNERS = 4
PAIRS = LMO * PARTNERS
PAO = 256
AUX = 768
ROWS = AUX // 8
HEIGHT = AUX // 16
CHUNKS = AUX // 2 // 128
ROTS = 4
PIECE = PAO // ROTS
ONCE = 8

AT_ONCE = 128 + ROTS * PAIRS
AT_RANK = AT_ONCE + PAIRS
AT_LIST = AT_RANK + PAIRS

MASKS = (1, 4, 3, 12)


def order(rot):
    return [MASKS[(rot + step) % 4] for step in range(4)]


def flip(position, mask):
    if mask == 0:
        return position
    if mask == 3:
        return 3 - position
    if mask == 2:
        return lax.rem(position + 2, 4)
    return position + 1 - 2 * lax.rem(position, 2)


def neighbour(mask):
    wide = lax.axis_index("wide")
    z, x = wide // 4, lax.rem(wide, 4)
    return (flip(z, mask // 4) * 4 + flip(x, mask % 4), lax.axis_index("narrow"))


def along_y(mask, core=0):
    narrow = lax.axis_index("narrow")
    y, c = narrow // 2, lax.rem(narrow, 2)
    return (lax.axis_index("wide"), flip(y, mask) * 2 + flip(c, core))


def reduce_total(
    tile, flipped, fitted, total, core_in, summed, first_out, first_in, second_out, second_in, block, turned, outgoing, tiles_in,
    core_sem, y_sem, wide_sem,
):
    narrow, wide = lax.axis_index("narrow"), lax.axis_index("wide")
    y, core = narrow // 2, lax.rem(narrow, 2)

    def send(src, dst, sems, device):
        return pltpu.make_async_remote_copy(
            src_ref=src, dst_ref=dst, send_sem=sems[0], recv_sem=sems[1],
            device_id=device, device_id_type=MESH,
        )

    def multiply(i, j):
        rows, columns = slice(i * 256, i * 256 + 256), slice(j * 256, j * 256 + 256)
        total[j, rows] = jnp.dot(
            flipped[rows, :],
            fitted[:, :, columns].reshape(LMO * PAO, 256),
            preferred_element_type=jnp.float32,
        )

    def symmetrise(i, j):
        at_i, at_j = slice(i * 256, i * 256 + 256), slice(j * 256, j * 256 + 256)
        half = 0.5 * (total[j, at_i] + jnp.transpose(total[i, at_j]))
        total[j, at_i] = half
        if i != j:
            total[i, at_j] = jnp.transpose(half)

    def band(place, c):
        return pl.ds(pl.multiple_of((place * 2 + c) * ROWS, ROWS), ROWS)

    steps = []
    for i in range(CHUNKS):
        for j in range(i, CHUNKS):
            multiply(i, j)
            if i != j:
                multiply(j, i)
        for j in range(i, CHUNKS):
            symmetrise(i, j)
        for place in range(4):
            steps.append(
                send(total.at[i, band(place, 1 - core)], core_in.at[i, place],
                     (core_sem.at[0, i, place], core_sem.at[1, i, place]), along_y(0, 1))
            )
            steps[-1].start()

    plan = ((1, 3, (1, 2)), (3, 1, (3, 2)))
    firsts, seconds = {}, {}
    chunks = [(h, chunk) for chunk in range(CHUNKS) for h in range(2)]

    def columns(h, chunk):
        start = chunk * 256 + h * 128
        return slice(start, start + 128)

    for h, chunk in chunks:
        near, far, sent = plan[h]
        if h == 0:
            for step in steps[4 * chunk : 4 * chunk + 4]:
                step.wait_recv()
            at = pl.ds(chunk * 256, 256)
            for place in range(4):
                summed[place, :, at] = total[chunk, band(place, core)] + core_in[chunk, place]
        for place, u in enumerate(sent):
            first_out[h, chunk, place] = summed[flip(y, u), :, columns(h, chunk)].astype(first_out.dtype)
        firsts[h, chunk] = send(
            first_out.at[h, chunk], first_in.at[h, chunk],
            (y_sem.at[0, h, chunk], y_sem.at[1, h, chunk]), along_y(near),
        )
        firsts[h, chunk].start()
    block[pl.ds(ROWS, 128 - ROWS), :] = jnp.zeros((128 - ROWS, AUX), jnp.float32)
    for h, chunk in chunks:
        near, far, sent = plan[h]
        firsts[h, chunk].wait_recv()
        passed = summed[flip(y, far), :, columns(h, chunk)] + first_in[h, chunk, 1].astype(jnp.float32)
        second_out[h, chunk] = passed.astype(second_out.dtype)
        seconds[h, chunk] = send(
            second_out.at[h, chunk], second_in.at[h, chunk],
            (y_sem.at[2, h, chunk], y_sem.at[3, h, chunk]), along_y(far),
        )
        seconds[h, chunk].start()
    for h, chunk in chunks:
        at = columns(h, chunk)
        kept = summed[y, :, at] + first_in[h, chunk, 0].astype(jnp.float32)
        seconds[h, chunk].wait_recv()
        block[pl.ds(0, ROWS), at] = kept + second_in[h, chunk].astype(jnp.float32)
        turned[at, :] = jnp.transpose(block[:, at])
        outgoing[at, :] = turned[at, :].astype(outgoing.dtype)

    def rows(t):
        peer = flip(wide // 4, t // 4) * 4 + flip(lax.rem(wide, 4), t % 4)
        return pl.ds(pl.multiple_of(peer * HEIGHT, HEIGHT), HEIGHT)

    spread = []
    for t in range(1, 16):
        spread.append(
            send(outgoing.at[rows(t)], tiles_in.at[t - 1],
                 (wide_sem.at[0, t - 1], wide_sem.at[1, t - 1]), neighbour(t))
        )
        spread[-1].start()
    result = turned[rows(0), :]
    for t in range(1, 16):
        spread[t - 1].wait_recv()
        result = result + tiles_in[t - 1].astype(jnp.float32)
    tile[...] = result[:, :ROWS]

    for step in steps + list(firsts.values()) + list(seconds.values()) + spread:
        step.wait_send()


def fill_table(table, source, slot, partners):
    wide, narrow = lax.axis_index("wide"), lax.axis_index("narrow")
    z, x = wide // 4, lax.rem(wide, 4)

    def group(mask):
        return flip(z, mask // 4) * 4 + flip(x, mask % 4)

    for rot in range(ROTS):
        m1, m2, m3, m4 = order(rot)
        senders = [group(mask) for mask in (0, m1, m2, m1 ^ m2)]
        for receiver, mask in enumerate((m3, m3 ^ m4, m4, 0)):
            first = (group(mask) * 8 + narrow) * LMO

            def scan(i, found):
                found = list(found)
                for k in range(PARTNERS):
                    listed = partners[k, first + i]
                    owner = lax.div(listed, LMO)
                    place = listed - owner * LMO
                    holder = lax.div(owner, 8)
                    for q in range(4):
                        hit = holder == senders[q]
                        low, high, summed = found[3 * q : 3 * q + 3]
                        found[3 * q] = jnp.where(hit, jnp.minimum(low, place), low)
                        found[3 * q + 1] = jnp.where(hit, jnp.maximum(high, place), high)
                        found[3 * q + 2] = jnp.where(hit, summed + place, summed)
                return tuple(found)

            found = lax.fori_loop(0, LMO, scan, (jnp.int32(LMO - 1), jnp.int32(0), jnp.int32(0)) * 4)
            for q in range(4):
                low, high, summed = found[3 * q : 3 * q + 3]
                twice = summed - low - high
                for k, chosen in enumerate((twice, low + high - twice)):
                    chosen = jnp.minimum(jnp.maximum(chosen, 0), LMO - 1)
                    table[rot * 32 + receiver * 8 + k * 4 + q] = chosen + (q * LMO if q < 3 else 0)

    first = (wide * 8 + narrow) * LMO

    def split(i, carry):
        for k in range(PARTNERS):
            listed = partners[k, first + i]
            owner = lax.div(listed, LMO)
            source[i * PARTNERS + k] = lax.div(owner, 8)
            slot[i * PARTNERS + k] = listed - owner * LMO
        return carry

    lax.fori_loop(0, LMO, split, 0)

    def place(pair, carry):
        mine, mine_slot = source[pair], slot[pair]

        def same(i, count):
            for k in range(PARTNERS):
                other = i * PARTNERS + k
                count = jnp.where((source[other] == mine) & (slot[other] == mine_slot), count + 1, count)
            return count

        alone = lax.fori_loop(0, LMO, same, jnp.int32(0)) == 1
        table[AT_ONCE + pair] = jnp.where(alone, 1, 0)
        table[AT_RANK + pair] = jnp.where(alone, carry, ONCE)
        sz = lax.div(mine, 4)
        sx = mine - sz * 4
        digit = {}
        for low_mask, high_mask, here, there in ((1, 3, x, sx), (4, 12, z, sz)):
            digit[low_mask] = jnp.where((flip(here, 1) == there) | (flip(here, 2) == there), 1, 0)
            digit[high_mask] = jnp.where((flip(here, 3) == there) | (flip(here, 2) == there), 1, 0)
        for rot in range(ROTS):
            m1, m2, m3, m4 = order(rot)
            block = (digit[m3] + 2 * digit[m4]) * 4 + digit[m1] + 2 * digit[m2]
            table[128 + rot * PAIRS + pair] = block
        return jnp.where(alone, carry + 1, carry)

    lax.fori_loop(0, PAIRS, place, jnp.int32(0))

    def listed_once(rank, carry):
        def find(pair, chosen):
            return jnp.where(table[AT_RANK + pair] == rank, pair, chosen)

        table[AT_LIST + rank] = lax.fori_loop(0, PAIRS, find, jnp.int32(0))
        return carry

    lax.fori_loop(0, ONCE, listed_once, 0)


def kernel(partners, lmo_energy, factors, integrals, pao_energy, tile, *scratch):
    row = list(scratch[0:4])
    last = list(scratch[4:8])
    send3 = list(scratch[8:12])
    send4 = list(scratch[12:16])
    passing = list(scratch[16:20])
    final = [list(scratch[20:24]), list(scratch[24:28])]
    (table, source, slot, own_rows, other_energy, flipped, fitted, energy, early_sum, product,
     local_sem, send_sem, recv_sem) = scratch[28:41]
    reduction = scratch[41:]

    barrier = pltpu.get_barrier_semaphore()
    greeted = [neighbour(mask) for mask in MASKS] + [along_y(0, 1), along_y(1), along_y(3)]
    for device in greeted:
        pl.semaphore_signal(barrier, inc=1, device_id=device, device_id_type=MESH)
    pl.semaphore_wait(barrier, len(greeted))

    def copy(rot, kind, src, dst, mask):
        return pltpu.make_async_remote_copy(
            src_ref=src,
            dst_ref=dst,
            send_sem=send_sem.at[rot, kind],
            recv_sem=recv_sem.at[rot, kind],
            device_id=neighbour(mask),
            device_id_type=MESH,
        )

    copies = []
    for rot in range(ROTS):
        m1, m2, m3, m4 = order(rot)
        own = factors.at[:, pl.ds(rot * PIECE, PIECE), :]
        row_copies = [
            copy(rot, 0, own, row[rot].at[pl.ds(6, 6)], m1),
            copy(rot, 1, own, row[rot].at[pl.ds(12, 6)], m2),
            copy(rot, 2, row[rot].at[pl.ds(6, 6)], last[rot], m2),
        ]
        for k, first, count in ((0, 0, 3), (0, 3, 1), (1, 0, 4)):
            at, kind = pl.ds(first, count), len(row_copies)
            place = [pl.ds(4 * block + first, count) for block in range(4)]
            row_copies += [
                copy(rot, kind, send3[rot].at[k, 1, at], passing[rot].at[k, at], m3),
                copy(rot, kind + 1, send3[rot].at[k, 0, at], final[k][rot].at[place[1]], m3),
                copy(rot, kind + 2, send4[rot].at[k, at], final[k][rot].at[place[2]], m4),
                copy(rot, kind + 3, passing[rot].at[k, at], final[k][rot].at[place[3]], m4),
            ]
        copies.append(row_copies)
    for rot in range(ROTS):
        copies[rot][0].start()
    for rot in range(ROTS):
        copies[rot][1].start()
    local = []
    for rot in range(ROTS):
        own = factors.at[:, pl.ds(rot * PIECE, PIECE), :]
        local.append(pltpu.make_async_copy(own, row[rot].at[pl.ds(0, 6)], local_sem.at[rot]))
        local[rot].start()
    local.append(pltpu.make_async_copy(integrals, fitted, local_sem.at[ROTS]))
    local[ROTS].start()

    fill_table(table, source, slot, partners)

    first = (lax.axis_index("wide") * 8 + lax.axis_index("narrow")) * LMO
    own_rows[...] = jnp.zeros_like(own_rows)
    for i in range(LMO):
        own_rows[i : i + 1, :] = pao_energy[pl.ds(first + i, 1), :] - lmo_energy[first + i]

    def fetch(i, carry):
        for k in range(PARTNERS):
            listed = partners[k, first + i]
            other_energy[i * PARTNERS + k] = pao_energy[pl.ds(listed, 1), :] - lmo_energy[listed]
        return carry

    lax.fori_loop(0, LMO, fetch, 0)
    columns = jnp.transpose(own_rows[...])
    for copying in local:
        copying.wait()
    for i in range(LMO):
        energy[i] = jnp.broadcast_to(columns[:, i : i + 1], (PAO, PAO))
        flipped[:, i * PAO : (i + 1) * PAO] = jnp.transpose(fitted[i])

    for rot in range(ROTS):
        copies[rot][0].wait_recv()
        copies[rot][2].start()
    for rot in range(ROTS):
        copies[rot][1].wait_recv()

    def gather(rot, receiver, k, start, stop):
        held = row[rot] if start < 3 else last[rot]

        def body(q, carry):
            value = held[table[rot * 32 + receiver * 8 + k * 4 + q]]
            if receiver < 2:
                send3[rot][k, receiver, q] = value
            elif receiver == 2:
                send4[rot][k, q] = value
            else:
                final[k][rot][q] = value
            return carry

        lax.fori_loop(start, stop, body, 0)

    for receiver, kind in ((1, 3), (0, 4), (2, 5)):
        for rot in range(ROTS):
            gather(rot, receiver, 0, 0, 3)
            copies[rot][kind].start()
    for rot in range(ROTS):
        copies[rot][2].wait_recv()
        gather(rot, 1, 0, 3, 4)
        copies[rot][7].start()
    for rot in range(ROTS):
        for receiver, kind in ((0, 8), (2, 9)):
            gather(rot, receiver, 0, 3, 4)
            copies[rot][kind].start()
    for rot in range(ROTS):
        for receiver in (1, 0, 2):
            gather(rot, receiver, 1, 0, 3)
            gather(rot, receiver, 1, 3, 4)
    for kind in (3, 7):
        for rot in range(ROTS):
            copies[rot][kind].wait_recv()
            copies[rot][kind + 3].start()
    for kind in (11, 12, 13):
        for rot in range(ROTS):
            copies[rot][kind].start()
    for rot in range(ROTS):
        for k in range(2):
            gather(rot, 3, k, 0, 3)
            gather(rot, 3, k, 3, 4)
    product[ONCE] = jnp.zeros((PAO, AUX), jnp.float32)
    total = reduction[0]
    blocks = [(rank // 3, pl.ds(rank % 3 * PAO, PAO)) for rank in range(ONCE)]
    for rank in range(ONCE):
        pair = table[AT_LIST + rank]
        total[blocks[rank]] = 1.0 / (energy[lax.div(pair, PARTNERS)] + other_energy[pair])
    for rot in range(ROTS):
        for kind in (4, 5, 6, 8, 9, 10):
            copies[rot][kind].wait_recv()

    def one(i, carry):
        mine = jnp.concatenate([row[rot][i] for rot in range(ROTS)], axis=0)
        others = jnp.concatenate(
            [
                final[0][rot][table[128 + rot * PAIRS + i * PARTNERS + k]]
                for k in range(PARTNERS)
                for rot in range(ROTS)
            ],
            axis=0,
        )
        integral = lax.dot_general(
            mine, others, (((1,), (1,)), ((), ())), preferred_element_type=jnp.float32
        )
        parts = []
        for k in range(PARTNERS):
            pair = i * PARTNERS + k
            keep = jnp.where(table[AT_ONCE + pair] == 1, 0.0, 1.0)
            parts.append(
                integral[:, k * PAO : (k + 1) * PAO] / (energy[i] + other_energy[pair]) * keep
            )
        amplitude = jnp.concatenate(parts, axis=1).astype(jnp.bfloat16)
        early_sum[i] = jnp.dot(amplitude, others, preferred_element_type=jnp.float32)
        return carry

    lax.fori_loop(0, LMO // 2, one, 0)
    for rot in range(ROTS):
        copies[rot][11].wait_recv()
        copies[rot][14].start()
    lax.fori_loop(LMO // 2, LMO, one, 0)
    for rot in range(ROTS):
        for kind in (12, 13, 14):
            copies[rot][kind].wait_recv()

    for rank in range(ONCE):
        pair = table[AT_LIST + rank]
        i = lax.div(pair, PARTNERS)
        mine = jnp.concatenate([row[rot][i] for rot in range(ROTS)], axis=0)
        other = jnp.concatenate(
            [final[1][rot][table[128 + rot * PAIRS + pair]] for rot in range(ROTS)], axis=0
        )
        integral = lax.dot_general(
            mine, other, (((1,), (1,)), ((), ())), preferred_element_type=jnp.float32
        )
        amplitude = (integral * total[blocks[rank]]).astype(jnp.bfloat16)
        product[rank] = jnp.dot(amplitude, other, preferred_element_type=jnp.float32)

    def combine(i, carry):
        gathered = early_sum[i]
        for k in range(PARTNERS):
            gathered = gathered + product[table[AT_RANK + i * PARTNERS + k]]
        fitted[i] = gathered.astype(jnp.bfloat16)
        return carry

    lax.fori_loop(0, LMO, combine, 0)

    reduce_total(tile, flipped, fitted, *reduction)

    for rot in range(ROTS):
        for kind in range(15):
            copies[rot][kind].wait_send()


def local(factors, integrals, pao_energy, lmo_energy, partners):
    vmem = pl.BlockSpec(memory_space=pltpu.VMEM)
    smem = pl.BlockSpec(memory_space=pltpu.SMEM)
    anywhere = pl.BlockSpec(memory_space=pl.ANY)
    piece = (PIECE, AUX)
    scratch = []
    for shape in ((18,), (6,), (2, 2, 4), (2, 4), (2, 4), (16,), (16,)):
        scratch += [pltpu.VMEM(shape + piece, jnp.bfloat16) for _ in range(ROTS)]
    scratch += [
        pltpu.SMEM((AT_LIST + ONCE,), jnp.int32),
        pltpu.SMEM((PAIRS,), jnp.int32),
        pltpu.SMEM((PAIRS,), jnp.int32),
        pltpu.VMEM((8, PAO), jnp.float32),
        pltpu.VMEM((PAIRS, 1, PAO), jnp.float32),
        pltpu.VMEM((AUX, LMO * PAO), jnp.bfloat16),
        pltpu.VMEM((LMO, PAO, AUX), jnp.bfloat16),
        pltpu.VMEM((LMO, PAO, PAO), jnp.float32),
        pltpu.VMEM((LMO, PAO, AUX), jnp.float32),
        pltpu.VMEM((ONCE + 1, PAO, AUX), jnp.float32),
        pltpu.SemaphoreType.DMA((ROTS + 1,)),
        pltpu.SemaphoreType.DMA((ROTS, 15)),
        pltpu.SemaphoreType.DMA((ROTS, 15)),
        pltpu.VMEM((CHUNKS, AUX, 256), jnp.float32),
        pltpu.VMEM((CHUNKS, 4, ROWS, 256), jnp.float32),
        pltpu.VMEM((4, ROWS, AUX), jnp.float32),
        pltpu.VMEM((2, CHUNKS, 2, ROWS, 128), jnp.bfloat16),
        pltpu.VMEM((2, CHUNKS, 2, ROWS, 128), jnp.bfloat16),
        pltpu.VMEM((2, CHUNKS, ROWS, 128), jnp.bfloat16),
        pltpu.VMEM((2, CHUNKS, ROWS, 128), jnp.bfloat16),
        pltpu.VMEM((128, AUX), jnp.float32),
        pltpu.VMEM((AUX, 128), jnp.float32),
        pltpu.VMEM((AUX, 128), jnp.bfloat16),
        pltpu.VMEM((15, HEIGHT, 128), jnp.bfloat16),
        pltpu.SemaphoreType.DMA((2, CHUNKS, 4)),
        pltpu.SemaphoreType.DMA((4, 2, CHUNKS)),
        pltpu.SemaphoreType.DMA((2, 15)),
    ]
    return pl.pallas_call(
        kernel,
        out_shape=jax.ShapeDtypeStruct((HEIGHT, ROWS), jnp.float32),
        in_specs=[smem, smem, anywhere, anywhere, vmem],
        out_specs=vmem,
        scratch_shapes=scratch,
        compiler_params=pltpu.CompilerParams(
            collective_id=0, has_side_effects=True, vmem_limit_bytes=60 * 2**20
        ),
    )(partners.T, lmo_energy, factors, integrals, pao_energy)


def solution(mesh):
    in_specs = (P(("wide", "narrow"), None, None), P(("wide", "narrow"), None, None), P(), P(), P())
    out_specs = P("wide", "narrow")
    return jax.shard_map(local, mesh=mesh, in_specs=in_specs, out_specs=out_specs, check_vma=False)
```

```python
import jax
import jax.numpy as jnp
from jax import lax
from jax.experimental import pallas as pl
from jax.experimental.pallas import tpu as pltpu
from jax.sharding import PartitionSpec as P

MESH = pl.DeviceIdType.MESH
LMO = 6
PARTNERS = 4
PAIRS = LMO * PARTNERS
PAO = 256
AUX = 768
ROWS = AUX // 8
HEIGHT = AUX // 16
CHUNKS = AUX // 2 // 128
ROTS = 4
PIECE = PAO // ROTS
ONCE = 8

AT_ONCE = 128 + ROTS * PAIRS
AT_RANK = AT_ONCE + PAIRS
AT_LIST = AT_RANK + PAIRS

MASKS = (1, 4, 3, 12)


def order(rot):
    return [MASKS[(rot + step) % 4] for step in range(4)]


def flip(position, mask):
    if mask == 0:
        return position
    if mask == 3:
        return 3 - position
    if mask == 2:
        return lax.rem(position + 2, 4)
    return position + 1 - 2 * lax.rem(position, 2)


def neighbour(mask):
    wide = lax.axis_index("wide")
    z, x = wide // 4, lax.rem(wide, 4)
    return (flip(z, mask // 4) * 4 + flip(x, mask % 4), lax.axis_index("narrow"))


def along_y(mask, core=0):
    narrow = lax.axis_index("narrow")
    y, c = narrow // 2, lax.rem(narrow, 2)
    return (lax.axis_index("wide"), flip(y, mask) * 2 + flip(c, core))


def reduce_total(
    tile, flipped, fitted, total, core_in, summed, first_out, first_in, second_out, second_in, block, turned, outgoing, tiles_in,
    core_sem, y_sem, wide_sem,
):
    narrow, wide = lax.axis_index("narrow"), lax.axis_index("wide")
    y, core = narrow // 2, lax.rem(narrow, 2)

    def send(src, dst, sems, device):
        return pltpu.make_async_remote_copy(
            src_ref=src, dst_ref=dst, send_sem=sems[0], recv_sem=sems[1],
            device_id=device, device_id_type=MESH,
        )

    def multiply(i, j):
        rows, columns = slice(i * 256, i * 256 + 256), slice(j * 256, j * 256 + 256)
        total[j, rows] = jnp.dot(
            flipped[rows, :],
            fitted[:, :, columns].reshape(LMO * PAO, 256),
            preferred_element_type=jnp.float32,
        )

    def symmetrise(i, j):
        at_i, at_j = slice(i * 256, i * 256 + 256), slice(j * 256, j * 256 + 256)
        half = 0.5 * (total[j, at_i] + jnp.transpose(total[i, at_j]))
        total[j, at_i] = half
        if i != j:
            total[i, at_j] = jnp.transpose(half)

    def band(place, c):
        return pl.ds(pl.multiple_of((place * 2 + c) * ROWS, ROWS), ROWS)

    steps = []
    for i in range(CHUNKS):
        for j in range(i, CHUNKS):
            multiply(i, j)
            if i != j:
                multiply(j, i)
        for j in range(i, CHUNKS):
            symmetrise(i, j)
        for place in range(4):
            steps.append(
                send(total.at[i, band(place, 1 - core)], core_in.at[i, place],
                     (core_sem.at[0, i, place], core_sem.at[1, i, place]), along_y(0, 1))
            )
            steps[-1].start()

    plan = ((1, 3, (1, 2)), (3, 1, (3, 2)))
    firsts, seconds = {}, {}
    chunks = [(h, chunk) for chunk in range(CHUNKS) for h in range(2)]

    def columns(h, chunk):
        start = chunk * 256 + h * 128
        return slice(start, start + 128)

    for h, chunk in chunks:
        near, far, sent = plan[h]
        if h == 0:
            for step in steps[4 * chunk : 4 * chunk + 4]:
                step.wait_recv()
            at = pl.ds(chunk * 256, 256)
            for place in range(4):
                summed[place, :, at] = total[chunk, band(place, core)] + core_in[chunk, place]
        for place, u in enumerate(sent):
            first_out[h, chunk, place] = summed[flip(y, u), :, columns(h, chunk)].astype(first_out.dtype)
        firsts[h, chunk] = send(
            first_out.at[h, chunk], first_in.at[h, chunk],
            (y_sem.at[0, h, chunk], y_sem.at[1, h, chunk]), along_y(near),
        )
        firsts[h, chunk].start()
    block[pl.ds(ROWS, 128 - ROWS), :] = jnp.zeros((128 - ROWS, AUX), jnp.float32)
    for h, chunk in chunks:
        near, far, sent = plan[h]
        firsts[h, chunk].wait_recv()
        passed = summed[flip(y, far), :, columns(h, chunk)] + first_in[h, chunk, 1].astype(jnp.float32)
        second_out[h, chunk] = passed.astype(second_out.dtype)
        seconds[h, chunk] = send(
            second_out.at[h, chunk], second_in.at[h, chunk],
            (y_sem.at[2, h, chunk], y_sem.at[3, h, chunk]), along_y(far),
        )
        seconds[h, chunk].start()
    def row_of(t):
        peer = flip(wide // 4, t // 4) * 4 + flip(lax.rem(wide, 4), t % 4)
        return peer * HEIGHT

    def rows(t):
        return pl.ds(pl.multiple_of(row_of(t), HEIGHT), HEIGHT)

    spread = []
    for t in range(1, 16):
        spread.append(
            send(outgoing.at[rows(t)], tiles_in.at[t - 1],
                 (wide_sem.at[0, t - 1], wide_sem.at[1, t - 1]), neighbour(t))
        )

    def send_tiles(chunk):
        for t in range(1, 16):
            end = row_of(t) + HEIGHT

            @pl.when((end > chunk * 256) & (end <= chunk * 256 + 256))
            def _():
                spread[t - 1].start()

    for h, chunk in chunks:
        at = columns(h, chunk)
        kept = summed[y, :, at] + first_in[h, chunk, 0].astype(jnp.float32)
        seconds[h, chunk].wait_recv()
        block[pl.ds(0, ROWS), at] = kept + second_in[h, chunk].astype(jnp.float32)
        turned[at, :] = jnp.transpose(block[:, at])
        outgoing[at, :] = turned[at, :].astype(outgoing.dtype)
        if h == 1:
            send_tiles(chunk)

    result = turned[rows(0), :]
    for t in range(1, 16):
        spread[t - 1].wait_recv()
        result = result + tiles_in[t - 1].astype(jnp.float32)
    tile[...] = result[:, :ROWS]

    for step in steps + list(firsts.values()) + list(seconds.values()) + spread:
        step.wait_send()


def fill_table(table, source, slot, partners):
    wide, narrow = lax.axis_index("wide"), lax.axis_index("narrow")
    z, x = wide // 4, lax.rem(wide, 4)

    def group(mask):
        return flip(z, mask // 4) * 4 + flip(x, mask % 4)

    for rot in range(ROTS):
        m1, m2, m3, m4 = order(rot)
        senders = [group(mask) for mask in (0, m1, m2, m1 ^ m2)]
        for receiver, mask in enumerate((m3, m3 ^ m4, m4, 0)):
            first = (group(mask) * 8 + narrow) * LMO

            def scan(i, found):
                found = list(found)
                for k in range(PARTNERS):
                    listed = partners[k, first + i]
                    owner = lax.div(listed, LMO)
                    place = listed - owner * LMO
                    holder = lax.div(owner, 8)
                    for q in range(4):
                        hit = holder == senders[q]
                        low, high, summed = found[3 * q : 3 * q + 3]
                        found[3 * q] = jnp.where(hit, jnp.minimum(low, place), low)
                        found[3 * q + 1] = jnp.where(hit, jnp.maximum(high, place), high)
                        found[3 * q + 2] = jnp.where(hit, summed + place, summed)
                return tuple(found)

            found = lax.fori_loop(0, LMO, scan, (jnp.int32(LMO - 1), jnp.int32(0), jnp.int32(0)) * 4)
            for q in range(4):
                low, high, summed = found[3 * q : 3 * q + 3]
                twice = summed - low - high
                for k, chosen in enumerate((twice, low + high - twice)):
                    chosen = jnp.minimum(jnp.maximum(chosen, 0), LMO - 1)
                    table[rot * 32 + receiver * 8 + k * 4 + q] = chosen + (q * LMO if q < 3 else 0)

    first = (wide * 8 + narrow) * LMO

    def split(i, carry):
        for k in range(PARTNERS):
            listed = partners[k, first + i]
            owner = lax.div(listed, LMO)
            source[i * PARTNERS + k] = lax.div(owner, 8)
            slot[i * PARTNERS + k] = listed - owner * LMO
        return carry

    lax.fori_loop(0, LMO, split, 0)

    def place(pair, carry):
        mine, mine_slot = source[pair], slot[pair]

        def same(i, count):
            for k in range(PARTNERS):
                other = i * PARTNERS + k
                count = jnp.where((source[other] == mine) & (slot[other] == mine_slot), count + 1, count)
            return count

        alone = lax.fori_loop(0, LMO, same, jnp.int32(0)) == 1
        table[AT_ONCE + pair] = jnp.where(alone, 1, 0)
        table[AT_RANK + pair] = jnp.where(alone, carry, ONCE)
        sz = lax.div(mine, 4)
        sx = mine - sz * 4
        digit = {}
        for low_mask, high_mask, here, there in ((1, 3, x, sx), (4, 12, z, sz)):
            digit[low_mask] = jnp.where((flip(here, 1) == there) | (flip(here, 2) == there), 1, 0)
            digit[high_mask] = jnp.where((flip(here, 3) == there) | (flip(here, 2) == there), 1, 0)
        for rot in range(ROTS):
            m1, m2, m3, m4 = order(rot)
            block = (digit[m3] + 2 * digit[m4]) * 4 + digit[m1] + 2 * digit[m2]
            table[128 + rot * PAIRS + pair] = block
        return jnp.where(alone, carry + 1, carry)

    lax.fori_loop(0, PAIRS, place, jnp.int32(0))

    def listed_once(rank, carry):
        def find(pair, chosen):
            return jnp.where(table[AT_RANK + pair] == rank, pair, chosen)

        table[AT_LIST + rank] = lax.fori_loop(0, PAIRS, find, jnp.int32(0))
        return carry

    lax.fori_loop(0, ONCE, listed_once, 0)


def kernel(partners, lmo_energy, factors, integrals, pao_energy, tile, *scratch):
    row = list(scratch[0:4])
    last = list(scratch[4:8])
    send3 = list(scratch[8:12])
    send4 = list(scratch[12:16])
    passing = list(scratch[16:20])
    final = [list(scratch[20:24]), list(scratch[24:28])]
    (table, source, slot, own_rows, other_energy, flipped, fitted, energy, early_sum, product,
     local_sem, send_sem, recv_sem) = scratch[28:41]
    reduction = scratch[41:]

    barrier = pltpu.get_barrier_semaphore()
    greeted = [neighbour(mask) for mask in MASKS] + [along_y(0, 1), along_y(1), along_y(3)]
    for device in greeted:
        pl.semaphore_signal(barrier, inc=1, device_id=device, device_id_type=MESH)
    pl.semaphore_wait(barrier, len(greeted))

    def copy(rot, kind, src, dst, mask):
        return pltpu.make_async_remote_copy(
            src_ref=src,
            dst_ref=dst,
            send_sem=send_sem.at[rot, kind],
            recv_sem=recv_sem.at[rot, kind],
            device_id=neighbour(mask),
            device_id_type=MESH,
        )

    copies = []
    for rot in range(ROTS):
        m1, m2, m3, m4 = order(rot)
        own = factors.at[:, pl.ds(rot * PIECE, PIECE), :]
        row_copies = [
            copy(rot, 0, own, row[rot].at[pl.ds(6, 6)], m1),
            copy(rot, 1, own, row[rot].at[pl.ds(12, 6)], m2),
            copy(rot, 2, row[rot].at[pl.ds(6, 6)], last[rot], m2),
        ]
        for k, first, count in ((0, 0, 3), (0, 3, 1), (1, 0, 4)):
            at, kind = pl.ds(first, count), len(row_copies)
            place = [pl.ds(4 * block + first, count) for block in range(4)]
            row_copies += [
                copy(rot, kind, send3[rot].at[k, 1, at], passing[rot].at[k, at], m3),
                copy(rot, kind + 1, send3[rot].at[k, 0, at], final[k][rot].at[place[1]], m3),
                copy(rot, kind + 2, send4[rot].at[k, at], final[k][rot].at[place[2]], m4),
                copy(rot, kind + 3, passing[rot].at[k, at], final[k][rot].at[place[3]], m4),
            ]
        copies.append(row_copies)
    for rot in range(ROTS):
        copies[rot][0].start()
    for rot in range(ROTS):
        copies[rot][1].start()
    local = []
    for rot in range(ROTS):
        own = factors.at[:, pl.ds(rot * PIECE, PIECE), :]
        local.append(pltpu.make_async_copy(own, row[rot].at[pl.ds(0, 6)], local_sem.at[rot]))
        local[rot].start()
    local.append(pltpu.make_async_copy(integrals, fitted, local_sem.at[ROTS]))
    local[ROTS].start()

    fill_table(table, source, slot, partners)

    first = (lax.axis_index("wide") * 8 + lax.axis_index("narrow")) * LMO
    own_rows[...] = jnp.zeros_like(own_rows)
    for i in range(LMO):
        own_rows[i : i + 1, :] = pao_energy[pl.ds(first + i, 1), :] - lmo_energy[first + i]

    def fetch(i, carry):
        for k in range(PARTNERS):
            listed = partners[k, first + i]
            other_energy[i * PARTNERS + k] = pao_energy[pl.ds(listed, 1), :] - lmo_energy[listed]
        return carry

    lax.fori_loop(0, LMO, fetch, 0)
    columns = jnp.transpose(own_rows[...])
    for copying in local:
        copying.wait()
    for i in range(LMO):
        energy[i] = jnp.broadcast_to(columns[:, i : i + 1], (PAO, PAO))
        flipped[:, i * PAO : (i + 1) * PAO] = jnp.transpose(fitted[i])

    for rot in range(ROTS):
        copies[rot][0].wait_recv()
        copies[rot][2].start()
    for rot in range(ROTS):
        copies[rot][1].wait_recv()

    def gather(rot, receiver, k, start, stop):
        held = row[rot] if start < 3 else last[rot]

        def body(q, carry):
            value = held[table[rot * 32 + receiver * 8 + k * 4 + q]]
            if receiver < 2:
                send3[rot][k, receiver, q] = value
            elif receiver == 2:
                send4[rot][k, q] = value
            else:
                final[k][rot][q] = value
            return carry

        lax.fori_loop(start, stop, body, 0)

    for receiver, kind in ((1, 3), (0, 4), (2, 5)):
        for rot in range(ROTS):
            gather(rot, receiver, 0, 0, 3)
            copies[rot][kind].start()
    for rot in range(ROTS):
        copies[rot][2].wait_recv()
        gather(rot, 1, 0, 3, 4)
        copies[rot][7].start()
    for rot in range(ROTS):
        for receiver, kind in ((0, 8), (2, 9)):
            gather(rot, receiver, 0, 3, 4)
            copies[rot][kind].start()
    for rot in range(ROTS):
        for receiver in (1, 0, 2):
            gather(rot, receiver, 1, 0, 3)
            gather(rot, receiver, 1, 3, 4)
    for kind in (3, 7):
        for rot in range(ROTS):
            copies[rot][kind].wait_recv()
            copies[rot][kind + 3].start()
    for kind in (11, 12, 13):
        for rot in range(ROTS):
            copies[rot][kind].start()
    for rot in range(ROTS):
        for k in range(2):
            gather(rot, 3, k, 0, 3)
            gather(rot, 3, k, 3, 4)
    product[ONCE] = jnp.zeros((PAO, AUX), jnp.float32)
    total = reduction[0]
    blocks = [(rank // 3, pl.ds(rank % 3 * PAO, PAO)) for rank in range(ONCE)]
    for rank in range(ONCE):
        pair = table[AT_LIST + rank]
        total[blocks[rank]] = 1.0 / (energy[lax.div(pair, PARTNERS)] + other_energy[pair])
    for rot in range(ROTS):
        for kind in (4, 5, 6, 8, 9, 10):
            copies[rot][kind].wait_recv()

    def one(i, carry):
        mine = jnp.concatenate([row[rot][i] for rot in range(ROTS)], axis=0)
        others = jnp.concatenate(
            [
                final[0][rot][table[128 + rot * PAIRS + i * PARTNERS + k]]
                for k in range(PARTNERS)
                for rot in range(ROTS)
            ],
            axis=0,
        )
        integral = lax.dot_general(
            mine, others, (((1,), (1,)), ((), ())), preferred_element_type=jnp.float32
        )
        parts = []
        for k in range(PARTNERS):
            pair = i * PARTNERS + k
            keep = jnp.where(table[AT_ONCE + pair] == 1, 0.0, 1.0)
            parts.append(
                integral[:, k * PAO : (k + 1) * PAO] / (energy[i] + other_energy[pair]) * keep
            )
        amplitude = jnp.concatenate(parts, axis=1).astype(jnp.bfloat16)
        early_sum[i] = jnp.dot(amplitude, others, preferred_element_type=jnp.float32)
        return carry

    lax.fori_loop(0, LMO // 2, one, 0)
    for rot in range(ROTS):
        copies[rot][11].wait_recv()
        copies[rot][14].start()
    lax.fori_loop(LMO // 2, LMO, one, 0)
    for rot in range(ROTS):
        for kind in (12, 13, 14):
            copies[rot][kind].wait_recv()

    for rank in range(ONCE):
        pair = table[AT_LIST + rank]
        i = lax.div(pair, PARTNERS)
        mine = jnp.concatenate([row[rot][i] for rot in range(ROTS)], axis=0)
        other = jnp.concatenate(
            [final[1][rot][table[128 + rot * PAIRS + pair]] for rot in range(ROTS)], axis=0
        )
        integral = lax.dot_general(
            mine, other, (((1,), (1,)), ((), ())), preferred_element_type=jnp.float32
        )
        amplitude = (integral * total[blocks[rank]]).astype(jnp.bfloat16)
        product[rank] = jnp.dot(amplitude, other, preferred_element_type=jnp.float32)

    def combine(i, carry):
        gathered = early_sum[i]
        for k in range(PARTNERS):
            gathered = gathered + product[table[AT_RANK + i * PARTNERS + k]]
        fitted[i] = gathered.astype(jnp.bfloat16)
        return carry

    lax.fori_loop(0, LMO, combine, 0)

    reduce_total(tile, flipped, fitted, *reduction)

    for rot in range(ROTS):
        for kind in range(15):
            copies[rot][kind].wait_send()


def local(factors, integrals, pao_energy, lmo_energy, partners):
    vmem = pl.BlockSpec(memory_space=pltpu.VMEM)
    smem = pl.BlockSpec(memory_space=pltpu.SMEM)
    anywhere = pl.BlockSpec(memory_space=pl.ANY)
    piece = (PIECE, AUX)
    scratch = []
    for shape in ((18,), (6,), (2, 2, 4), (2, 4), (2, 4), (16,), (16,)):
        scratch += [pltpu.VMEM(shape + piece, jnp.bfloat16) for _ in range(ROTS)]
    scratch += [
        pltpu.SMEM((AT_LIST + ONCE,), jnp.int32),
        pltpu.SMEM((PAIRS,), jnp.int32),
        pltpu.SMEM((PAIRS,), jnp.int32),
        pltpu.VMEM((8, PAO), jnp.float32),
        pltpu.VMEM((PAIRS, 1, PAO), jnp.float32),
        pltpu.VMEM((AUX, LMO * PAO), jnp.bfloat16),
        pltpu.VMEM((LMO, PAO, AUX), jnp.bfloat16),
        pltpu.VMEM((LMO, PAO, PAO), jnp.float32),
        pltpu.VMEM((LMO, PAO, AUX), jnp.float32),
        pltpu.VMEM((ONCE + 1, PAO, AUX), jnp.float32),
        pltpu.SemaphoreType.DMA((ROTS + 1,)),
        pltpu.SemaphoreType.DMA((ROTS, 15)),
        pltpu.SemaphoreType.DMA((ROTS, 15)),
        pltpu.VMEM((CHUNKS, AUX, 256), jnp.float32),
        pltpu.VMEM((CHUNKS, 4, ROWS, 256), jnp.float32),
        pltpu.VMEM((4, ROWS, AUX), jnp.float32),
        pltpu.VMEM((2, CHUNKS, 2, ROWS, 128), jnp.bfloat16),
        pltpu.VMEM((2, CHUNKS, 2, ROWS, 128), jnp.bfloat16),
        pltpu.VMEM((2, CHUNKS, ROWS, 128), jnp.bfloat16),
        pltpu.VMEM((2, CHUNKS, ROWS, 128), jnp.bfloat16),
        pltpu.VMEM((128, AUX), jnp.float32),
        pltpu.VMEM((AUX, 128), jnp.float32),
        pltpu.VMEM((AUX, 128), jnp.bfloat16),
        pltpu.VMEM((15, HEIGHT, 128), jnp.bfloat16),
        pltpu.SemaphoreType.DMA((2, CHUNKS, 4)),
        pltpu.SemaphoreType.DMA((4, 2, CHUNKS)),
        pltpu.SemaphoreType.DMA((2, 15)),
    ]
    return pl.pallas_call(
        kernel,
        out_shape=jax.ShapeDtypeStruct((HEIGHT, ROWS), jnp.float32),
        in_specs=[smem, smem, anywhere, anywhere, vmem],
        out_specs=vmem,
        scratch_shapes=scratch,
        compiler_params=pltpu.CompilerParams(
            collective_id=0, has_side_effects=True, vmem_limit_bytes=60 * 2**20
        ),
    )(partners.T, lmo_energy, factors, integrals, pao_energy)


def solution(mesh):
    in_specs = (P(("wide", "narrow"), None, None), P(("wide", "narrow"), None, None), P(), P(), P())
    out_specs = P("wide", "narrow")
    return jax.shard_map(local, mesh=mesh, in_specs=in_specs, out_specs=out_specs, check_vma=False)
```

```python
import jax
import jax.numpy as jnp
from jax import lax
from jax.experimental import pallas as pl
from jax.experimental.pallas import tpu as pltpu
from jax.sharding import PartitionSpec as P

MESH = pl.DeviceIdType.MESH
LMO = 6
LMOS = 768
PARTNERS = 4
PAIRS = LMO * PARTNERS
PAO = 256
AUX = 768
ROWS = AUX // 8
HEIGHT = AUX // 16
CHUNKS = AUX // 2 // 128
ROTS = 4
PIECE = PAO // ROTS
ONCE = 8

AT_ONCE = 128 + ROTS * PAIRS
AT_RANK = AT_ONCE + PAIRS
AT_LIST = AT_RANK + PAIRS

MASKS = (1, 4, 3, 12)


def order(rot):
    return [MASKS[(rot + step) % 4] for step in range(4)]


def flip(position, mask):
    if mask == 0:
        return position
    if mask == 3:
        return 3 - position
    if mask == 2:
        return lax.rem(position + 2, 4)
    return position + 1 - 2 * lax.rem(position, 2)


def neighbour(mask):
    wide = lax.axis_index("wide")
    z, x = wide // 4, lax.rem(wide, 4)
    return (flip(z, mask // 4) * 4 + flip(x, mask % 4), lax.axis_index("narrow"))


def along_y(mask, core=0):
    narrow = lax.axis_index("narrow")
    y, c = narrow // 2, lax.rem(narrow, 2)
    return (lax.axis_index("wide"), flip(y, mask) * 2 + flip(c, core))


def reduce_total(
    tile, flipped, fitted, total, core_in, summed, first_out, first_in, second_out, second_in, block, turned, outgoing, tiles_in,
    core_sem, y_sem, wide_sem,
):
    narrow, wide = lax.axis_index("narrow"), lax.axis_index("wide")
    y, core = narrow // 2, lax.rem(narrow, 2)

    def send(src, dst, sems, device):
        return pltpu.make_async_remote_copy(
            src_ref=src, dst_ref=dst, send_sem=sems[0], recv_sem=sems[1],
            device_id=device, device_id_type=MESH,
        )

    def multiply(i, j):
        rows, columns = slice(i * 256, i * 256 + 256), slice(j * 256, j * 256 + 256)
        total[j, rows] = jnp.dot(
            flipped[rows, :],
            fitted[:, :, columns].reshape(LMO * PAO, 256),
            preferred_element_type=jnp.float32,
        )

    def symmetrise(i, j):
        at_i, at_j = slice(i * 256, i * 256 + 256), slice(j * 256, j * 256 + 256)
        half = 0.5 * (total[j, at_i] + jnp.transpose(total[i, at_j]))
        total[j, at_i] = half
        if i != j:
            total[i, at_j] = jnp.transpose(half)

    def band(place, c):
        return pl.ds(pl.multiple_of((place * 2 + c) * ROWS, ROWS), ROWS)

    steps = []
    for i in range(CHUNKS):
        for j in range(i, CHUNKS):
            multiply(i, j)
            if i != j:
                multiply(j, i)
        for j in range(i, CHUNKS):
            symmetrise(i, j)
        for place in range(4):
            steps.append(
                send(total.at[i, band(place, 1 - core)], core_in.at[i, place],
                     (core_sem.at[0, i, place], core_sem.at[1, i, place]), along_y(0, 1))
            )
            steps[-1].start()

    plan = ((1, 3, (1, 2)), (3, 1, (3, 2)))
    firsts, seconds = {}, {}
    chunks = [(h, chunk) for chunk in range(CHUNKS) for h in range(2)]

    def columns(h, chunk):
        start = chunk * 256 + h * 128
        return slice(start, start + 128)

    for h, chunk in chunks:
        near, far, sent = plan[h]
        if h == 0:
            for step in steps[4 * chunk : 4 * chunk + 4]:
                step.wait_recv()
            at = pl.ds(chunk * 256, 256)
            for place in range(4):
                summed[place, :, at] = total[chunk, band(place, core)] + core_in[chunk, place]
        for place, u in enumerate(sent):
            first_out[h, chunk, place] = summed[flip(y, u), :, columns(h, chunk)].astype(first_out.dtype)
        firsts[h, chunk] = send(
            first_out.at[h, chunk], first_in.at[h, chunk],
            (y_sem.at[0, h, chunk], y_sem.at[1, h, chunk]), along_y(near),
        )
        firsts[h, chunk].start()
    block[pl.ds(ROWS, 128 - ROWS), :] = jnp.zeros((128 - ROWS, AUX), jnp.float32)
    for h, chunk in chunks:
        near, far, sent = plan[h]
        firsts[h, chunk].wait_recv()
        passed = summed[flip(y, far), :, columns(h, chunk)] + first_in[h, chunk, 1].astype(jnp.float32)
        second_out[h, chunk] = passed.astype(second_out.dtype)
        seconds[h, chunk] = send(
            second_out.at[h, chunk], second_in.at[h, chunk],
            (y_sem.at[2, h, chunk], y_sem.at[3, h, chunk]), along_y(far),
        )
        seconds[h, chunk].start()
    def row_of(t):
        peer = flip(wide // 4, t // 4) * 4 + flip(lax.rem(wide, 4), t % 4)
        return peer * HEIGHT

    def rows(t):
        return pl.ds(pl.multiple_of(row_of(t), HEIGHT), HEIGHT)

    spread = []
    for t in range(1, 16):
        spread.append(
            send(outgoing.at[rows(t)], tiles_in.at[t - 1],
                 (wide_sem.at[0, t - 1], wide_sem.at[1, t - 1]), neighbour(t))
        )

    def send_tiles(chunk):
        for t in range(1, 16):
            end = row_of(t) + HEIGHT

            @pl.when((end > chunk * 256) & (end <= chunk * 256 + 256))
            def _():
                spread[t - 1].start()

    for h, chunk in chunks:
        at = columns(h, chunk)
        kept = summed[y, :, at] + first_in[h, chunk, 0].astype(jnp.float32)
        seconds[h, chunk].wait_recv()
        block[pl.ds(0, ROWS), at] = kept + second_in[h, chunk].astype(jnp.float32)
        turned[at, :] = jnp.transpose(block[:, at])
        outgoing[at, :] = turned[at, :].astype(outgoing.dtype)
        if h == 1:
            send_tiles(chunk)

    result = turned[rows(0), :]
    for t in range(1, 16):
        spread[t - 1].wait_recv()
        result = result + tiles_in[t - 1].astype(jnp.float32)
    tile[...] = result[:, :ROWS]

    for step in steps + list(firsts.values()) + list(seconds.values()) + spread:
        step.wait_send()


def fill_table(table, source, slot, partners):
    wide, narrow = lax.axis_index("wide"), lax.axis_index("narrow")
    z, x = wide // 4, lax.rem(wide, 4)

    def group(mask):
        return flip(z, mask // 4) * 4 + flip(x, mask % 4)

    for rot in range(ROTS):
        m1, m2, m3, m4 = order(rot)
        senders = [group(mask) for mask in (0, m1, m2, m1 ^ m2)]
        for receiver, mask in enumerate((m3, m3 ^ m4, m4, 0)):
            first = (group(mask) * 8 + narrow) * LMO

            def scan(i, found):
                found = list(found)
                for k in range(PARTNERS):
                    listed = partners[k, first + i]
                    owner = lax.div(listed, LMO)
                    place = listed - owner * LMO
                    holder = lax.div(owner, 8)
                    for q in range(4):
                        hit = holder == senders[q]
                        low, high, summed = found[3 * q : 3 * q + 3]
                        found[3 * q] = jnp.where(hit, jnp.minimum(low, place), low)
                        found[3 * q + 1] = jnp.where(hit, jnp.maximum(high, place), high)
                        found[3 * q + 2] = jnp.where(hit, summed + place, summed)
                return tuple(found)

            found = lax.fori_loop(0, LMO, scan, (jnp.int32(LMO - 1), jnp.int32(0), jnp.int32(0)) * 4)
            for q in range(4):
                low, high, summed = found[3 * q : 3 * q + 3]
                twice = summed - low - high
                for k, chosen in enumerate((twice, low + high - twice)):
                    chosen = jnp.minimum(jnp.maximum(chosen, 0), LMO - 1)
                    table[rot * 32 + receiver * 8 + k * 4 + q] = chosen + (q * LMO if q < 3 else 0)

    first = (wide * 8 + narrow) * LMO

    def split(i, carry):
        for k in range(PARTNERS):
            listed = partners[k, first + i]
            owner = lax.div(listed, LMO)
            source[i * PARTNERS + k] = lax.div(owner, 8)
            slot[i * PARTNERS + k] = listed - owner * LMO
        return carry

    lax.fori_loop(0, LMO, split, 0)

    def place(pair, carry):
        mine, mine_slot = source[pair], slot[pair]

        def same(i, count):
            for k in range(PARTNERS):
                other = i * PARTNERS + k
                count = jnp.where((source[other] == mine) & (slot[other] == mine_slot), count + 1, count)
            return count

        alone = lax.fori_loop(0, LMO, same, jnp.int32(0)) == 1
        table[AT_ONCE + pair] = jnp.where(alone, 1, 0)
        table[AT_RANK + pair] = jnp.where(alone, carry, ONCE)
        sz = lax.div(mine, 4)
        sx = mine - sz * 4
        digit = {}
        for low_mask, high_mask, here, there in ((1, 3, x, sx), (4, 12, z, sz)):
            digit[low_mask] = jnp.where((flip(here, 1) == there) | (flip(here, 2) == there), 1, 0)
            digit[high_mask] = jnp.where((flip(here, 3) == there) | (flip(here, 2) == there), 1, 0)
        for rot in range(ROTS):
            m1, m2, m3, m4 = order(rot)
            block = (digit[m3] + 2 * digit[m4]) * 4 + digit[m1] + 2 * digit[m2]
            table[128 + rot * PAIRS + pair] = block
        return jnp.where(alone, carry + 1, carry)

    lax.fori_loop(0, PAIRS, place, jnp.int32(0))

    def listed_once(rank, carry):
        def find(pair, chosen):
            return jnp.where(table[AT_RANK + pair] == rank, pair, chosen)

        table[AT_LIST + rank] = lax.fori_loop(0, PAIRS, find, jnp.int32(0))
        return carry

    lax.fori_loop(0, ONCE, listed_once, 0)


def kernel(partners_in, lmo_energy_in, factors, integrals, pao_energy_in, tile, *scratch):
    row = list(scratch[0:4])
    last = list(scratch[4:8])
    send3 = list(scratch[8:12])
    send4 = list(scratch[12:16])
    passing = list(scratch[16:20])
    final = [list(scratch[20:24]), list(scratch[24:28])]
    (table, source, slot, own_rows, other_energy, flipped, fitted, energy, early_sum, product,
     partners, lmo_energy, pao_energy, local_sem, send_sem, recv_sem) = scratch[28:44]
    reduction = scratch[44:]

    barrier = pltpu.get_barrier_semaphore()
    greeted = [neighbour(mask) for mask in MASKS] + [along_y(0, 1), along_y(1), along_y(3)]
    for device in greeted:
        pl.semaphore_signal(barrier, inc=1, device_id=device, device_id_type=MESH)
    pl.semaphore_wait(barrier, len(greeted))

    def copy(rot, kind, src, dst, mask):
        return pltpu.make_async_remote_copy(
            src_ref=src,
            dst_ref=dst,
            send_sem=send_sem.at[rot, kind],
            recv_sem=recv_sem.at[rot, kind],
            device_id=neighbour(mask),
            device_id_type=MESH,
        )

    copies = []
    for rot in range(ROTS):
        m1, m2, m3, m4 = order(rot)
        own = factors.at[:, pl.ds(rot * PIECE, PIECE), :]
        row_copies = [
            copy(rot, 0, own, row[rot].at[pl.ds(6, 6)], m1),
            copy(rot, 1, own, row[rot].at[pl.ds(12, 6)], m2),
            copy(rot, 2, row[rot].at[pl.ds(6, 6)], last[rot], m2),
        ]
        for k, first, count in ((0, 0, 3), (0, 3, 1), (1, 0, 4)):
            at, kind = pl.ds(first, count), len(row_copies)
            place = [pl.ds(4 * block + first, count) for block in range(4)]
            row_copies += [
                copy(rot, kind, send3[rot].at[k, 1, at], passing[rot].at[k, at], m3),
                copy(rot, kind + 1, send3[rot].at[k, 0, at], final[k][rot].at[place[1]], m3),
                copy(rot, kind + 2, send4[rot].at[k, at], final[k][rot].at[place[2]], m4),
                copy(rot, kind + 3, passing[rot].at[k, at], final[k][rot].at[place[3]], m4),
            ]
        copies.append(row_copies)
    for rot in range(ROTS):
        copies[rot][0].start()
    for rot in range(ROTS):
        copies[rot][1].start()
    small = []
    for item, (src, dst) in enumerate(
        ((partners_in, partners), (lmo_energy_in, lmo_energy), (pao_energy_in, pao_energy))
    ):
        small.append(pltpu.make_async_copy(src, dst, local_sem.at[ROTS + 1 + item]))
        small[item].start()
    local = []
    for rot in range(ROTS):
        own = factors.at[:, pl.ds(rot * PIECE, PIECE), :]
        local.append(pltpu.make_async_copy(own, row[rot].at[pl.ds(0, 6)], local_sem.at[rot]))
        local[rot].start()
    local.append(pltpu.make_async_copy(integrals, fitted, local_sem.at[ROTS]))
    local[ROTS].start()

    for copying in small:
        copying.wait()
    fill_table(table, source, slot, partners)

    first = (lax.axis_index("wide") * 8 + lax.axis_index("narrow")) * LMO
    own_rows[...] = jnp.zeros_like(own_rows)
    for i in range(LMO):
        own_rows[i : i + 1, :] = pao_energy[pl.ds(first + i, 1), :] - lmo_energy[first + i]

    def fetch(i, carry):
        for k in range(PARTNERS):
            listed = partners[k, first + i]
            other_energy[i * PARTNERS + k] = pao_energy[pl.ds(listed, 1), :] - lmo_energy[listed]
        return carry

    lax.fori_loop(0, LMO, fetch, 0)
    columns = jnp.transpose(own_rows[...])
    for copying in local:
        copying.wait()
    for i in range(LMO):
        energy[i] = jnp.broadcast_to(columns[:, i : i + 1], (PAO, PAO))
        flipped[:, i * PAO : (i + 1) * PAO] = jnp.transpose(fitted[i])

    for rot in range(ROTS):
        copies[rot][0].wait_recv()
        copies[rot][2].start()
    for rot in range(ROTS):
        copies[rot][1].wait_recv()

    def gather(rot, receiver, k, start, stop):
        held = row[rot] if start < 3 else last[rot]

        def body(q, carry):
            value = held[table[rot * 32 + receiver * 8 + k * 4 + q]]
            if receiver < 2:
                send3[rot][k, receiver, q] = value
            elif receiver == 2:
                send4[rot][k, q] = value
            else:
                final[k][rot][q] = value
            return carry

        lax.fori_loop(start, stop, body, 0)

    for receiver, kind in ((1, 3), (0, 4), (2, 5)):
        for rot in range(ROTS):
            gather(rot, receiver, 0, 0, 3)
            copies[rot][kind].start()
    for rot in range(ROTS):
        copies[rot][2].wait_recv()
        gather(rot, 1, 0, 3, 4)
        copies[rot][7].start()
    for rot in range(ROTS):
        for receiver, kind in ((0, 8), (2, 9)):
            gather(rot, receiver, 0, 3, 4)
            copies[rot][kind].start()
    for rot in range(ROTS):
        for receiver in (1, 0, 2):
            gather(rot, receiver, 1, 0, 3)
            gather(rot, receiver, 1, 3, 4)
    for kind in (3, 7):
        for rot in range(ROTS):
            copies[rot][kind].wait_recv()
            copies[rot][kind + 3].start()
    for kind in (11, 12, 13):
        for rot in range(ROTS):
            copies[rot][kind].start()
    for rot in range(ROTS):
        for k in range(2):
            gather(rot, 3, k, 0, 3)
            gather(rot, 3, k, 3, 4)
    product[ONCE] = jnp.zeros((PAO, AUX), jnp.float32)
    total = reduction[0]
    blocks = [(rank // 3, pl.ds(rank % 3 * PAO, PAO)) for rank in range(ONCE)]
    for rank in range(ONCE):
        pair = table[AT_LIST + rank]
        total[blocks[rank]] = 1.0 / (energy[lax.div(pair, PARTNERS)] + other_energy[pair])
    for rot in range(ROTS):
        for kind in (4, 5, 6, 8, 9, 10):
            copies[rot][kind].wait_recv()

    def one(i, carry):
        mine = jnp.concatenate([row[rot][i] for rot in range(ROTS)], axis=0)
        others = jnp.concatenate(
            [
                final[0][rot][table[128 + rot * PAIRS + i * PARTNERS + k]]
                for k in range(PARTNERS)
                for rot in range(ROTS)
            ],
            axis=0,
        )
        integral = lax.dot_general(
            mine, others, (((1,), (1,)), ((), ())), preferred_element_type=jnp.float32
        )
        parts = []
        for k in range(PARTNERS):
            pair = i * PARTNERS + k
            keep = jnp.where(table[AT_ONCE + pair] == 1, 0.0, 1.0)
            parts.append(
                integral[:, k * PAO : (k + 1) * PAO] / (energy[i] + other_energy[pair]) * keep
            )
        amplitude = jnp.concatenate(parts, axis=1).astype(jnp.bfloat16)
        early_sum[i] = jnp.dot(amplitude, others, preferred_element_type=jnp.float32)
        return carry

    lax.fori_loop(0, LMO // 2, one, 0)
    for rot in range(ROTS):
        copies[rot][11].wait_recv()
        copies[rot][14].start()
    lax.fori_loop(LMO // 2, LMO, one, 0)
    for rot in range(ROTS):
        for kind in (12, 13, 14):
            copies[rot][kind].wait_recv()

    for rank in range(ONCE):
        pair = table[AT_LIST + rank]
        i = lax.div(pair, PARTNERS)
        mine = jnp.concatenate([row[rot][i] for rot in range(ROTS)], axis=0)
        other = jnp.concatenate(
            [final[1][rot][table[128 + rot * PAIRS + pair]] for rot in range(ROTS)], axis=0
        )
        integral = lax.dot_general(
            mine, other, (((1,), (1,)), ((), ())), preferred_element_type=jnp.float32
        )
        amplitude = (integral * total[blocks[rank]]).astype(jnp.bfloat16)
        product[rank] = jnp.dot(amplitude, other, preferred_element_type=jnp.float32)

    def combine(i, carry):
        gathered = early_sum[i]
        for k in range(PARTNERS):
            gathered = gathered + product[table[AT_RANK + i * PARTNERS + k]]
        fitted[i] = gathered.astype(jnp.bfloat16)
        return carry

    lax.fori_loop(0, LMO, combine, 0)

    reduce_total(tile, flipped, fitted, *reduction)

    for rot in range(ROTS):
        for kind in range(15):
            copies[rot][kind].wait_send()


def local(factors, integrals, pao_energy, lmo_energy, partners):
    vmem = pl.BlockSpec(memory_space=pltpu.VMEM)
    anywhere = pl.BlockSpec(memory_space=pl.ANY)
    piece = (PIECE, AUX)
    scratch = []
    for shape in ((18,), (6,), (2, 2, 4), (2, 4), (2, 4), (16,), (16,)):
        scratch += [pltpu.VMEM(shape + piece, jnp.bfloat16) for _ in range(ROTS)]
    scratch += [
        pltpu.SMEM((AT_LIST + ONCE,), jnp.int32),
        pltpu.SMEM((PAIRS,), jnp.int32),
        pltpu.SMEM((PAIRS,), jnp.int32),
        pltpu.VMEM((8, PAO), jnp.float32),
        pltpu.VMEM((PAIRS, 1, PAO), jnp.float32),
        pltpu.VMEM((AUX, LMO * PAO), jnp.bfloat16),
        pltpu.VMEM((LMO, PAO, AUX), jnp.bfloat16),
        pltpu.VMEM((LMO, PAO, PAO), jnp.float32),
        pltpu.VMEM((LMO, PAO, AUX), jnp.float32),
        pltpu.VMEM((ONCE + 1, PAO, AUX), jnp.float32),
        pltpu.SMEM((PARTNERS, LMOS), jnp.int32),
        pltpu.SMEM((LMOS,), jnp.float32),
        pltpu.VMEM((LMOS, PAO), jnp.float32),
        pltpu.SemaphoreType.DMA((ROTS + 4,)),
        pltpu.SemaphoreType.DMA((ROTS, 15)),
        pltpu.SemaphoreType.DMA((ROTS, 15)),
        pltpu.VMEM((CHUNKS, AUX, 256), jnp.float32),
        pltpu.VMEM((CHUNKS, 4, ROWS, 256), jnp.float32),
        pltpu.VMEM((4, ROWS, AUX), jnp.float32),
        pltpu.VMEM((2, CHUNKS, 2, ROWS, 128), jnp.bfloat16),
        pltpu.VMEM((2, CHUNKS, 2, ROWS, 128), jnp.bfloat16),
        pltpu.VMEM((2, CHUNKS, ROWS, 128), jnp.bfloat16),
        pltpu.VMEM((2, CHUNKS, ROWS, 128), jnp.bfloat16),
        pltpu.VMEM((128, AUX), jnp.float32),
        pltpu.VMEM((AUX, 128), jnp.float32),
        pltpu.VMEM((AUX, 128), jnp.bfloat16),
        pltpu.VMEM((15, HEIGHT, 128), jnp.bfloat16),
        pltpu.SemaphoreType.DMA((2, CHUNKS, 4)),
        pltpu.SemaphoreType.DMA((4, 2, CHUNKS)),
        pltpu.SemaphoreType.DMA((2, 15)),
    ]
    return pl.pallas_call(
        kernel,
        out_shape=jax.ShapeDtypeStruct((HEIGHT, ROWS), jnp.float32),
        in_specs=[anywhere] * 5,
        out_specs=vmem,
        scratch_shapes=scratch,
        compiler_params=pltpu.CompilerParams(
            collective_id=0, has_side_effects=True, vmem_limit_bytes=60 * 2**20
        ),
    )(partners.T, lmo_energy, factors, integrals, pao_energy)


def solution(mesh):
    in_specs = (P(("wide", "narrow"), None, None), P(("wide", "narrow"), None, None), P(), P(), P())
    out_specs = P("wide", "narrow")
    return jax.shard_map(local, mesh=mesh, in_specs=in_specs, out_specs=out_specs, check_vma=False)
```

```python
import jax
import jax.numpy as jnp
from jax import lax
from jax.experimental import pallas as pl
from jax.experimental.pallas import tpu as pltpu
from jax.sharding import PartitionSpec as P

MESH = pl.DeviceIdType.MESH
LMO = 6
LMOS = 768
PARTNERS = 4
PAIRS = LMO * PARTNERS
PAO = 256
AUX = 768
ROWS = AUX // 8
HEIGHT = AUX // 16
CHUNKS = AUX // 2 // 128
ROTS = 4
PIECE = PAO // ROTS
ONCE = 8

AT_ONCE = 128 + ROTS * PAIRS
AT_RANK = AT_ONCE + PAIRS
AT_LIST = AT_RANK + PAIRS

MASKS = (1, 4, 3, 12)


def order(rot):
    return [MASKS[(rot + step) % 4] for step in range(4)]


def flip(position, mask):
    if mask == 0:
        return position
    if mask == 3:
        return 3 - position
    if mask == 2:
        return lax.rem(position + 2, 4)
    return position + 1 - 2 * lax.rem(position, 2)


def neighbour(mask):
    wide = lax.axis_index("wide")
    z, x = wide // 4, lax.rem(wide, 4)
    return (flip(z, mask // 4) * 4 + flip(x, mask % 4), lax.axis_index("narrow"))


def along_y(mask, core=0):
    narrow = lax.axis_index("narrow")
    y, c = narrow // 2, lax.rem(narrow, 2)
    return (lax.axis_index("wide"), flip(y, mask) * 2 + flip(c, core))


def reduce_total(
    sent, tile, flipped, fitted, total, core_in, summed, first_out, first_in, second_out, second_in, block, turned, outgoing, tiles_in,
    core_sem, y_sem, wide_sem,
):
    narrow, wide = lax.axis_index("narrow"), lax.axis_index("wide")
    y, core = narrow // 2, lax.rem(narrow, 2)

    def send(src, dst, sems, device):
        return pltpu.make_async_remote_copy(
            src_ref=src, dst_ref=dst, send_sem=sems[0], recv_sem=sems[1],
            device_id=device, device_id_type=MESH,
        )

    def multiply(i, j):
        rows, columns = slice(i * 256, i * 256 + 256), slice(j * 256, j * 256 + 256)
        total[j, rows] = jnp.dot(
            flipped[rows, :],
            fitted[:, :, columns].reshape(LMO * PAO, 256),
            preferred_element_type=jnp.float32,
        )

    def symmetrise(i, j):
        at_i, at_j = slice(i * 256, i * 256 + 256), slice(j * 256, j * 256 + 256)
        half = 0.5 * (total[j, at_i] + jnp.transpose(total[i, at_j]))
        total[j, at_i] = half
        if i != j:
            total[i, at_j] = jnp.transpose(half)

    def band(place, c):
        return pl.ds(pl.multiple_of((place * 2 + c) * ROWS, ROWS), ROWS)

    steps = []
    for i in range(CHUNKS):
        for j in range(i, CHUNKS):
            multiply(i, j)
            if i != j:
                multiply(j, i)
        for j in range(i, CHUNKS):
            symmetrise(i, j)
        for place in range(4):
            steps.append(
                send(total.at[i, band(place, 1 - core)], core_in.at[i, place],
                     (core_sem.at[0, i, place], core_sem.at[1, i, place]), along_y(0, 1))
            )
            steps[-1].start()

    plan = ((1, 3, (1, 2)), (3, 1, (3, 2)))
    firsts, seconds = {}, {}
    chunks = [(h, chunk) for chunk in range(CHUNKS) for h in range(2)]

    def columns(h, chunk):
        start = chunk * 256 + h * 128
        return slice(start, start + 128)

    for h, chunk in chunks:
        near, far, leaving = plan[h]
        if h == 0:
            for step in steps[4 * chunk : 4 * chunk + 4]:
                step.wait_recv()
            at = pl.ds(chunk * 256, 256)
            for place in range(4):
                summed[place, :, at] = total[chunk, band(place, core)] + core_in[chunk, place]
        for place, u in enumerate(leaving):
            first_out[h, chunk, place] = summed[flip(y, u), :, columns(h, chunk)].astype(first_out.dtype)
        firsts[h, chunk] = send(
            first_out.at[h, chunk], first_in.at[h, chunk],
            (y_sem.at[0, h, chunk], y_sem.at[1, h, chunk]), along_y(near),
        )
        firsts[h, chunk].start()
    block[pl.ds(ROWS, 128 - ROWS), :] = jnp.zeros((128 - ROWS, AUX), jnp.float32)
    for h, chunk in chunks:
        near, far, leaving = plan[h]
        firsts[h, chunk].wait_recv()
        passed = summed[flip(y, far), :, columns(h, chunk)] + first_in[h, chunk, 1].astype(jnp.float32)
        second_out[h, chunk] = passed.astype(second_out.dtype)
        seconds[h, chunk] = send(
            second_out.at[h, chunk], second_in.at[h, chunk],
            (y_sem.at[2, h, chunk], y_sem.at[3, h, chunk]), along_y(far),
        )
        seconds[h, chunk].start()
    def row_of(t):
        peer = flip(wide // 4, t // 4) * 4 + flip(lax.rem(wide, 4), t % 4)
        return peer * HEIGHT

    def rows(t):
        return pl.ds(pl.multiple_of(row_of(t), HEIGHT), HEIGHT)

    spread = []
    for t in range(1, 16):
        spread.append(
            send(outgoing.at[rows(t)], tiles_in.at[t - 1],
                 (wide_sem.at[0, t - 1], wide_sem.at[1, t - 1]), neighbour(t))
        )

    def send_tiles(chunk):
        for t in range(1, 16):
            end = row_of(t) + HEIGHT

            @pl.when((end > chunk * 256) & (end <= chunk * 256 + 256))
            def _():
                spread[t - 1].start()

    for h, chunk in chunks:
        at = columns(h, chunk)
        kept = summed[y, :, at] + first_in[h, chunk, 0].astype(jnp.float32)
        seconds[h, chunk].wait_recv()
        block[pl.ds(0, ROWS), at] = kept + second_in[h, chunk].astype(jnp.float32)
        turned[at, :] = jnp.transpose(block[:, at])
        outgoing[at, :] = turned[at, :].astype(outgoing.dtype)
        if h == 1:
            send_tiles(chunk)

    for step in sent + steps + list(firsts.values()) + list(seconds.values()):
        step.wait_send()
    result = turned[rows(0), :]
    for t in range(1, 16):
        spread[t - 1].wait_recv()
        result = result + tiles_in[t - 1].astype(jnp.float32)
    tile[...] = result[:, :ROWS]

    for step in spread:
        step.wait_send()


def fill_table(table, source, slot, partners):
    wide, narrow = lax.axis_index("wide"), lax.axis_index("narrow")
    z, x = wide // 4, lax.rem(wide, 4)

    def group(mask):
        return flip(z, mask // 4) * 4 + flip(x, mask % 4)

    for rot in range(ROTS):
        m1, m2, m3, m4 = order(rot)
        senders = [group(mask) for mask in (0, m1, m2, m1 ^ m2)]
        for receiver, mask in enumerate((m3, m3 ^ m4, m4, 0)):
            first = (group(mask) * 8 + narrow) * LMO

            def scan(i, found):
                found = list(found)
                for k in range(PARTNERS):
                    listed = partners[k, first + i]
                    owner = lax.div(listed, LMO)
                    place = listed - owner * LMO
                    holder = lax.div(owner, 8)
                    for q in range(4):
                        hit = holder == senders[q]
                        low, high, summed = found[3 * q : 3 * q + 3]
                        found[3 * q] = jnp.where(hit, jnp.minimum(low, place), low)
                        found[3 * q + 1] = jnp.where(hit, jnp.maximum(high, place), high)
                        found[3 * q + 2] = jnp.where(hit, summed + place, summed)
                return tuple(found)

            found = lax.fori_loop(0, LMO, scan, (jnp.int32(LMO - 1), jnp.int32(0), jnp.int32(0)) * 4)
            for q in range(4):
                low, high, summed = found[3 * q : 3 * q + 3]
                twice = summed - low - high
                for k, chosen in enumerate((twice, low + high - twice)):
                    chosen = jnp.minimum(jnp.maximum(chosen, 0), LMO - 1)
                    table[rot * 32 + receiver * 8 + k * 4 + q] = chosen + (q * LMO if q < 3 else 0)

    first = (wide * 8 + narrow) * LMO

    def split(i, carry):
        for k in range(PARTNERS):
            listed = partners[k, first + i]
            owner = lax.div(listed, LMO)
            source[i * PARTNERS + k] = lax.div(owner, 8)
            slot[i * PARTNERS + k] = listed - owner * LMO
        return carry

    lax.fori_loop(0, LMO, split, 0)

    def place(pair, carry):
        mine, mine_slot = source[pair], slot[pair]

        def same(i, count):
            for k in range(PARTNERS):
                other = i * PARTNERS + k
                count = jnp.where((source[other] == mine) & (slot[other] == mine_slot), count + 1, count)
            return count

        alone = lax.fori_loop(0, LMO, same, jnp.int32(0)) == 1
        table[AT_ONCE + pair] = jnp.where(alone, 1, 0)
        table[AT_RANK + pair] = jnp.where(alone, carry, ONCE)
        sz = lax.div(mine, 4)
        sx = mine - sz * 4
        digit = {}
        for low_mask, high_mask, here, there in ((1, 3, x, sx), (4, 12, z, sz)):
            digit[low_mask] = jnp.where((flip(here, 1) == there) | (flip(here, 2) == there), 1, 0)
            digit[high_mask] = jnp.where((flip(here, 3) == there) | (flip(here, 2) == there), 1, 0)
        for rot in range(ROTS):
            m1, m2, m3, m4 = order(rot)
            block = (digit[m3] + 2 * digit[m4]) * 4 + digit[m1] + 2 * digit[m2]
            table[128 + rot * PAIRS + pair] = block
        return jnp.where(alone, carry + 1, carry)

    lax.fori_loop(0, PAIRS, place, jnp.int32(0))

    def listed_once(rank, carry):
        def find(pair, chosen):
            return jnp.where(table[AT_RANK + pair] == rank, pair, chosen)

        table[AT_LIST + rank] = lax.fori_loop(0, PAIRS, find, jnp.int32(0))
        return carry

    lax.fori_loop(0, ONCE, listed_once, 0)


def kernel(partners_in, lmo_energy_in, factors, integrals, pao_energy_in, tile, *scratch):
    row = list(scratch[0:4])
    last = list(scratch[4:8])
    send3 = list(scratch[8:12])
    send4 = list(scratch[12:16])
    passing = list(scratch[16:20])
    final = [list(scratch[20:24]), list(scratch[24:28])]
    (table, source, slot, own_rows, other_energy, flipped, fitted, energy, early_sum, product,
     partners, lmo_energy, pao_energy, local_sem, send_sem, recv_sem) = scratch[28:44]
    reduction = scratch[44:]

    barrier = pltpu.get_barrier_semaphore()
    greeted = [neighbour(mask) for mask in MASKS] + [along_y(0, 1), along_y(1), along_y(3)]
    for device in greeted:
        pl.semaphore_signal(barrier, inc=1, device_id=device, device_id_type=MESH)
    pl.semaphore_wait(barrier, len(greeted))

    def copy(rot, kind, src, dst, mask):
        return pltpu.make_async_remote_copy(
            src_ref=src,
            dst_ref=dst,
            send_sem=send_sem.at[rot, kind],
            recv_sem=recv_sem.at[rot, kind],
            device_id=neighbour(mask),
            device_id_type=MESH,
        )

    copies = []
    for rot in range(ROTS):
        m1, m2, m3, m4 = order(rot)
        own = factors.at[:, pl.ds(rot * PIECE, PIECE), :]
        row_copies = [
            copy(rot, 0, own, row[rot].at[pl.ds(6, 6)], m1),
            copy(rot, 1, own, row[rot].at[pl.ds(12, 6)], m2),
            copy(rot, 2, row[rot].at[pl.ds(6, 6)], last[rot], m2),
        ]
        for k, first, count in ((0, 0, 3), (0, 3, 1), (1, 0, 4)):
            at, kind = pl.ds(first, count), len(row_copies)
            place = [pl.ds(4 * block + first, count) for block in range(4)]
            row_copies += [
                copy(rot, kind, send3[rot].at[k, 1, at], passing[rot].at[k, at], m3),
                copy(rot, kind + 1, send3[rot].at[k, 0, at], final[k][rot].at[place[1]], m3),
                copy(rot, kind + 2, send4[rot].at[k, at], final[k][rot].at[place[2]], m4),
                copy(rot, kind + 3, passing[rot].at[k, at], final[k][rot].at[place[3]], m4),
            ]
        copies.append(row_copies)
    for rot in range(ROTS):
        copies[rot][0].start()
    for rot in range(ROTS):
        copies[rot][1].start()
    small = []
    for item, (src, dst) in enumerate(
        ((partners_in, partners), (lmo_energy_in, lmo_energy), (pao_energy_in, pao_energy))
    ):
        small.append(pltpu.make_async_copy(src, dst, local_sem.at[ROTS + 1 + item]))
        small[item].start()
    local = []
    for rot in range(ROTS):
        own = factors.at[:, pl.ds(rot * PIECE, PIECE), :]
        local.append(pltpu.make_async_copy(own, row[rot].at[pl.ds(0, 6)], local_sem.at[rot]))
        local[rot].start()
    local.append(pltpu.make_async_copy(integrals, fitted, local_sem.at[ROTS]))
    local[ROTS].start()

    for copying in small:
        copying.wait()
    fill_table(table, source, slot, partners)

    first = (lax.axis_index("wide") * 8 + lax.axis_index("narrow")) * LMO
    own_rows[...] = jnp.zeros_like(own_rows)
    for i in range(LMO):
        own_rows[i : i + 1, :] = pao_energy[pl.ds(first + i, 1), :] - lmo_energy[first + i]

    def fetch(i, carry):
        for k in range(PARTNERS):
            listed = partners[k, first + i]
            other_energy[i * PARTNERS + k] = pao_energy[pl.ds(listed, 1), :] - lmo_energy[listed]
        return carry

    lax.fori_loop(0, LMO, fetch, 0)
    columns = jnp.transpose(own_rows[...])
    for copying in local:
        copying.wait()
    for i in range(LMO):
        energy[i] = jnp.broadcast_to(columns[:, i : i + 1], (PAO, PAO))
        flipped[:, i * PAO : (i + 1) * PAO] = jnp.transpose(fitted[i])

    for rot in range(ROTS):
        copies[rot][0].wait_recv()
        copies[rot][2].start()
    for rot in range(ROTS):
        copies[rot][1].wait_recv()

    def gather(rot, receiver, k, start, stop):
        held = row[rot] if start < 3 else last[rot]

        def body(q, carry):
            value = held[table[rot * 32 + receiver * 8 + k * 4 + q]]
            if receiver < 2:
                send3[rot][k, receiver, q] = value
            elif receiver == 2:
                send4[rot][k, q] = value
            else:
                final[k][rot][q] = value
            return carry

        lax.fori_loop(start, stop, body, 0)

    for receiver, kind in ((1, 3), (0, 4), (2, 5)):
        for rot in range(ROTS):
            gather(rot, receiver, 0, 0, 3)
            copies[rot][kind].start()
    for rot in range(ROTS):
        copies[rot][2].wait_recv()
        gather(rot, 1, 0, 3, 4)
        copies[rot][7].start()
    for rot in range(ROTS):
        for receiver, kind in ((0, 8), (2, 9)):
            gather(rot, receiver, 0, 3, 4)
            copies[rot][kind].start()
    for rot in range(ROTS):
        for receiver in (1, 0, 2):
            gather(rot, receiver, 1, 0, 3)
            gather(rot, receiver, 1, 3, 4)
    for kind in (3, 7):
        for rot in range(ROTS):
            copies[rot][kind].wait_recv()
            copies[rot][kind + 3].start()
    for kind in (11, 12, 13):
        for rot in range(ROTS):
            copies[rot][kind].start()
    for rot in range(ROTS):
        for k in range(2):
            gather(rot, 3, k, 0, 3)
            gather(rot, 3, k, 3, 4)
    product[ONCE] = jnp.zeros((PAO, AUX), jnp.float32)
    total = reduction[0]
    blocks = [(rank // 3, pl.ds(rank % 3 * PAO, PAO)) for rank in range(ONCE)]
    for rank in range(ONCE):
        pair = table[AT_LIST + rank]
        total[blocks[rank]] = 1.0 / (energy[lax.div(pair, PARTNERS)] + other_energy[pair])
    for rot in range(ROTS):
        for kind in (4, 5, 6, 8, 9, 10):
            copies[rot][kind].wait_recv()

    def one(i, carry):
        mine = jnp.concatenate([row[rot][i] for rot in range(ROTS)], axis=0)
        others = jnp.concatenate(
            [
                final[0][rot][table[128 + rot * PAIRS + i * PARTNERS + k]]
                for k in range(PARTNERS)
                for rot in range(ROTS)
            ],
            axis=0,
        )
        integral = lax.dot_general(
            mine, others, (((1,), (1,)), ((), ())), preferred_element_type=jnp.float32
        )
        parts = []
        for k in range(PARTNERS):
            pair = i * PARTNERS + k
            keep = jnp.where(table[AT_ONCE + pair] == 1, 0.0, 1.0)
            parts.append(
                integral[:, k * PAO : (k + 1) * PAO] / (energy[i] + other_energy[pair]) * keep
            )
        amplitude = jnp.concatenate(parts, axis=1).astype(jnp.bfloat16)
        early_sum[i] = jnp.dot(amplitude, others, preferred_element_type=jnp.float32)
        return carry

    lax.fori_loop(0, LMO // 2, one, 0)
    for rot in range(ROTS):
        copies[rot][11].wait_recv()
        copies[rot][14].start()
    lax.fori_loop(LMO // 2, LMO, one, 0)
    for rot in range(ROTS):
        for kind in range(11):
            copies[rot][kind].wait_send()
    for rot in range(ROTS):
        for kind in (12, 13, 14):
            copies[rot][kind].wait_recv()

    for rank in range(ONCE):
        pair = table[AT_LIST + rank]
        i = lax.div(pair, PARTNERS)
        mine = jnp.concatenate([row[rot][i] for rot in range(ROTS)], axis=0)
        other = jnp.concatenate(
            [final[1][rot][table[128 + rot * PAIRS + pair]] for rot in range(ROTS)], axis=0
        )
        integral = lax.dot_general(
            mine, other, (((1,), (1,)), ((), ())), preferred_element_type=jnp.float32
        )
        amplitude = (integral * total[blocks[rank]]).astype(jnp.bfloat16)
        product[rank] = jnp.dot(amplitude, other, preferred_element_type=jnp.float32)

    def combine(i, carry):
        gathered = early_sum[i]
        for k in range(PARTNERS):
            gathered = gathered + product[table[AT_RANK + i * PARTNERS + k]]
        fitted[i] = gathered.astype(jnp.bfloat16)
        return carry

    lax.fori_loop(0, LMO, combine, 0)

    sent = [copies[rot][kind] for rot in range(ROTS) for kind in range(11, 15)]
    reduce_total(sent, tile, flipped, fitted, *reduction)


def local(factors, integrals, pao_energy, lmo_energy, partners):
    vmem = pl.BlockSpec(memory_space=pltpu.VMEM)
    anywhere = pl.BlockSpec(memory_space=pl.ANY)
    piece = (PIECE, AUX)
    scratch = []
    for shape in ((18,), (6,), (2, 2, 4), (2, 4), (2, 4), (16,), (16,)):
        scratch += [pltpu.VMEM(shape + piece, jnp.bfloat16) for _ in range(ROTS)]
    scratch += [
        pltpu.SMEM((AT_LIST + ONCE,), jnp.int32),
        pltpu.SMEM((PAIRS,), jnp.int32),
        pltpu.SMEM((PAIRS,), jnp.int32),
        pltpu.VMEM((8, PAO), jnp.float32),
        pltpu.VMEM((PAIRS, 1, PAO), jnp.float32),
        pltpu.VMEM((AUX, LMO * PAO), jnp.bfloat16),
        pltpu.VMEM((LMO, PAO, AUX), jnp.bfloat16),
        pltpu.VMEM((LMO, PAO, PAO), jnp.float32),
        pltpu.VMEM((LMO, PAO, AUX), jnp.float32),
        pltpu.VMEM((ONCE + 1, PAO, AUX), jnp.float32),
        pltpu.SMEM((PARTNERS, LMOS), jnp.int32),
        pltpu.SMEM((LMOS,), jnp.float32),
        pltpu.VMEM((LMOS, PAO), jnp.float32),
        pltpu.SemaphoreType.DMA((ROTS + 4,)),
        pltpu.SemaphoreType.DMA((ROTS, 15)),
        pltpu.SemaphoreType.DMA((ROTS, 15)),
        pltpu.VMEM((CHUNKS, AUX, 256), jnp.float32),
        pltpu.VMEM((CHUNKS, 4, ROWS, 256), jnp.float32),
        pltpu.VMEM((4, ROWS, AUX), jnp.float32),
        pltpu.VMEM((2, CHUNKS, 2, ROWS, 128), jnp.bfloat16),
        pltpu.VMEM((2, CHUNKS, 2, ROWS, 128), jnp.bfloat16),
        pltpu.VMEM((2, CHUNKS, ROWS, 128), jnp.bfloat16),
        pltpu.VMEM((2, CHUNKS, ROWS, 128), jnp.bfloat16),
        pltpu.VMEM((128, AUX), jnp.float32),
        pltpu.VMEM((AUX, 128), jnp.float32),
        pltpu.VMEM((AUX, 128), jnp.bfloat16),
        pltpu.VMEM((15, HEIGHT, 128), jnp.bfloat16),
        pltpu.SemaphoreType.DMA((2, CHUNKS, 4)),
        pltpu.SemaphoreType.DMA((4, 2, CHUNKS)),
        pltpu.SemaphoreType.DMA((2, 15)),
    ]
    return pl.pallas_call(
        kernel,
        out_shape=jax.ShapeDtypeStruct((HEIGHT, ROWS), jnp.float32),
        in_specs=[anywhere] * 5,
        out_specs=vmem,
        scratch_shapes=scratch,
        compiler_params=pltpu.CompilerParams(
            collective_id=0, has_side_effects=True, vmem_limit_bytes=60 * 2**20
        ),
    )(partners.T, lmo_energy, factors, integrals, pao_energy)


def solution(mesh):
    in_specs = (P(("wide", "narrow"), None, None), P(("wide", "narrow"), None, None), P(), P(), P())
    out_specs = P("wide", "narrow")
    return jax.shard_map(local, mesh=mesh, in_specs=in_specs, out_specs=out_specs, check_vma=False)
```

```python
import jax
import jax.numpy as jnp
from jax import lax
from jax.experimental import pallas as pl
from jax.experimental.pallas import tpu as pltpu
from jax.sharding import PartitionSpec as P

MESH = pl.DeviceIdType.MESH
LMO = 6
LMOS = 768
PARTNERS = 4
PAIRS = LMO * PARTNERS
PAO = 256
AUX = 768
ROWS = AUX // 8
HEIGHT = AUX // 16
CHUNKS = AUX // 2 // 128
ROTS = 4
PIECE = PAO // ROTS
ONCE = 8

AT_ONCE = 128 + ROTS * PAIRS
AT_RANK = AT_ONCE + PAIRS
AT_LIST = AT_RANK + PAIRS

MASKS = (1, 4, 3, 12)


def order(rot):
    return [MASKS[(rot + step) % 4] for step in range(4)]


def flip(position, mask):
    if mask == 0:
        return position
    if mask == 3:
        return 3 - position
    if mask == 2:
        return lax.rem(position + 2, 4)
    return position + 1 - 2 * lax.rem(position, 2)


def neighbour(mask):
    wide = lax.axis_index("wide")
    z, x = wide // 4, lax.rem(wide, 4)
    return (flip(z, mask // 4) * 4 + flip(x, mask % 4), lax.axis_index("narrow"))


def along_y(mask, core=0):
    narrow = lax.axis_index("narrow")
    y, c = narrow // 2, lax.rem(narrow, 2)
    return (lax.axis_index("wide"), flip(y, mask) * 2 + flip(c, core))


def reduce_total(
    tile, flipped, fitted, total, core_in, summed, first_out, first_in, second_out, second_in, block, turned, outgoing, tiles_in,
    core_sem, y_sem, wide_sem,
):
    narrow, wide = lax.axis_index("narrow"), lax.axis_index("wide")
    y, core = narrow // 2, lax.rem(narrow, 2)

    def send(src, dst, sems, device):
        return pltpu.make_async_remote_copy(
            src_ref=src, dst_ref=dst, send_sem=sems[0], recv_sem=sems[1],
            device_id=device, device_id_type=MESH,
        )

    def multiply(i, j):
        rows, columns = slice(i * 256, i * 256 + 256), slice(j * 256, j * 256 + 256)
        total[j, rows] = jnp.dot(
            flipped[rows, :],
            fitted[:, :, columns].reshape(LMO * PAO, 256),
            preferred_element_type=jnp.float32,
        )

    def symmetrise(i, j):
        at_i, at_j = slice(i * 256, i * 256 + 256), slice(j * 256, j * 256 + 256)
        half = 0.5 * (total[j, at_i] + jnp.transpose(total[i, at_j]))
        total[j, at_i] = half
        if i != j:
            total[i, at_j] = jnp.transpose(half)

    def band(place, c):
        return pl.ds(pl.multiple_of((place * 2 + c) * ROWS, ROWS), ROWS)

    steps = []
    for i in range(CHUNKS):
        for j in range(i, CHUNKS):
            multiply(i, j)
            if i != j:
                multiply(j, i)
        for j in range(i, CHUNKS):
            symmetrise(i, j)
        for place in range(4):
            steps.append(
                send(total.at[i, band(place, 1 - core)], core_in.at[i, place],
                     (core_sem.at[0, i, place], core_sem.at[1, i, place]), along_y(0, 1))
            )
            steps[-1].start()

    plan = ((1, 3, (1, 2)), (3, 1, (3, 2)))
    firsts, seconds = {}, {}
    chunks = [(h, chunk) for chunk in range(CHUNKS) for h in range(2)]

    def columns(h, chunk):
        start = chunk * 256 + h * 128
        return slice(start, start + 128)

    for h, chunk in chunks:
        near, far, sent = plan[h]
        if h == 0:
            for step in steps[4 * chunk : 4 * chunk + 4]:
                step.wait_recv()
            at = pl.ds(chunk * 256, 256)
            for place in range(4):
                summed[place, :, at] = total[chunk, band(place, core)] + core_in[chunk, place]
        for place, u in enumerate(sent):
            first_out[h, chunk, place] = summed[flip(y, u), :, columns(h, chunk)].astype(first_out.dtype)
        firsts[h, chunk] = send(
            first_out.at[h, chunk], first_in.at[h, chunk],
            (y_sem.at[0, h, chunk], y_sem.at[1, h, chunk]), along_y(near),
        )
        firsts[h, chunk].start()
    block[pl.ds(ROWS, 128 - ROWS), :] = jnp.zeros((128 - ROWS, AUX), jnp.float32)
    for h, chunk in chunks:
        near, far, sent = plan[h]
        firsts[h, chunk].wait_recv()
        passed = summed[flip(y, far), :, columns(h, chunk)] + first_in[h, chunk, 1].astype(jnp.float32)
        second_out[h, chunk] = passed.astype(second_out.dtype)
        seconds[h, chunk] = send(
            second_out.at[h, chunk], second_in.at[h, chunk],
            (y_sem.at[2, h, chunk], y_sem.at[3, h, chunk]), along_y(far),
        )
        seconds[h, chunk].start()
    def row_of(t):
        peer = flip(wide // 4, t // 4) * 4 + flip(lax.rem(wide, 4), t % 4)
        return peer * HEIGHT

    def rows(t):
        return pl.ds(pl.multiple_of(row_of(t), HEIGHT), HEIGHT)

    spread = []
    for t in range(1, 16):
        spread.append(
            send(outgoing.at[rows(t)], tiles_in.at[t - 1],
                 (wide_sem.at[0, t - 1], wide_sem.at[1, t - 1]), neighbour(t))
        )

    def send_tiles(start):
        for t in range(1, 16):
            end = row_of(t) + HEIGHT

            @pl.when((end > start) & (end <= start + 128))
            def _():
                spread[t - 1].start()

    for h, chunk in chunks:
        at = columns(h, chunk)
        kept = summed[y, :, at] + first_in[h, chunk, 0].astype(jnp.float32)
        seconds[h, chunk].wait_recv()
        block[pl.ds(0, ROWS), at] = kept + second_in[h, chunk].astype(jnp.float32)
        turned[at, :] = jnp.transpose(block[:, at])
        outgoing[at, :] = turned[at, :].astype(outgoing.dtype)
        send_tiles(at.start)

    result = turned[rows(0), :]
    for t in range(1, 16):
        spread[t - 1].wait_recv()
        result = result + tiles_in[t - 1].astype(jnp.float32)
    tile[...] = result[:, :ROWS]

    for step in steps + list(firsts.values()) + list(seconds.values()) + spread:
        step.wait_send()


def fill_table(table, source, slot, partners):
    wide, narrow = lax.axis_index("wide"), lax.axis_index("narrow")
    z, x = wide // 4, lax.rem(wide, 4)

    def group(mask):
        return flip(z, mask // 4) * 4 + flip(x, mask % 4)

    for rot in range(ROTS):
        m1, m2, m3, m4 = order(rot)
        senders = [group(mask) for mask in (0, m1, m2, m1 ^ m2)]
        for receiver, mask in enumerate((m3, m3 ^ m4, m4, 0)):
            first = (group(mask) * 8 + narrow) * LMO

            def scan(i, found):
                found = list(found)
                for k in range(PARTNERS):
                    listed = partners[k, first + i]
                    owner = lax.div(listed, LMO)
                    place = listed - owner * LMO
                    holder = lax.div(owner, 8)
                    for q in range(4):
                        hit = holder == senders[q]
                        low, high, summed = found[3 * q : 3 * q + 3]
                        found[3 * q] = jnp.where(hit, jnp.minimum(low, place), low)
                        found[3 * q + 1] = jnp.where(hit, jnp.maximum(high, place), high)
                        found[3 * q + 2] = jnp.where(hit, summed + place, summed)
                return tuple(found)

            found = lax.fori_loop(0, LMO, scan, (jnp.int32(LMO - 1), jnp.int32(0), jnp.int32(0)) * 4)
            for q in range(4):
                low, high, summed = found[3 * q : 3 * q + 3]
                twice = summed - low - high
                for k, chosen in enumerate((twice, low + high - twice)):
                    chosen = jnp.minimum(jnp.maximum(chosen, 0), LMO - 1)
                    table[rot * 32 + receiver * 8 + k * 4 + q] = chosen + (q * LMO if q < 3 else 0)

    first = (wide * 8 + narrow) * LMO

    def split(i, carry):
        for k in range(PARTNERS):
            listed = partners[k, first + i]
            owner = lax.div(listed, LMO)
            source[i * PARTNERS + k] = lax.div(owner, 8)
            slot[i * PARTNERS + k] = listed - owner * LMO
        return carry

    lax.fori_loop(0, LMO, split, 0)

    def place(pair, carry):
        mine, mine_slot = source[pair], slot[pair]

        def same(i, count):
            for k in range(PARTNERS):
                other = i * PARTNERS + k
                count = jnp.where((source[other] == mine) & (slot[other] == mine_slot), count + 1, count)
            return count

        alone = lax.fori_loop(0, LMO, same, jnp.int32(0)) == 1
        table[AT_ONCE + pair] = jnp.where(alone, 1, 0)
        table[AT_RANK + pair] = jnp.where(alone, carry, ONCE)
        sz = lax.div(mine, 4)
        sx = mine - sz * 4
        digit = {}
        for low_mask, high_mask, here, there in ((1, 3, x, sx), (4, 12, z, sz)):
            digit[low_mask] = jnp.where((flip(here, 1) == there) | (flip(here, 2) == there), 1, 0)
            digit[high_mask] = jnp.where((flip(here, 3) == there) | (flip(here, 2) == there), 1, 0)
        for rot in range(ROTS):
            m1, m2, m3, m4 = order(rot)
            block = (digit[m3] + 2 * digit[m4]) * 4 + digit[m1] + 2 * digit[m2]
            table[128 + rot * PAIRS + pair] = block
        return jnp.where(alone, carry + 1, carry)

    lax.fori_loop(0, PAIRS, place, jnp.int32(0))

    def listed_once(rank, carry):
        def find(pair, chosen):
            return jnp.where(table[AT_RANK + pair] == rank, pair, chosen)

        table[AT_LIST + rank] = lax.fori_loop(0, PAIRS, find, jnp.int32(0))
        return carry

    lax.fori_loop(0, ONCE, listed_once, 0)


def kernel(partners_in, lmo_energy_in, factors, integrals, pao_energy_in, tile, *scratch):
    row = list(scratch[0:4])
    last = list(scratch[4:8])
    send3 = list(scratch[8:12])
    send4 = list(scratch[12:16])
    passing = list(scratch[16:20])
    final = [list(scratch[20:24]), list(scratch[24:28])]
    (table, source, slot, own_rows, other_energy, flipped, fitted, energy, early_sum, product,
     partners, lmo_energy, pao_energy, local_sem, send_sem, recv_sem) = scratch[28:44]
    reduction = scratch[44:]

    barrier = pltpu.get_barrier_semaphore()
    greeted = [neighbour(mask) for mask in MASKS] + [along_y(0, 1), along_y(1), along_y(3)]
    for device in greeted:
        pl.semaphore_signal(barrier, inc=1, device_id=device, device_id_type=MESH)
    pl.semaphore_wait(barrier, len(greeted))

    def copy(rot, kind, src, dst, mask):
        return pltpu.make_async_remote_copy(
            src_ref=src,
            dst_ref=dst,
            send_sem=send_sem.at[rot, kind],
            recv_sem=recv_sem.at[rot, kind],
            device_id=neighbour(mask),
            device_id_type=MESH,
        )

    copies = []
    for rot in range(ROTS):
        m1, m2, m3, m4 = order(rot)
        own = factors.at[:, pl.ds(rot * PIECE, PIECE), :]
        row_copies = [
            copy(rot, 0, own, row[rot].at[pl.ds(6, 6)], m1),
            copy(rot, 1, own, row[rot].at[pl.ds(12, 6)], m2),
            copy(rot, 2, row[rot].at[pl.ds(6, 6)], last[rot], m2),
        ]
        for k, first, count in ((0, 0, 3), (0, 3, 1), (1, 0, 4)):
            at, kind = pl.ds(first, count), len(row_copies)
            place = [pl.ds(4 * block + first, count) for block in range(4)]
            row_copies += [
                copy(rot, kind, send3[rot].at[k, 1, at], passing[rot].at[k, at], m3),
                copy(rot, kind + 1, send3[rot].at[k, 0, at], final[k][rot].at[place[1]], m3),
                copy(rot, kind + 2, send4[rot].at[k, at], final[k][rot].at[place[2]], m4),
                copy(rot, kind + 3, passing[rot].at[k, at], final[k][rot].at[place[3]], m4),
            ]
        copies.append(row_copies)
    for rot in range(ROTS):
        copies[rot][0].start()
    for rot in range(ROTS):
        copies[rot][1].start()
    small = []
    for item, (src, dst) in enumerate(
        ((partners_in, partners), (lmo_energy_in, lmo_energy), (pao_energy_in, pao_energy))
    ):
        small.append(pltpu.make_async_copy(src, dst, local_sem.at[ROTS + 1 + item]))
        small[item].start()
    local = []
    for rot in range(ROTS):
        own = factors.at[:, pl.ds(rot * PIECE, PIECE), :]
        local.append(pltpu.make_async_copy(own, row[rot].at[pl.ds(0, 6)], local_sem.at[rot]))
        local[rot].start()
    local.append(pltpu.make_async_copy(integrals, fitted, local_sem.at[ROTS]))
    local[ROTS].start()

    for copying in small:
        copying.wait()
    fill_table(table, source, slot, partners)

    first = (lax.axis_index("wide") * 8 + lax.axis_index("narrow")) * LMO
    own_rows[...] = jnp.zeros_like(own_rows)
    for i in range(LMO):
        own_rows[i : i + 1, :] = pao_energy[pl.ds(first + i, 1), :] - lmo_energy[first + i]

    def fetch(i, carry):
        for k in range(PARTNERS):
            listed = partners[k, first + i]
            other_energy[i * PARTNERS + k] = pao_energy[pl.ds(listed, 1), :] - lmo_energy[listed]
        return carry

    lax.fori_loop(0, LMO, fetch, 0)
    columns = jnp.transpose(own_rows[...])
    for copying in local:
        copying.wait()
    for i in range(LMO):
        energy[i] = jnp.broadcast_to(columns[:, i : i + 1], (PAO, PAO))
        flipped[:, i * PAO : (i + 1) * PAO] = jnp.transpose(fitted[i])

    for rot in range(ROTS):
        copies[rot][0].wait_recv()
        copies[rot][2].start()
    for rot in range(ROTS):
        copies[rot][1].wait_recv()

    def gather(rot, receiver, k, start, stop):
        held = row[rot] if start < 3 else last[rot]

        def body(q, carry):
            value = held[table[rot * 32 + receiver * 8 + k * 4 + q]]
            if receiver < 2:
                send3[rot][k, receiver, q] = value
            elif receiver == 2:
                send4[rot][k, q] = value
            else:
                final[k][rot][q] = value
            return carry

        lax.fori_loop(start, stop, body, 0)

    for receiver, kind in ((1, 3), (0, 4), (2, 5)):
        for rot in range(ROTS):
            gather(rot, receiver, 0, 0, 3)
            copies[rot][kind].start()
    for rot in range(ROTS):
        copies[rot][2].wait_recv()
        gather(rot, 1, 0, 3, 4)
        copies[rot][7].start()
    for rot in range(ROTS):
        for receiver, kind in ((0, 8), (2, 9)):
            gather(rot, receiver, 0, 3, 4)
            copies[rot][kind].start()
    for rot in range(ROTS):
        for receiver in (1, 0, 2):
            gather(rot, receiver, 1, 0, 3)
            gather(rot, receiver, 1, 3, 4)
    for kind in (3, 7):
        for rot in range(ROTS):
            copies[rot][kind].wait_recv()
            copies[rot][kind + 3].start()
    for kind in (11, 12, 13):
        for rot in range(ROTS):
            copies[rot][kind].start()
    for rot in range(ROTS):
        for k in range(2):
            gather(rot, 3, k, 0, 3)
            gather(rot, 3, k, 3, 4)
    product[ONCE] = jnp.zeros((PAO, AUX), jnp.float32)
    total = reduction[0]
    blocks = [(rank // 3, pl.ds(rank % 3 * PAO, PAO)) for rank in range(ONCE)]
    for rank in range(ONCE):
        pair = table[AT_LIST + rank]
        total[blocks[rank]] = 1.0 / (energy[lax.div(pair, PARTNERS)] + other_energy[pair])
    for rot in range(ROTS):
        for kind in (4, 5, 6, 8, 9, 10):
            copies[rot][kind].wait_recv()

    def one(i, carry):
        mine = jnp.concatenate([row[rot][i] for rot in range(ROTS)], axis=0)
        others = jnp.concatenate(
            [
                final[0][rot][table[128 + rot * PAIRS + i * PARTNERS + k]]
                for k in range(PARTNERS)
                for rot in range(ROTS)
            ],
            axis=0,
        )
        integral = lax.dot_general(
            mine, others, (((1,), (1,)), ((), ())), preferred_element_type=jnp.float32
        )
        parts = []
        for k in range(PARTNERS):
            pair = i * PARTNERS + k
            keep = jnp.where(table[AT_ONCE + pair] == 1, 0.0, 1.0)
            parts.append(
                integral[:, k * PAO : (k + 1) * PAO] / (energy[i] + other_energy[pair]) * keep
            )
        amplitude = jnp.concatenate(parts, axis=1).astype(jnp.bfloat16)
        early_sum[i] = jnp.dot(amplitude, others, preferred_element_type=jnp.float32)
        return carry

    lax.fori_loop(0, LMO // 2, one, 0)
    for rot in range(ROTS):
        copies[rot][11].wait_recv()
        copies[rot][14].start()
    lax.fori_loop(LMO // 2, LMO, one, 0)
    for rot in range(ROTS):
        for kind in (12, 13, 14):
            copies[rot][kind].wait_recv()

    for rank in range(ONCE):
        pair = table[AT_LIST + rank]
        i = lax.div(pair, PARTNERS)
        mine = jnp.concatenate([row[rot][i] for rot in range(ROTS)], axis=0)
        other = jnp.concatenate(
            [final[1][rot][table[128 + rot * PAIRS + pair]] for rot in range(ROTS)], axis=0
        )
        integral = lax.dot_general(
            mine, other, (((1,), (1,)), ((), ())), preferred_element_type=jnp.float32
        )
        amplitude = (integral * total[blocks[rank]]).astype(jnp.bfloat16)
        product[rank] = jnp.dot(amplitude, other, preferred_element_type=jnp.float32)

    def combine(i, carry):
        gathered = early_sum[i]
        for k in range(PARTNERS):
            gathered = gathered + product[table[AT_RANK + i * PARTNERS + k]]
        fitted[i] = gathered.astype(jnp.bfloat16)
        return carry

    lax.fori_loop(0, LMO, combine, 0)

    reduce_total(tile, flipped, fitted, *reduction)

    for rot in range(ROTS):
        for kind in range(15):
            copies[rot][kind].wait_send()


def local(factors, integrals, pao_energy, lmo_energy, partners):
    vmem = pl.BlockSpec(memory_space=pltpu.VMEM)
    anywhere = pl.BlockSpec(memory_space=pl.ANY)
    piece = (PIECE, AUX)
    scratch = []
    for shape in ((18,), (6,), (2, 2, 4), (2, 4), (2, 4), (16,), (16,)):
        scratch += [pltpu.VMEM(shape + piece, jnp.bfloat16) for _ in range(ROTS)]
    scratch += [
        pltpu.SMEM((AT_LIST + ONCE,), jnp.int32),
        pltpu.SMEM((PAIRS,), jnp.int32),
        pltpu.SMEM((PAIRS,), jnp.int32),
        pltpu.VMEM((8, PAO), jnp.float32),
        pltpu.VMEM((PAIRS, 1, PAO), jnp.float32),
        pltpu.VMEM((AUX, LMO * PAO), jnp.bfloat16),
        pltpu.VMEM((LMO, PAO, AUX), jnp.bfloat16),
        pltpu.VMEM((LMO, PAO, PAO), jnp.float32),
        pltpu.VMEM((LMO, PAO, AUX), jnp.float32),
        pltpu.VMEM((ONCE + 1, PAO, AUX), jnp.float32),
        pltpu.SMEM((PARTNERS, LMOS), jnp.int32),
        pltpu.SMEM((LMOS,), jnp.float32),
        pltpu.VMEM((LMOS, PAO), jnp.float32),
        pltpu.SemaphoreType.DMA((ROTS + 4,)),
        pltpu.SemaphoreType.DMA((ROTS, 15)),
        pltpu.SemaphoreType.DMA((ROTS, 15)),
        pltpu.VMEM((CHUNKS, AUX, 256), jnp.float32),
        pltpu.VMEM((CHUNKS, 4, ROWS, 256), jnp.float32),
        pltpu.VMEM((4, ROWS, AUX), jnp.float32),
        pltpu.VMEM((2, CHUNKS, 2, ROWS, 128), jnp.bfloat16),
        pltpu.VMEM((2, CHUNKS, 2, ROWS, 128), jnp.bfloat16),
        pltpu.VMEM((2, CHUNKS, ROWS, 128), jnp.bfloat16),
        pltpu.VMEM((2, CHUNKS, ROWS, 128), jnp.bfloat16),
        pltpu.VMEM((128, AUX), jnp.float32),
        pltpu.VMEM((AUX, 128), jnp.float32),
        pltpu.VMEM((AUX, 128), jnp.bfloat16),
        pltpu.VMEM((15, HEIGHT, 128), jnp.bfloat16),
        pltpu.SemaphoreType.DMA((2, CHUNKS, 4)),
        pltpu.SemaphoreType.DMA((4, 2, CHUNKS)),
        pltpu.SemaphoreType.DMA((2, 15)),
    ]
    return pl.pallas_call(
        kernel,
        out_shape=jax.ShapeDtypeStruct((HEIGHT, ROWS), jnp.float32),
        in_specs=[anywhere] * 5,
        out_specs=vmem,
        scratch_shapes=scratch,
        compiler_params=pltpu.CompilerParams(
            collective_id=0, has_side_effects=True, vmem_limit_bytes=60 * 2**20
        ),
    )(partners.T, lmo_energy, factors, integrals, pao_energy)


def solution(mesh):
    in_specs = (P(("wide", "narrow"), None, None), P(("wide", "narrow"), None, None), P(), P(), P())
    out_specs = P("wide", "narrow")
    return jax.shard_map(local, mesh=mesh, in_specs=in_specs, out_specs=out_specs, check_vma=False)
```

```python
import jax
import jax.numpy as jnp
from jax import lax
from jax.experimental import pallas as pl
from jax.experimental.pallas import tpu as pltpu
from jax.sharding import PartitionSpec as P

MESH = pl.DeviceIdType.MESH
LMO = 6
LMOS = 768
PARTNERS = 4
PAIRS = LMO * PARTNERS
PAO = 256
AUX = 768
ROWS = AUX // 8
HEIGHT = AUX // 16
CHUNKS = AUX // 2 // 128
ROTS = 4
PIECE = PAO // ROTS
ONCE = 8

AT_ONCE = 128 + ROTS * PAIRS
AT_RANK = AT_ONCE + PAIRS
AT_LIST = AT_RANK + PAIRS

MASKS = (1, 4, 3, 12)


def order(rot):
    return [MASKS[(rot + step) % 4] for step in range(4)]


def flip(position, mask):
    if mask == 0:
        return position
    if mask == 3:
        return 3 - position
    if mask == 2:
        return lax.rem(position + 2, 4)
    return position + 1 - 2 * lax.rem(position, 2)


def neighbour(mask):
    wide = lax.axis_index("wide")
    z, x = wide // 4, lax.rem(wide, 4)
    return (flip(z, mask // 4) * 4 + flip(x, mask % 4), lax.axis_index("narrow"))


def along_y(mask, core=0):
    narrow = lax.axis_index("narrow")
    y, c = narrow // 2, lax.rem(narrow, 2)
    return (lax.axis_index("wide"), flip(y, mask) * 2 + flip(c, core))


def reduce_total(
    tile, flipped, fitted, total, core_in, summed, first_out, first_in, second_out, second_in, block, turned, outgoing, tiles_in,
    core_sem, y_sem, wide_sem,
):
    narrow, wide = lax.axis_index("narrow"), lax.axis_index("wide")
    y, core = narrow // 2, lax.rem(narrow, 2)

    def send(src, dst, sems, device):
        return pltpu.make_async_remote_copy(
            src_ref=src, dst_ref=dst, send_sem=sems[0], recv_sem=sems[1],
            device_id=device, device_id_type=MESH,
        )

    def multiply(i, j):
        rows, columns = slice(i * 256, i * 256 + 256), slice(j * 256, j * 256 + 256)
        total[j, rows] = jnp.dot(
            flipped[rows, :],
            fitted[:, :, columns].reshape(LMO * PAO, 256),
            preferred_element_type=jnp.float32,
        )

    def symmetrise(i, j):
        at_i, at_j = slice(i * 256, i * 256 + 256), slice(j * 256, j * 256 + 256)
        half = 0.5 * (total[j, at_i] + jnp.transpose(total[i, at_j]))
        total[j, at_i] = half
        if i != j:
            total[i, at_j] = jnp.transpose(half)

    def band(place, c):
        return pl.ds(pl.multiple_of((place * 2 + c) * ROWS, ROWS), ROWS)

    steps = []
    for i in range(CHUNKS):
        for j in range(i, CHUNKS):
            multiply(i, j)
            if i != j:
                multiply(j, i)
        for j in range(i, CHUNKS):
            symmetrise(i, j)
        for place in range(4):
            steps.append(
                send(total.at[i, band(place, 1 - core)], core_in.at[i, place],
                     (core_sem.at[0, i, place], core_sem.at[1, i, place]), along_y(0, 1))
            )
            steps[-1].start()

    plan = ((1, 3, (1, 2)), (3, 1, (3, 2)))
    firsts, seconds = {}, {}
    chunks = [(h, chunk) for chunk in range(CHUNKS) for h in range(2)]

    def columns(h, chunk):
        start = chunk * 256 + h * 128
        return slice(start, start + 128)

    for h, chunk in chunks:
        near, far, sent = plan[h]
        if h == 0:
            for step in steps[4 * chunk : 4 * chunk + 4]:
                step.wait_recv()
            at = pl.ds(chunk * 256, 256)
            for place in range(4):
                summed[place, :, at] = total[chunk, band(place, core)] + core_in[chunk, place]
        for place, u in enumerate(sent):
            first_out[h, chunk, place] = summed[flip(y, u), :, columns(h, chunk)].astype(first_out.dtype)
        firsts[h, chunk] = send(
            first_out.at[h, chunk], first_in.at[h, chunk],
            (y_sem.at[0, h, chunk], y_sem.at[1, h, chunk]), along_y(near),
        )
        firsts[h, chunk].start()
    block[pl.ds(ROWS, 128 - ROWS), :] = jnp.zeros((128 - ROWS, AUX), jnp.float32)
    def pass_on(h, chunk):
        near, far, sent = plan[h]
        firsts[h, chunk].wait_recv()
        passed = summed[flip(y, far), :, columns(h, chunk)] + first_in[h, chunk, 1].astype(jnp.float32)
        second_out[h, chunk] = passed.astype(second_out.dtype)
        seconds[h, chunk] = send(
            second_out.at[h, chunk], second_in.at[h, chunk],
            (y_sem.at[2, h, chunk], y_sem.at[3, h, chunk]), along_y(far),
        )
        seconds[h, chunk].start()
    def row_of(t):
        peer = flip(wide // 4, t // 4) * 4 + flip(lax.rem(wide, 4), t % 4)
        return peer * HEIGHT

    def rows(t):
        return pl.ds(pl.multiple_of(row_of(t), HEIGHT), HEIGHT)

    spread = []
    for t in range(1, 16):
        spread.append(
            send(outgoing.at[rows(t)], tiles_in.at[t - 1],
                 (wide_sem.at[0, t - 1], wide_sem.at[1, t - 1]), neighbour(t))
        )

    def send_tiles(start):
        for t in range(1, 16):
            end = row_of(t) + HEIGHT

            @pl.when((end > start) & (end <= start + 128))
            def _():
                spread[t - 1].start()

    def finish(h, chunk):
        at = columns(h, chunk)
        kept = summed[y, :, at] + first_in[h, chunk, 0].astype(jnp.float32)
        seconds[h, chunk].wait_recv()
        block[pl.ds(0, ROWS), at] = kept + second_in[h, chunk].astype(jnp.float32)
        turned[at, :] = jnp.transpose(block[:, at])
        outgoing[at, :] = turned[at, :].astype(outgoing.dtype)
        send_tiles(at.start)

    for step in range(len(chunks) + 4):
        if step < len(chunks):
            pass_on(*chunks[step])
        if step >= 4:
            finish(*chunks[step - 4])
    result = turned[rows(0), :]
    for t in range(1, 16):
        spread[t - 1].wait_recv()
        result = result + tiles_in[t - 1].astype(jnp.float32)
    tile[...] = result[:, :ROWS]

    for step in steps + list(firsts.values()) + list(seconds.values()) + spread:
        step.wait_send()


def fill_table(table, source, slot, partners):
    wide, narrow = lax.axis_index("wide"), lax.axis_index("narrow")
    z, x = wide // 4, lax.rem(wide, 4)

    def group(mask):
        return flip(z, mask // 4) * 4 + flip(x, mask % 4)

    for rot in range(ROTS):
        m1, m2, m3, m4 = order(rot)
        senders = [group(mask) for mask in (0, m1, m2, m1 ^ m2)]
        for receiver, mask in enumerate((m3, m3 ^ m4, m4, 0)):
            first = (group(mask) * 8 + narrow) * LMO

            def scan(i, found):
                found = list(found)
                for k in range(PARTNERS):
                    listed = partners[k, first + i]
                    owner = lax.div(listed, LMO)
                    place = listed - owner * LMO
                    holder = lax.div(owner, 8)
                    for q in range(4):
                        hit = holder == senders[q]
                        low, high, summed = found[3 * q : 3 * q + 3]
                        found[3 * q] = jnp.where(hit, jnp.minimum(low, place), low)
                        found[3 * q + 1] = jnp.where(hit, jnp.maximum(high, place), high)
                        found[3 * q + 2] = jnp.where(hit, summed + place, summed)
                return tuple(found)

            found = lax.fori_loop(0, LMO, scan, (jnp.int32(LMO - 1), jnp.int32(0), jnp.int32(0)) * 4)
            for q in range(4):
                low, high, summed = found[3 * q : 3 * q + 3]
                twice = summed - low - high
                for k, chosen in enumerate((twice, low + high - twice)):
                    chosen = jnp.minimum(jnp.maximum(chosen, 0), LMO - 1)
                    table[rot * 32 + receiver * 8 + k * 4 + q] = chosen + (q * LMO if q < 3 else 0)

    first = (wide * 8 + narrow) * LMO

    def split(i, carry):
        for k in range(PARTNERS):
            listed = partners[k, first + i]
            owner = lax.div(listed, LMO)
            source[i * PARTNERS + k] = lax.div(owner, 8)
            slot[i * PARTNERS + k] = listed - owner * LMO
        return carry

    lax.fori_loop(0, LMO, split, 0)

    def place(pair, carry):
        mine, mine_slot = source[pair], slot[pair]

        def same(i, count):
            for k in range(PARTNERS):
                other = i * PARTNERS + k
                count = jnp.where((source[other] == mine) & (slot[other] == mine_slot), count + 1, count)
            return count

        alone = lax.fori_loop(0, LMO, same, jnp.int32(0)) == 1
        table[AT_ONCE + pair] = jnp.where(alone, 1, 0)
        table[AT_RANK + pair] = jnp.where(alone, carry, ONCE)
        sz = lax.div(mine, 4)
        sx = mine - sz * 4
        digit = {}
        for low_mask, high_mask, here, there in ((1, 3, x, sx), (4, 12, z, sz)):
            digit[low_mask] = jnp.where((flip(here, 1) == there) | (flip(here, 2) == there), 1, 0)
            digit[high_mask] = jnp.where((flip(here, 3) == there) | (flip(here, 2) == there), 1, 0)
        for rot in range(ROTS):
            m1, m2, m3, m4 = order(rot)
            block = (digit[m3] + 2 * digit[m4]) * 4 + digit[m1] + 2 * digit[m2]
            table[128 + rot * PAIRS + pair] = block
        return jnp.where(alone, carry + 1, carry)

    lax.fori_loop(0, PAIRS, place, jnp.int32(0))

    def listed_once(rank, carry):
        def find(pair, chosen):
            return jnp.where(table[AT_RANK + pair] == rank, pair, chosen)

        table[AT_LIST + rank] = lax.fori_loop(0, PAIRS, find, jnp.int32(0))
        return carry

    lax.fori_loop(0, ONCE, listed_once, 0)


def kernel(partners_in, lmo_energy_in, factors, integrals, pao_energy_in, tile, *scratch):
    row = list(scratch[0:4])
    last = list(scratch[4:8])
    send3 = list(scratch[8:12])
    send4 = list(scratch[12:16])
    passing = list(scratch[16:20])
    final = [list(scratch[20:24]), list(scratch[24:28])]
    (table, source, slot, own_rows, other_energy, flipped, fitted, energy, early_sum, product,
     partners, lmo_energy, pao_energy, local_sem, send_sem, recv_sem) = scratch[28:44]
    reduction = scratch[44:]

    barrier = pltpu.get_barrier_semaphore()
    greeted = [neighbour(mask) for mask in MASKS] + [along_y(0, 1), along_y(1), along_y(3)]
    for device in greeted:
        pl.semaphore_signal(barrier, inc=1, device_id=device, device_id_type=MESH)
    pl.semaphore_wait(barrier, len(greeted))

    def copy(rot, kind, src, dst, mask):
        return pltpu.make_async_remote_copy(
            src_ref=src,
            dst_ref=dst,
            send_sem=send_sem.at[rot, kind],
            recv_sem=recv_sem.at[rot, kind],
            device_id=neighbour(mask),
            device_id_type=MESH,
        )

    copies = []
    for rot in range(ROTS):
        m1, m2, m3, m4 = order(rot)
        own = factors.at[:, pl.ds(rot * PIECE, PIECE), :]
        row_copies = [
            copy(rot, 0, own, row[rot].at[pl.ds(6, 6)], m1),
            copy(rot, 1, own, row[rot].at[pl.ds(12, 6)], m2),
            copy(rot, 2, row[rot].at[pl.ds(6, 6)], last[rot], m2),
        ]
        for k, first, count in ((0, 0, 3), (0, 3, 1), (1, 0, 4)):
            at, kind = pl.ds(first, count), len(row_copies)
            place = [pl.ds(4 * block + first, count) for block in range(4)]
            row_copies += [
                copy(rot, kind, send3[rot].at[k, 1, at], passing[rot].at[k, at], m3),
                copy(rot, kind + 1, send3[rot].at[k, 0, at], final[k][rot].at[place[1]], m3),
                copy(rot, kind + 2, send4[rot].at[k, at], final[k][rot].at[place[2]], m4),
                copy(rot, kind + 3, passing[rot].at[k, at], final[k][rot].at[place[3]], m4),
            ]
        copies.append(row_copies)
    for rot in range(ROTS):
        copies[rot][0].start()
    for rot in range(ROTS):
        copies[rot][1].start()
    small = []
    for item, (src, dst) in enumerate(
        ((partners_in, partners), (lmo_energy_in, lmo_energy), (pao_energy_in, pao_energy))
    ):
        small.append(pltpu.make_async_copy(src, dst, local_sem.at[ROTS + 1 + item]))
        small[item].start()
    local = []
    for rot in range(ROTS):
        own = factors.at[:, pl.ds(rot * PIECE, PIECE), :]
        local.append(pltpu.make_async_copy(own, row[rot].at[pl.ds(0, 6)], local_sem.at[rot]))
        local[rot].start()
    local.append(pltpu.make_async_copy(integrals, fitted, local_sem.at[ROTS]))
    local[ROTS].start()

    for copying in small:
        copying.wait()
    fill_table(table, source, slot, partners)

    first = (lax.axis_index("wide") * 8 + lax.axis_index("narrow")) * LMO
    own_rows[...] = jnp.zeros_like(own_rows)
    for i in range(LMO):
        own_rows[i : i + 1, :] = pao_energy[pl.ds(first + i, 1), :] - lmo_energy[first + i]

    def fetch(i, carry):
        for k in range(PARTNERS):
            listed = partners[k, first + i]
            other_energy[i * PARTNERS + k] = pao_energy[pl.ds(listed, 1), :] - lmo_energy[listed]
        return carry

    lax.fori_loop(0, LMO, fetch, 0)
    columns = jnp.transpose(own_rows[...])
    for copying in local:
        copying.wait()
    for i in range(LMO):
        energy[i] = jnp.broadcast_to(columns[:, i : i + 1], (PAO, PAO))
        flipped[:, i * PAO : (i + 1) * PAO] = jnp.transpose(fitted[i])

    for rot in range(ROTS):
        copies[rot][0].wait_recv()
        copies[rot][2].start()
    for rot in range(ROTS):
        copies[rot][1].wait_recv()

    def gather(rot, receiver, k, start, stop):
        held = row[rot] if start < 3 else last[rot]

        def body(q, carry):
            value = held[table[rot * 32 + receiver * 8 + k * 4 + q]]
            if receiver < 2:
                send3[rot][k, receiver, q] = value
            elif receiver == 2:
                send4[rot][k, q] = value
            else:
                final[k][rot][q] = value
            return carry

        lax.fori_loop(start, stop, body, 0)

    for receiver, kind in ((1, 3), (0, 4), (2, 5)):
        for rot in range(ROTS):
            gather(rot, receiver, 0, 0, 3)
            copies[rot][kind].start()
    for rot in range(ROTS):
        copies[rot][2].wait_recv()
        gather(rot, 1, 0, 3, 4)
        copies[rot][7].start()
    for rot in range(ROTS):
        for receiver, kind in ((0, 8), (2, 9)):
            gather(rot, receiver, 0, 3, 4)
            copies[rot][kind].start()
    for rot in range(ROTS):
        for receiver in (1, 0, 2):
            gather(rot, receiver, 1, 0, 3)
            gather(rot, receiver, 1, 3, 4)
    for kind in (3, 7):
        for rot in range(ROTS):
            copies[rot][kind].wait_recv()
            copies[rot][kind + 3].start()
    for kind in (11, 12, 13):
        for rot in range(ROTS):
            copies[rot][kind].start()
    for rot in range(ROTS):
        for k in range(2):
            gather(rot, 3, k, 0, 3)
            gather(rot, 3, k, 3, 4)
    product[ONCE] = jnp.zeros((PAO, AUX), jnp.float32)
    total = reduction[0]
    blocks = [(rank // 3, pl.ds(rank % 3 * PAO, PAO)) for rank in range(ONCE)]
    for rank in range(ONCE):
        pair = table[AT_LIST + rank]
        total[blocks[rank]] = 1.0 / (energy[lax.div(pair, PARTNERS)] + other_energy[pair])
    for rot in range(ROTS):
        for kind in (4, 5, 6, 8, 9, 10):
            copies[rot][kind].wait_recv()

    def one(i, carry):
        mine = jnp.concatenate([row[rot][i] for rot in range(ROTS)], axis=0)
        others = jnp.concatenate(
            [
                final[0][rot][table[128 + rot * PAIRS + i * PARTNERS + k]]
                for k in range(PARTNERS)
                for rot in range(ROTS)
            ],
            axis=0,
        )
        integral = lax.dot_general(
            mine, others, (((1,), (1,)), ((), ())), preferred_element_type=jnp.float32
        )
        parts = []
        for k in range(PARTNERS):
            pair = i * PARTNERS + k
            keep = jnp.where(table[AT_ONCE + pair] == 1, 0.0, 1.0)
            parts.append(
                integral[:, k * PAO : (k + 1) * PAO] / (energy[i] + other_energy[pair]) * keep
            )
        amplitude = jnp.concatenate(parts, axis=1).astype(jnp.bfloat16)
        early_sum[i] = jnp.dot(amplitude, others, preferred_element_type=jnp.float32)
        return carry

    lax.fori_loop(0, LMO // 2, one, 0)
    for rot in range(ROTS):
        copies[rot][11].wait_recv()
        copies[rot][14].start()
    lax.fori_loop(LMO // 2, LMO, one, 0)
    for rot in range(ROTS):
        for kind in (12, 13, 14):
            copies[rot][kind].wait_recv()

    for rank in range(ONCE):
        pair = table[AT_LIST + rank]
        i = lax.div(pair, PARTNERS)
        mine = jnp.concatenate([row[rot][i] for rot in range(ROTS)], axis=0)
        other = jnp.concatenate(
            [final[1][rot][table[128 + rot * PAIRS + pair]] for rot in range(ROTS)], axis=0
        )
        integral = lax.dot_general(
            mine, other, (((1,), (1,)), ((), ())), preferred_element_type=jnp.float32
        )
        amplitude = (integral * total[blocks[rank]]).astype(jnp.bfloat16)
        product[rank] = jnp.dot(amplitude, other, preferred_element_type=jnp.float32)

    def combine(i, carry):
        gathered = early_sum[i]
        for k in range(PARTNERS):
            gathered = gathered + product[table[AT_RANK + i * PARTNERS + k]]
        fitted[i] = gathered.astype(jnp.bfloat16)
        return carry

    lax.fori_loop(0, LMO, combine, 0)

    reduce_total(tile, flipped, fitted, *reduction)

    for rot in range(ROTS):
        for kind in range(15):
            copies[rot][kind].wait_send()


def local(factors, integrals, pao_energy, lmo_energy, partners):
    vmem = pl.BlockSpec(memory_space=pltpu.VMEM)
    anywhere = pl.BlockSpec(memory_space=pl.ANY)
    piece = (PIECE, AUX)
    scratch = []
    for shape in ((18,), (6,), (2, 2, 4), (2, 4), (2, 4), (16,), (16,)):
        scratch += [pltpu.VMEM(shape + piece, jnp.bfloat16) for _ in range(ROTS)]
    scratch += [
        pltpu.SMEM((AT_LIST + ONCE,), jnp.int32),
        pltpu.SMEM((PAIRS,), jnp.int32),
        pltpu.SMEM((PAIRS,), jnp.int32),
        pltpu.VMEM((8, PAO), jnp.float32),
        pltpu.VMEM((PAIRS, 1, PAO), jnp.float32),
        pltpu.VMEM((AUX, LMO * PAO), jnp.bfloat16),
        pltpu.VMEM((LMO, PAO, AUX), jnp.bfloat16),
        pltpu.VMEM((LMO, PAO, PAO), jnp.float32),
        pltpu.VMEM((LMO, PAO, AUX), jnp.float32),
        pltpu.VMEM((ONCE + 1, PAO, AUX), jnp.float32),
        pltpu.SMEM((PARTNERS, LMOS), jnp.int32),
        pltpu.SMEM((LMOS,), jnp.float32),
        pltpu.VMEM((LMOS, PAO), jnp.float32),
        pltpu.SemaphoreType.DMA((ROTS + 4,)),
        pltpu.SemaphoreType.DMA((ROTS, 15)),
        pltpu.SemaphoreType.DMA((ROTS, 15)),
        pltpu.VMEM((CHUNKS, AUX, 256), jnp.float32),
        pltpu.VMEM((CHUNKS, 4, ROWS, 256), jnp.float32),
        pltpu.VMEM((4, ROWS, AUX), jnp.float32),
        pltpu.VMEM((2, CHUNKS, 2, ROWS, 128), jnp.bfloat16),
        pltpu.VMEM((2, CHUNKS, 2, ROWS, 128), jnp.bfloat16),
        pltpu.VMEM((2, CHUNKS, ROWS, 128), jnp.bfloat16),
        pltpu.VMEM((2, CHUNKS, ROWS, 128), jnp.bfloat16),
        pltpu.VMEM((128, AUX), jnp.float32),
        pltpu.VMEM((AUX, 128), jnp.float32),
        pltpu.VMEM((AUX, 128), jnp.bfloat16),
        pltpu.VMEM((15, HEIGHT, 128), jnp.bfloat16),
        pltpu.SemaphoreType.DMA((2, CHUNKS, 4)),
        pltpu.SemaphoreType.DMA((4, 2, CHUNKS)),
        pltpu.SemaphoreType.DMA((2, 15)),
    ]
    return pl.pallas_call(
        kernel,
        out_shape=jax.ShapeDtypeStruct((HEIGHT, ROWS), jnp.float32),
        in_specs=[anywhere] * 5,
        out_specs=vmem,
        scratch_shapes=scratch,
        compiler_params=pltpu.CompilerParams(
            collective_id=0, has_side_effects=True, vmem_limit_bytes=60 * 2**20
        ),
    )(partners.T, lmo_energy, factors, integrals, pao_energy)


def solution(mesh):
    in_specs = (P(("wide", "narrow"), None, None), P(("wide", "narrow"), None, None), P(), P(), P())
    out_specs = P("wide", "narrow")
    return jax.shard_map(local, mesh=mesh, in_specs=in_specs, out_specs=out_specs, check_vma=False)
```
